32 devices in a mesh: section: 2 (over x), dp: 4 (over z), tensor: 4 (over y, core).
Axes of the slice: x: 2, y: 2, z: 4, core: 2. Of those that a mesh axis runs over, the one named last changes fastest.
Arguments:
- inputs: bfloat16 [2, 8, 512, 768], P(None, 'dp'), may hold values from -6 to 6
- cotangent: bfloat16 [2, 8, 512, 768], P(None, 'dp'), may hold values from -6 to 6
- segment_ids: int32 [2, 8, 512], P(None, 'dp'), may hold values from 0 to 1
- column_ids: int32 [2, 8, 512], P(None, 'dp'), may hold values from 0 to 255
- row_ids: int32 [2, 8, 512], P(None, 'dp'), may hold values from 0 to 255
- answer_ids: int32 [2, 8, 512], P(None, 'dp'), may hold values from 0 to 1
- lengths: int32 [2, 8], P(None, 'dp'), may hold values from 128 to 512, as said below
- type_table: bfloat16 [516, 768], replicated, may hold values from -4 to 4
- query_weight: bfloat16 [2, 768, 768], P('section', None, 'tensor'), may hold values from -0.21875 to 0.21875
- query_bias: bfloat16 [2, 768], P('section', 'tensor'), may hold values from -3 to 3
- key_weight: bfloat16 [2, 768, 768], P('section', None, 'tensor'), may hold values from -0.21875 to 0.21875
- value_weight: bfloat16 [2, 768, 768], P('section', None, 'tensor'), may hold values from -0.21875 to 0.21875
- value_bias: bfloat16 [2, 768], P('section', 'tensor'), may hold values from -3 to 3
- output_weight: bfloat16 [2, 768, 768], P('section', 'tensor'), may hold values from -1.75 to 1.75
- output_bias: bfloat16 [2, 768], P('section'), may hold values from -2 to 2
- first_gain: bfloat16 [2, 768], P('section'), may hold values from 0.5 to 1.5
- first_shift: bfloat16 [2, 768], P('section'), may hold values from -2 to 2
- up_weight: bfloat16 [2, 768, 3072], P('section', None, 'tensor'), may hold values from -0.21875 to 0.21875
- up_bias: bfloat16 [2, 3072], P('section', 'tensor'), may hold values from -3 to 3
- down_weight: bfloat16 [2, 3072, 768], P('section', 'tensor'), may hold values from -0.109375 to 0.109375
- down_bias: bfloat16 [2, 768], P('section'), may hold values from -2 to 2
- second_gain: bfloat16 [2, 768], P('section'), may hold values from 0.5 to 1.5
- second_shift: bfloat16 [2, 768], P('section'), may hold values from -2 to 2
Outputs:
- layer_outputs: bfloat16 [2, 2, 8, 512, 768], P('section', None, 'dp', None, 'tensor')
- layer_input_grads: float32 [2, 2, 8, 512, 768], P('section', None, 'dp', None, 'tensor')
- query_weight_grad: float32 [2, 768, 768], P('section', 'dp', 'tensor')
- query_bias_grad: float32 [2, 768], P('section', 'tensor')
- key_weight_grad: float32 [2, 768, 768], P('section', 'dp', 'tensor')
- value_weight_grad: float32 [2, 768, 768], P('section', 'dp', 'tensor')
- value_bias_grad: float32 [2, 768], P('section', 'tensor')
- output_weight_grad: float32 [2, 768, 768], P('section', 'tensor', 'dp')
- output_bias_grad: float32 [2, 768], P('section', 'tensor')
- first_gain_grad: float32 [2, 768], P('section', 'tensor')
- first_shift_grad: float32 [2, 768], P('section', 'tensor')
- up_weight_grad: float32 [2, 768, 3072], P('section', 'dp', 'tensor')
- up_bias_grad: float32 [2, 3072], P('section', 'tensor')
- down_weight_grad: float32 [2, 3072, 768], P('section', 'tensor', 'dp')
- down_bias_grad: float32 [2, 768], P('section', 'tensor')
- second_gain_grad: float32 [2, 768], P('section', 'tensor')
- second_shift_grad: float32 [2, 768], P('section', 'tensor')
- type_table_grad: float32 [516, 768], P('section', 'tensor')
The draws below stay inside these ranges and needn't reach their ends.
Inputs may be any that keep to these rules, and one draw needn't show every extreme that they name: `lengths`: in each micro-batch some item has all 512 tokens.
All inputs are finite; a program needn't handle non-finite values.
Results may differ from the reference program's by a relative error of at most 0.025.
Values may be sent and summed in bfloat16 or wider, within the bound.
A program may use at most 192 MiB of HBM per device.

```python
import jax
import jax.numpy as jnp
from jax import lax

H = 12
HD = 64
FF = 3072
COLS = 256
ROWS = 256
SEQ = 512
MB = 2
D = 768
TYPES = 516
ITEMS = 8
LAYERS = 2


def draw_lengths(key, part):
    key = jax.random.fold_in(key, 7)
    first_key, second_key = jax.random.split(key)
    drawn = jax.random.randint(first_key, (MB, ITEMS), SEQ // 4, SEQ + 1)
    chosen = jax.random.randint(second_key, (MB, 1), 0, ITEMS)
    return jnp.where(jnp.arange(ITEMS)[None, :] == chosen, SEQ, drawn).astype(jnp.int32)


def plant(array, key, low, high):
    longest = array.shape.index(max(array.shape))
    spots = []
    for shift in (0, 1):
        where = [jax.random.randint(jax.random.fold_in(key, axis), (), 0, length) for axis, length in enumerate(array.shape)]
        where[longest] = (where[longest] + shift) % array.shape[longest]
        spots.append(tuple(where))
    return array.at[spots[0]].set(low).at[spots[1]].set(high)


def with_spikes(array, stream_key, source, target, shards_of, factor):
    def block_of(dim):
        return (jnp.arange(array.shape[dim]) // (array.shape[dim] // shards_of)).reshape((-1,) + (1,) * (array.ndim - 1 - dim))

    first = jax.random.permutation(stream_key, shards_of)[block_of(target)]
    far = (block_of(target) + shards_of // 2) % shards_of
    return jnp.where((block_of(source) == first) | (block_of(source) == far), factor * array, array)


def shard_levels(key, shape, pieces, low, largest):
    level = 1.0
    for axis_at, blocks in pieces:
        steps = jax.random.uniform(jax.random.fold_in(jax.random.fold_in(key, 6), axis_at), (blocks,), jnp.float32, low / len(pieces), largest / len(pieces))
        level = level * jnp.repeat(jnp.exp(steps), shape[axis_at] // blocks).reshape((-1,) + (1,) * (len(shape) - 1 - axis_at))
    return level


def scatter_about(own_key, dims, scale, reach, shards=(), kind=jnp.bfloat16):
    loudness = shard_levels(own_key, dims, shards, -0.22, 0.18) if shards else 1.0
    result = jax.random.normal(own_key, dims, jnp.float32) * scale * loudness
    return jnp.minimum(jnp.maximum(result, -reach), reach).astype(kind)


def gaussian_with(own_key, shape, width, reach, cuts, heavy, dtype=jnp.bfloat16):
    result = width * jax.random.normal(own_key, shape, jnp.float32)
    if cuts:
        result = result * shard_levels(own_key, shape, cuts, -0.22, 0.18)
    return jnp.clip(with_spikes(result, jax.random.fold_in(own_key, 3), *heavy), -reach, reach).astype(dtype)


def setup_inputs(seed: int = 0) -> dict:
    arg_keys = jax.random.split(jax.random.key(seed), 24)
    return {
        "inputs": scatter_about(arg_keys[0], (MB, ITEMS, SEQ, D), 1.0, 6.0, ((1, 4),)),
        "cotangent": gaussian_with(arg_keys[1], (MB, ITEMS, SEQ, D), 1.0, 6.0, ((1, 4),), (1, 3, 4, 2.0)),
        "segment_ids": plant(jax.random.randint(arg_keys[2], (MB, ITEMS, SEQ), 0, 2), jax.random.fold_in(arg_keys[2], 1), 0, 1).astype(jnp.int32),
        "column_ids": plant(jax.random.randint(arg_keys[3], (MB, ITEMS, SEQ), 0, COLS), jax.random.fold_in(arg_keys[3], 1), 0, COLS - 1).astype(jnp.int32),
        "row_ids": plant(jax.random.randint(arg_keys[4], (MB, ITEMS, SEQ), 0, ROWS), jax.random.fold_in(arg_keys[4], 1), 0, ROWS - 1).astype(jnp.int32),
        "answer_ids": plant(jax.random.randint(arg_keys[5], (MB, ITEMS, SEQ), 0, 2), jax.random.fold_in(arg_keys[5], 1), 0, 1).astype(jnp.int32),
        "lengths": draw_lengths(jax.random.fold_in(arg_keys[23], 71), 0),
        "type_table": scatter_about(arg_keys[7], (TYPES, D), 0.5, 4.0),
        "query_weight": scatter_about(arg_keys[8], (LAYERS, D, D), D ** -0.5, 0.21875, ((0, 2), (2, 4))),
        "query_bias": scatter_about(arg_keys[9], (LAYERS, D), 0.5, 3.0, ((0, 2), (1, 4))),
        "key_weight": scatter_about(arg_keys[10], (LAYERS, D, D), D ** -0.5, 0.21875, ((0, 2), (2, 4))),
        "value_weight": scatter_about(arg_keys[11], (LAYERS, D, D), D ** -0.5, 0.21875, ((0, 2), (2, 4))),
        "value_bias": scatter_about(arg_keys[12], (LAYERS, D), 0.5, 3.0, ((0, 2), (1, 4))),
        "output_weight": scatter_about(arg_keys[13], (LAYERS, D, D), (max(D // 64, 4)) ** -0.5, 1.75, ((0, 2), (1, 4))),
        "output_bias": scatter_about(arg_keys[14], (LAYERS, D), 0.3, 2.0, ((0, 2),)),
        "first_gain": jnp.clip(1.0 + 0.1 * jax.random.normal(arg_keys[15], (LAYERS, D), jnp.float32), 0.5, 1.5).astype(jnp.bfloat16),
        "first_shift": scatter_about(arg_keys[16], (LAYERS, D), 0.3, 2.0, ((0, 2),)),
        "up_weight": scatter_about(arg_keys[17], (LAYERS, D, FF), D ** -0.5, 0.21875, ((0, 2), (2, 4))),
        "up_bias": scatter_about(arg_keys[18], (LAYERS, FF), 0.5, 3.0, ((0, 2), (1, 4))),
        "down_weight": scatter_about(arg_keys[19], (LAYERS, FF, D), FF ** -0.5, 0.109375, ((0, 2), (1, 4))),
        "down_bias": scatter_about(arg_keys[20], (LAYERS, D), 0.3, 2.0, ((0, 2),)),
        "second_gain": jnp.clip(1.0 + 0.1 * jax.random.normal(arg_keys[21], (LAYERS, D), jnp.float32), 0.5, 1.5).astype(jnp.bfloat16),
        "second_shift": scatter_about(arg_keys[22], (LAYERS, D), 0.3, 2.0, ((0, 2),)),
    }


@jax.custom_vjp
def low(v):
    return lax.optimization_barrier(v.astype(jnp.bfloat16)).astype(jnp.float32)

@jax.custom_vjp
def low_back(v):
    return v

def low_keep(v):
    return (low(v), None)

def low_pass(kept, grad):
    return (grad,)

def back_keep(v):
    return (v, None)

def back_low(kept, grad):
    return (low(grad),)
low.defvjp(low_keep, low_pass)
low_back.defvjp(back_keep, back_low)
EPSILON = 1e-12
MASKED = -1e+30
HIGHEST = lax.Precision.HIGHEST

def layer_norm(value, gain, shift):
    averaged = lax.optimization_barrier(jnp.mean(value, axis=-1, keepdims=True))
    centered = value - averaged
    variance = lax.optimization_barrier(jnp.mean(centered * centered, axis=-1, keepdims=True))
    return centered * lax.rsqrt(variance + EPSILON) * gain + shift

def attend_item(packed):
    queries, keys_here, values, visible = packed
    scores = jnp.einsum('qhd,khd->hqk', queries, keys_here, precision=HIGHEST) * HD ** (-0.5)
    scores = low_back(scores)
    scores = jnp.where(visible[None, None, :], scores, MASKED)
    maximum = lax.optimization_barrier(jnp.max(scores, axis=-1, keepdims=True))
    raised = jnp.exp(scores - maximum)
    weights = raised / lax.optimization_barrier(jnp.sum(raised, axis=-1, keepdims=True))
    return jnp.einsum('hqk,khd->qhd', low(weights), values, precision=HIGHEST)

def layer_block(entering, visible, params):
    query_weight, query_bias, key_weight, value_weight, value_bias, output_weight, output_bias, first_gain, first_shift, up_weight, up_bias, down_weight, down_bias, second_gain, second_shift = params
    lowered = low(entering)

    def project(weight, bias_row):
        return low(low_back(jnp.matmul(lowered, weight, precision=HIGHEST) + bias_row))
    queries = project(query_weight, query_bias)
    keys_here = low(low_back(jnp.matmul(lowered, key_weight, precision=HIGHEST)))
    values = project(value_weight, value_bias)
    heads_shape = entering.shape[:2] + (H, HD)
    context = lax.map(jax.checkpoint(attend_item), (queries.reshape(heads_shape), keys_here.reshape(heads_shape), values.reshape(heads_shape), visible))
    context = low(low_back(context.reshape(entering.shape)))
    attended = low_back(jnp.matmul(context, output_weight, precision=HIGHEST) + output_bias)
    normed = layer_norm(entering + attended, first_gain, first_shift)
    hidden = low_back(jnp.matmul(low(normed), up_weight, precision=HIGHEST) + up_bias)
    active = low(jax.nn.gelu(hidden, approximate=False))
    branch_out = low_back(jnp.matmul(active, down_weight, precision=HIGHEST) + down_bias)
    return layer_norm(normed + branch_out, second_gain, second_shift)

def reference(inputs, cotangent, segment_ids, column_ids, row_ids, answer_ids, lengths, type_table, query_weight, query_bias, key_weight, value_weight, value_bias, output_weight, output_bias, first_gain, first_shift, up_weight, up_bias, down_weight, down_bias, second_gain, second_shift):
    stacked = tuple((item.astype(jnp.float32) for item in (query_weight, query_bias, key_weight, value_weight, value_bias, output_weight, output_bias, first_gain, first_shift, up_weight, up_bias, down_weight, down_bias, second_gain, second_shift)))
    item_count = MB * ITEMS
    flat_inputs = inputs.astype(jnp.float32).reshape(item_count, SEQ, D)
    visible = jnp.arange(SEQ)[None, :] < lengths.reshape(item_count, 1)
    type_index = (segment_ids.reshape(item_count, SEQ), column_ids.reshape(item_count, SEQ) + 2, row_ids.reshape(item_count, SEQ) + 2 + COLS, answer_ids.reshape(item_count, SEQ) + 2 + COLS + ROWS)

    def forward(embedded_in, type_rows, params, shifted):
        embedded = embedded_in + type_rows[type_index[0]] + type_rows[type_index[1]] + type_rows[type_index[2]] + type_rows[type_index[3]]
        first_out = low(low_back(layer_block(embedded, visible, tuple((param_pair[0] for param_pair in params)))))
        second_out = low(layer_block(first_out + shifted, visible, tuple((param_pair[1] for param_pair in params))))
        return (first_out, second_out)
    shifted = jnp.zeros_like(flat_inputs)
    (first_out, second_out), pullback = jax.vjp(forward, flat_inputs, type_table.astype(jnp.float32), stacked, shifted)
    grad_inputs, grad_types, grad_params, grad_shifted = pullback((jnp.zeros_like(first_out), cotangent.astype(jnp.float32).reshape(item_count, SEQ, D)))
    layer_outputs = jnp.stack([first_out, second_out]).reshape(LAYERS, MB, ITEMS, SEQ, D).astype(jnp.bfloat16)
    layer_input_grads = jnp.stack([grad_inputs, grad_shifted]).reshape(LAYERS, MB, ITEMS, SEQ, D)
    return (layer_outputs, layer_input_grads, grad_params[0], grad_params[1], grad_params[2], grad_params[3], grad_params[4], grad_params[5], grad_params[6], grad_params[7], grad_params[8], grad_params[9], grad_params[10], grad_params[11], grad_params[12], grad_params[13], grad_params[14], grad_types)
```

```python
import functools

import jax
import jax.numpy as jnp
from jax import lax
from jax.experimental import pallas as pl
from jax.experimental.pallas import tpu as pltpu
from jax.sharding import PartitionSpec as P

HD = 64
COLS = 256
ROWS = 256
EPSILON = 1e-12
MASKED = -1e30
BF = jnp.bfloat16
F32 = jnp.float32
MESH = pl.DeviceIdType.MESH
VMEM_LIMIT = 60 * 1024 * 1024
STEP = 128


def nn(left, right):
    return lax.dot_general(left, right, (((1,), (0,)), ((), ())), preferred_element_type=F32)


def nt(left, right):
    return lax.dot_general(left, right, (((1,), (1,)), ((), ())), preferred_element_type=F32)


def tn(left, right):
    return lax.dot_general(left, right, (((0,), (0,)), ((), ())), preferred_element_type=F32)


def normalize(value):
    centered = value - jnp.mean(value, axis=-1, keepdims=True)
    variance = jnp.mean(centered * centered, axis=-1, keepdims=True)
    scale = lax.rsqrt(variance + EPSILON)
    return centered * scale, scale


def place():
    section = lax.axis_index("section")
    data = lax.axis_index("dp")
    tensor = lax.axis_index("tensor")
    beside = tensor + 1 - 2 * (tensor % 2)
    across = tensor + 2 - 4 * ((tensor // 2) % 2)
    return section, data, tensor, beside, across


def greet(partners):
    barrier = pltpu.get_barrier_semaphore()
    for partner in partners:
        pl.semaphore_signal(barrier, inc=1, device_id=partner, device_id_type=MESH)
    pl.semaphore_wait(barrier, len(partners))


def remote(src, dst, send, recv, device):
    return pltpu.make_async_remote_copy(
        src_ref=src, dst_ref=dst, send_sem=send, recv_sem=recv, device_id=device, device_id_type=MESH
    )


def forward_kernel(
    inputs_ref,
    ids_ref,
    table_ref,
    length_ref,
    wa_ref,
    wu_ref,
    wd_ref,
    bias_ref,
    vec_ref,
    wa_out,
    wu_out,
    wd_out,
    p_out,
    lse_out,
    act_out,
    slope_out,
    n1_out,
    n2_out,
    rs1_out,
    rs2_out,
    x_out,
    y_out,
    wa,
    wu,
    wd,
    bias,
    p,
    lse,
    act,
    slope,
    xf,
    xb,
    first,
    low,
    n1,
    n2,
    rs1,
    rs2,
    y,
    gather_send,
    gather_recv,
    relay_send,
    relay_recv,
    local_sem,
    out_sem,
):
    section, data, tensor, beside, across = place()
    length, width = xf.shape
    ranks = wa.shape[0]
    heads = wa.shape[1] // (4 * HD)
    part = heads * HD
    steps = length // STEP
    sequences = inputs_ref.shape[1]
    near = (section, data, beside)
    far = (section, data, across)
    other = (1 - section, data, tensor)
    greet((near, far, other))

    shards = ((wa_ref, wa), (bias_ref, bias), (wu_ref, wu), (wd_ref, wd))
    to_far = []
    to_near = []
    onward = []
    own = []
    for number, (source, target) in enumerate(shards):
        to_far.append(
            remote(source, target.at[2], gather_send.at[number, 0], gather_recv.at[number, 0], far)
        )
        to_near.append(
            remote(source, target.at[1], gather_send.at[number, 1], gather_recv.at[number, 1], near)
        )
        onward.append(
            remote(
                target.at[2], target.at[3], gather_send.at[number, 2], gather_recv.at[number, 2], near
            )
        )
        own.append(pltpu.make_async_copy(source, target.at[0], local_sem.at[number]))
    for copy in to_far:
        copy.start()
    for copy in to_near:
        copy.start()
    for copy in own:
        copy.start()

    def pass_on(number):
        to_far[number].wait_recv()
        onward[number].start()

    def ready(number):
        own[number].wait()
        to_near[number].wait_recv()
        onward[number].wait_recv()

    out_copies = []

    def put_out(source, target):
        copy = pltpu.make_async_copy(source, target, out_sem.at[len(out_copies)])
        copy.start()
        out_copies.append(copy)

    relays = [
        remote(
            y.at[pl.ds(step * STEP, STEP)],
            xb.at[pl.ds(step * STEP, STEP)],
            relay_send.at[step],
            relay_recv.at[step],
            other,
        )
        for step in range(steps)
    ]

    @pl.when(section == 0)
    def _():
        copy = pltpu.make_async_copy(
            inputs_ref.at[tensor // sequences, tensor % sequences], xb, local_sem.at[4]
        )
        copy.start()
        copy.wait()

        def embed(step, carry):
            rows = pl.ds(pl.multiple_of(step * STEP, STEP), STEP)
            lane = lax.broadcasted_iota(jnp.int32, (STEP, table_ref.shape[0]), 1)
            picks = jnp.zeros((STEP, table_ref.shape[0]), F32)
            for column in range(4):
                picks = picks + jnp.where(ids_ref[rows, column : column + 1] == lane, 1.0, 0.0)
            value = xb[rows, :].astype(F32) + nn(picks.astype(BF), table_ref[...])
            xf[rows, :] = value
            xb[rows, :] = value.astype(BF)
            return carry

        lax.fori_loop(0, steps, embed, 0)

    pass_on(0)
    pass_on(1)

    @pl.when(section != 0)
    def _():
        for relay in relays:
            relay.wait_recv()
        xf[...] = xb[...].astype(F32)

    ready(0)
    ready(1)
    put_out(wa, wa_out)
    put_out(xb, x_out)

    def project(rank, carry):
        columns = jnp.transpose(bias[rank], (1, 0))
        p[rank, 0 : 3 * part, :] = (
            nt(wa[rank, 0 : 3 * part, :], xb[...]) + columns[0 : 3 * part, 1:2]
        ).astype(BF)
        return carry

    lax.fori_loop(0, ranks, project, 0)
    pass_on(2)

    visible = lax.broadcasted_iota(jnp.int32, (length, length), 0) < length_ref[0, 0]

    def attend(head, carry):
        rank = head // heads
        base = (head % heads) * HD
        query = p[rank, pl.ds(pl.multiple_of(base, HD), HD), :]
        keys = p[rank, pl.ds(pl.multiple_of(part + base, HD), HD), :]
        values = p[rank, pl.ds(pl.multiple_of(2 * part + base, HD), HD), :]
        query = (query.astype(F32) * HD ** (-0.5)).astype(BF)
        scores = jnp.where(visible, tn(keys, query), MASKED)
        maximum = jnp.max(scores, axis=0, keepdims=True)
        raised = jnp.exp(scores - maximum)
        total = jnp.sum(raised, axis=0, keepdims=True)
        context = nn(values, raised.astype(BF)) / total
        p[rank, pl.ds(pl.multiple_of(3 * part + base, HD), HD), :] = context.astype(BF)
        lse[head] = maximum + jnp.log(total)
        return carry

    lax.fori_loop(0, ranks * heads, attend, 0)
    put_out(p, p_out)
    put_out(lse, lse_out)

    def first_norm(step, carry):
        rows = pl.ds(pl.multiple_of(step * STEP, STEP), STEP)
        total = xf[rows, :] + vec_ref[0:1, :]
        for rank in range(ranks):
            total = total + tn(p[rank, 3 * part : 4 * part, rows], wa[rank, 3 * part : 4 * part, :])
        normal, scale = normalize(total)
        value = normal * vec_ref[1:2, :] + vec_ref[2:3, :]
        first[rows, :] = value
        low[rows, :] = value.astype(BF)
        n1[rows, :] = normal.astype(BF)
        rs1[rows, :] = jnp.broadcast_to(scale, (STEP, 128))
        return carry

    lax.fori_loop(0, steps, first_norm, 0)
    put_out(n1, n1_out)
    put_out(rs1, rs1_out)
    ready(2)
    put_out(wu, wu_out)
    block = 256
    blocks = wu.shape[2] // block

    def widen(index, carry):
        rank = index // blocks
        columns = pl.ds(pl.multiple_of((index % blocks) * block, block), block)
        hidden = nn(low[...], wu[rank, :, columns]) + bias[rank, 0:1, columns]
        inner = 0.5 * (1.0 + lax.erf(hidden * (0.5**0.5)))
        act[rank, :, columns] = (hidden * inner).astype(BF)
        density = jnp.exp(hidden * hidden * (-0.5)) * 0.3989422804014327
        slope[rank, :, columns] = (inner + hidden * density).astype(BF)
        return carry

    lax.fori_loop(0, ranks * blocks, widen, 0)
    put_out(act, act_out)
    put_out(slope, slope_out)
    pass_on(3)
    ready(3)
    put_out(wd, wd_out)

    for step in range(steps):
        rows = pl.ds(step * STEP, STEP)
        total = first[rows, :] + vec_ref[3:4, :]
        for rank in range(ranks):
            total = total + nn(act[rank, rows, :], wd[rank])
        normal, scale = normalize(total)
        y[rows, :] = (normal * vec_ref[4:5, :] + vec_ref[5:6, :]).astype(BF)
        n2[rows, :] = normal.astype(BF)
        rs2[rows, :] = jnp.broadcast_to(scale, (STEP, 128))

        @pl.when(section == 0)
        def _():
            relays[step].start()

    put_out(n2, n2_out)
    put_out(rs2, rs2_out)
    put_out(y, y_out)
    for copy in out_copies:
        copy.wait()
    for group in (to_far, to_near, onward):
        for copy in group:
            copy.wait_send()

    @pl.when(section == 0)
    def _():
        for relay in relays:
            relay.wait_send()


def forward(inputs, ids, table, length_here, wa, wu, wd, bias, vectors, ranks):
    length, width = inputs.shape[2], inputs.shape[3]
    rows_a = wa.shape[0]
    hidden = wu.shape[1]
    heads = ranks * (rows_a // (4 * HD))
    steps = length // STEP
    shapes = dict(
        wa=((ranks, rows_a, width), BF),
        wu=((ranks, width, hidden), BF),
        wd=((ranks, hidden, width), BF),
        p=((ranks, rows_a, length), BF),
        lse=((heads, 1, length), F32),
        act=((ranks, length, hidden), BF),
        slope=((ranks, length, hidden), BF),
        n1=((length, width), BF),
        n2=((length, width), BF),
        rs1=((length, 128), F32),
        rs2=((length, 128), F32),
        x=((length, width), BF),
        y=((length, width), BF),
    )

    def buffer(name):
        return pltpu.VMEM(*shapes[name])

    outs = ("wa", "wu", "wd", "p", "lse", "act", "slope", "n1", "n2", "rs1", "rs2", "x", "y")
    anywhere = pl.BlockSpec(memory_space=pl.ANY)
    inside = pl.BlockSpec(memory_space=pltpu.VMEM)
    return pl.pallas_call(
        forward_kernel,
        name="forward_layer",
        out_shape=tuple(jax.ShapeDtypeStruct(*shapes[name]) for name in outs),
        in_specs=[
            anywhere,
            inside,
            inside,
            pl.BlockSpec(memory_space=pltpu.SMEM),
            anywhere,
            anywhere,
            anywhere,
            anywhere,
            inside,
        ],
        out_specs=tuple(anywhere for _ in outs),
        scratch_shapes=[
            buffer("wa"),
            buffer("wu"),
            buffer("wd"),
            pltpu.VMEM((ranks,) + bias.shape, F32),
            buffer("p"),
            buffer("lse"),
            buffer("act"),
            buffer("slope"),
            pltpu.VMEM((length, width), F32),
            buffer("x"),
            pltpu.VMEM((length, width), F32),
            pltpu.VMEM((length, width), BF),
            buffer("n1"),
            buffer("n2"),
            buffer("rs1"),
            buffer("rs2"),
            buffer("y"),
            pltpu.SemaphoreType.DMA((4, 3)),
            pltpu.SemaphoreType.DMA((4, 3)),
            pltpu.SemaphoreType.DMA((steps,)),
            pltpu.SemaphoreType.DMA((steps,)),
            pltpu.SemaphoreType.DMA((5,)),
            pltpu.SemaphoreType.DMA((len(outs),)),
        ],
        compiler_params=pltpu.CompilerParams(
            collective_id=0, has_side_effects=True, vmem_limit_bytes=VMEM_LIMIT
        ),
        cost_estimate=pl.CostEstimate(
            flops=8_000_000_000, bytes_accessed=60_000_000, transcendentals=6_000_000
        ),
    )(inputs, ids, table, length_here, wa, wu, wd, bias, vectors)


def backward_kernel(
    cotangent_ref,
    wa_ref,
    wu_ref,
    wd_ref,
    p_ref,
    lse_ref,
    act_ref,
    slope_ref,
    n1_ref,
    n2_ref,
    rs1_ref,
    rs2_ref,
    x_ref,
    length_ref,
    vec_ref,
    sums_out,
    dx_out,
    vec_out,
    wa,
    wu,
    wd,
    p,
    lse,
    act,
    slope,
    n1,
    n2,
    rs1,
    rs2,
    xb,
    g,
    dsum,
    low,
    low_t,
    first_t,
    x_t,
    dcontext,
    dx,
    near_out,
    near_in,
    far_out,
    far_in,
    sums,
    load_sem,
    near_send,
    near_recv,
    far_send,
    far_recv,
    relay_send,
    relay_recv,
    out_sem,
):
    section, data, tensor, beside, across = place()
    length, width = g.shape
    ranks = wa.shape[0]
    heads = wa.shape[1] // (4 * HD)
    part = heads * HD
    steps = length // STEP
    sequences = cotangent_ref.shape[1]
    units = sums.shape[1]
    share = sums.shape[2]
    near = (section, data, beside)
    far = (section, data, across)
    other = (1 - section, data, tensor)
    greet((near, far, other))

    loads = {}
    for name, source, target in (
        ("n2", n2_ref, n2),
        ("rs2", rs2_ref, rs2),
        ("wd", wd_ref, wd),
        ("slope", slope_ref, slope),
        ("wu", wu_ref, wu),
        ("act", act_ref, act),
        ("n1", n1_ref, n1),
        ("rs1", rs1_ref, rs1),
        ("wa", wa_ref, wa),
        ("p", p_ref, p),
        ("lse", lse_ref, lse),
        ("xb", x_ref, xb),
    ):
        loads[name] = pltpu.make_async_copy(source, target, load_sem.at[len(loads)])
    start_g = pltpu.make_async_copy(
        cotangent_ref.at[tensor // sequences, tensor % sequences], g, load_sem.at[len(loads)]
    )
    relays = [
        remote(
            dx.at[pl.ds(step * STEP, STEP)],
            g.at[pl.ds(step * STEP, STEP)],
            relay_send.at[step],
            relay_recv.at[step],
            other,
        )
        for step in range(steps)
    ]

    @pl.when(section != 0)
    def _():
        start_g.start()

    for name in loads:
        loads[name].start()
    vec_out[...] = jnp.zeros_like(vec_out)
    loads["n2"].wait()
    loads["rs2"].wait()

    @pl.when(section != 0)
    def _():
        start_g.wait()

    def add_row(row, value):
        vec_out[row : row + 1, :] += jnp.sum(value, axis=0, keepdims=True)

    def norm_back(arriving, normal, scale, gain):
        scaled = arriving * gain
        return (
            scaled
            - jnp.mean(scaled, axis=-1, keepdims=True)
            - normal * jnp.mean(scaled * normal, axis=-1, keepdims=True)
        ) * scale

    for step in range(steps):
        rows = pl.ds(step * STEP, STEP)

        @pl.when(section == 0)
        def _():
            relays[step].wait_recv()

        arriving = g[rows, :].astype(F32)
        normal = n2[rows, :].astype(F32)
        add_row(12, arriving * normal)
        add_row(13, arriving)
        value = norm_back(arriving, normal, rs2[rows, 0:1], vec_ref[4:5, :])
        dsum[rows, :] = value
        value = value.astype(BF)
        low[rows, :] = value
        value = value.astype(F32)
        add_row(9, value)
        low_t[:, rows] = jnp.transpose(value, (1, 0)).astype(BF)

    def to_near(number, unit, which):
        return remote(
            near_out.at[unit, which],
            near_in.at[number, unit, which],
            near_send.at[unit, which],
            near_recv.at[number, unit, which],
            near,
        )

    def to_far(number, unit):
        return remote(
            far_out.at[number, unit],
            far_in.at[number, unit],
            far_send.at[number, unit],
            far_recv.at[number, unit],
            far,
        )

    def gradient(number, unit, rank):
        rows = pl.ds(pl.multiple_of(unit * share, share), share)
        if number == 0:
            return nn(low_t[rows, :], act[rank])
        if number == 1:
            return nn(first_t[rows, :], slope[rank])
        main = nt(x_t[rows, :], p[rank])
        edge = (3 * part // 256) * 256
        tail = nt(low_t[rows, :], p[rank, edge : 4 * part, :])
        lane = lax.broadcasted_iota(jnp.int32, tail.shape, 1)
        tail = jnp.where(lane < 3 * part - edge, main[:, edge:], tail)
        return jnp.concatenate([main[:, :edge], tail], axis=1)

    def reduce_stage(number):
        def body(index, carry):
            @pl.when(index < units)
            def _():
                for which, rank in ((1, 3), (0, 1)):
                    if number > 0:
                        to_near(number - 1, index, which).wait_send()
                    near_out[index, which] = gradient(number, index, rank).astype(BF)
                    to_near(number, index, which).start()

            @pl.when(index > 0)
            def _():
                unit = index - 1
                mine = gradient(number, unit, 2)
                to_near(number, unit, 1).wait_recv()
                far_out[number, unit] = (mine + near_in[number, unit, 1].astype(F32)).astype(BF)
                to_far(number, unit).start()
                mine = gradient(number, unit, 0)
                to_near(number, unit, 0).wait_recv()
                sums[number, unit] = (mine + near_in[number, unit, 0].astype(F32)).astype(BF)

            return carry

        lax.fori_loop(0, units + 1, body, 0)

    loads["act"].wait()

    @pl.when(section == 0)
    def _():
        reduce_stage(0)

    loads["wd"].wait()
    loads["slope"].wait()
    block = 256
    blocks = wu.shape[2] // block

    def narrow(index, carry):
        rank = index // blocks
        columns = pl.ds(pl.multiple_of((index % blocks) * block, block), block)
        value = nt(low[...], wd[rank, columns, :]) * slope[rank, :, columns].astype(F32)
        value = value.astype(BF)
        slope[rank, :, columns] = value
        vec_out[pl.ds(rank, 1), columns] = jnp.sum(value.astype(F32), axis=0, keepdims=True)
        return carry

    lax.fori_loop(0, ranks * blocks, narrow, 0)
    loads["n1"].wait()
    loads["rs1"].wait()

    def first_transpose(step, carry):
        rows = pl.ds(pl.multiple_of(step * STEP, STEP), STEP)
        value = n1[rows, :].astype(F32) * vec_ref[1:2, :] + vec_ref[2:3, :]
        first_t[:, rows] = jnp.transpose(value, (1, 0)).astype(BF)
        return carry

    lax.fori_loop(0, steps, first_transpose, 0)

    @pl.when(section == 0)
    def _():
        reduce_stage(1)

    loads["wu"].wait()

    if True:

        @pl.when(section != 0)
        def _():
            reduce_stage(0)

    def first_back(step, carry):
        rows = pl.ds(pl.multiple_of(step * STEP, STEP), STEP)
        arriving = dsum[rows, :]
        for rank in range(ranks):
            arriving = arriving + nt(slope[rank, rows, :], wu[rank])
        normal = n1[rows, :].astype(F32)
        add_row(10, arriving * normal)
        add_row(11, arriving)
        value = norm_back(arriving, normal, rs1[rows, 0:1], vec_ref[1:2, :])
        dsum[rows, :] = value
        value = value.astype(BF)
        low[rows, :] = value
        value = value.astype(F32)
        add_row(8, value)
        low_t[:, rows] = jnp.transpose(value, (1, 0)).astype(BF)
        return carry

    lax.fori_loop(0, steps, first_back, 0)
    loads["wa"].wait()
    loads["p"].wait()
    loads["lse"].wait()

    def context_back(rank, carry):
        dcontext[rank] = nt(wa[rank, 3 * part : 4 * part, :], low[...]).astype(BF)
        return carry

    lax.fori_loop(0, ranks, context_back, 0)
    visible = lax.broadcasted_iota(jnp.int32, (length, length), 0) < length_ref[0, 0]

    def attend_back(head, carry):
        rank = head // heads
        base = (head % heads) * HD
        at_query = pl.ds(pl.multiple_of(base, HD), HD)
        at_keys = pl.ds(pl.multiple_of(part + base, HD), HD)
        at_values = pl.ds(pl.multiple_of(2 * part + base, HD), HD)
        query = (p[rank, at_query, :].astype(F32) * HD ** (-0.5)).astype(BF)
        keys = p[rank, at_keys, :]
        values = p[rank, at_values, :]
        dout = dcontext[rank, at_query, :]
        weights = jnp.where(visible, jnp.exp(tn(keys, query) - lse[head]), 0.0)
        dweights = tn(values, dout)
        inner = jnp.sum(weights * dweights, axis=0, keepdims=True)
        dscores = (weights * (dweights - inner)).astype(BF)
        p[rank, at_query, :] = (nn(keys, dscores) * HD ** (-0.5)).astype(BF)
        p[rank, at_keys, :] = nt(query, dscores).astype(BF)
        p[rank, at_values, :] = nt(dout, weights.astype(BF)).astype(BF)
        return carry

    lax.fori_loop(0, ranks * heads, attend_back, 0)
    for rank in range(ranks):
        vec_out[4 + rank : 5 + rank, :] = nt(jnp.ones((8, length), BF), p[rank])[0:1, :]
    loads["xb"].wait()

    def entering_transpose(step, carry):
        rows = pl.ds(pl.multiple_of(step * STEP, STEP), STEP)
        x_t[:, rows] = jnp.transpose(xb[rows, :].astype(F32), (1, 0)).astype(BF)
        return carry

    lax.fori_loop(0, steps, entering_transpose, 0)

    for step in range(steps):
        rows = pl.ds(step * STEP, STEP)
        total = dsum[rows, :]
        for rank in range(ranks):
            total = total + tn(p[rank, 0 : 3 * part, rows], wa[rank, 0 : 3 * part, :])
        dx[rows, :] = total.astype(BF)

        @pl.when(section != 0)
        def _():
            relays[step].start()

    dx_copy = pltpu.make_async_copy(dx, dx_out, out_sem.at[0])
    dx_copy.start()

    @pl.when(section != 0)
    def _():
        reduce_stage(1)

    reduce_stage(2)

    def finish(index, carry):
        number = index // units
        unit = index % units
        to_far(number, unit).wait_recv()
        sums[number, unit] = (
            sums[number, unit].astype(F32) + far_in[number, unit].astype(F32)
        ).astype(BF)
        return carry

    lax.fori_loop(0, 3 * units, finish, 0)
    sums_copy = pltpu.make_async_copy(sums, sums_out, out_sem.at[1])
    sums_copy.start()
    for unit in range(units):
        for which in range(2):
            to_near(2, unit, which).wait_send()
    for number in range(3):
        for unit in range(units):
            to_far(number, unit).wait_send()

    @pl.when(section != 0)
    def _():
        for relay in relays:
            relay.wait_send()

    dx_copy.wait()
    sums_copy.wait()


def backward(cotangent, saved, length_here, vectors):
    wa, wu, wd, p, lse, act, slope, n1, n2, rs1, rs2, x = saved
    ranks = wa.shape[0]
    length, width = x.shape
    steps = length // STEP
    units = 4
    share = width // units
    anywhere = pl.BlockSpec(memory_space=pl.ANY)
    inside = pl.BlockSpec(memory_space=pltpu.VMEM)
    part = wa.shape[1] // 4

    def like(value):
        return pltpu.VMEM(value.shape, value.dtype)

    plane = (length, width)
    turned = (width, length)
    chunk = (share, width)
    return pl.pallas_call(
        backward_kernel,
        name="backward_layer",
        out_shape=(
            jax.ShapeDtypeStruct((3, units) + chunk, BF),
            jax.ShapeDtypeStruct(plane, BF),
            jax.ShapeDtypeStruct((16, width), F32),
        ),
        in_specs=[anywhere] * 13 + [pl.BlockSpec(memory_space=pltpu.SMEM), inside],
        out_specs=(anywhere, anywhere, inside),
        scratch_shapes=[like(value) for value in saved]
        + [
            pltpu.VMEM(plane, BF),
            pltpu.VMEM(plane, F32),
            pltpu.VMEM(plane, BF),
            pltpu.VMEM(turned, BF),
            pltpu.VMEM(turned, BF),
            pltpu.VMEM(turned, BF),
            pltpu.VMEM((ranks, part, length), BF),
            pltpu.VMEM(plane, BF),
            pltpu.VMEM((units, 2) + chunk, BF),
            pltpu.VMEM((3, units, 2) + chunk, BF),
            pltpu.VMEM((3, units) + chunk, BF),
            pltpu.VMEM((3, units) + chunk, BF),
            pltpu.VMEM((3, units) + chunk, BF),
            pltpu.SemaphoreType.DMA((13,)),
            pltpu.SemaphoreType.DMA((units, 2)),
            pltpu.SemaphoreType.DMA((3, units, 2)),
            pltpu.SemaphoreType.DMA((3, units)),
            pltpu.SemaphoreType.DMA((3, units)),
            pltpu.SemaphoreType.DMA((steps,)),
            pltpu.SemaphoreType.DMA((steps,)),
            pltpu.SemaphoreType.DMA((2,)),
        ],
        compiler_params=pltpu.CompilerParams(
            collective_id=1, has_side_effects=True, vmem_limit_bytes=VMEM_LIMIT
        ),
        cost_estimate=pl.CostEstimate(
            flops=17_000_000_000, bytes_accessed=60_000_000, transcendentals=3_000_000
        ),
    )(cotangent, *saved, length_here, vectors)


def on_device(
    inputs,
    cotangent,
    segment_ids,
    column_ids,
    row_ids,
    answer_ids,
    lengths,
    type_table,
    query_weight,
    query_bias,
    key_weight,
    value_weight,
    value_bias,
    output_weight,
    output_bias,
    first_gain,
    first_shift,
    up_weight,
    up_bias,
    down_weight,
    down_bias,
    second_gain,
    second_shift,
):
    section = lax.axis_index("section")
    tensor = lax.axis_index("tensor")
    ranks = lax.axis_size("tensor")
    micro_count, sequences, length, width = inputs.shape
    items = micro_count * sequences
    type_count = 4 + COLS + ROWS
    padded_types = -(-type_count // 16) * 16
    part = query_weight.shape[2]
    hidden = up_weight.shape[2]

    ids = jnp.stack(
        [segment_ids, column_ids + 2, row_ids + 2 + COLS, answer_ids + 2 + COLS + ROWS], axis=-1
    ).reshape(items, length, 4)
    own_ids = lax.dynamic_index_in_dim(ids, tensor, 0, keepdims=False)
    length_here = lax.dynamic_slice_in_dim(lengths.reshape(items), tensor, 1, 0).reshape(1, 1)
    table = jnp.pad(type_table, ((0, padded_types - type_count), (0, 0)))
    wa = jnp.concatenate(
        [query_weight[0].T, key_weight[0].T, value_weight[0].T, output_weight[0]], axis=0
    )
    gap = jnp.zeros((part,), F32)
    bias = jnp.zeros((8, hidden), F32)
    bias = bias.at[0].set(up_bias[0].astype(F32))
    bias = bias.at[1].set(
        jnp.concatenate([query_bias[0].astype(F32), gap, value_bias[0].astype(F32), gap])
    )
    vectors = jnp.concatenate(
        [output_bias, first_gain, first_shift, down_bias, second_gain, second_shift]
    ).astype(F32)
    vectors = jnp.pad(vectors, ((0, 2), (0, 0)))

    results = forward(
        inputs, own_ids, table, length_here, wa, up_weight[0], down_weight[0], bias, vectors, ranks
    )
    saved, leaving = results[:-1], results[-1]
    layer_outputs = lax.all_to_all(leaving, "tensor", split_axis=1, concat_axis=0, tiled=True)
    layer_outputs = layer_outputs.reshape(1, micro_count, sequences, length, width // ranks)

    sums, dx, vecs = backward(cotangent, saved, length_here, vectors)

    dcolumns = lax.all_to_all(dx, "tensor", split_axis=1, concat_axis=0, tiled=True)
    layer_input_grads = dcolumns.astype(F32).reshape(
        1, micro_count, sequences, length, width // ranks
    )
    picks = jax.nn.one_hot(ids.reshape(items * length, 4), type_count, dtype=BF).sum(axis=1)
    table_term = lax.dot_general(
        picks, dcolumns, (((0,), (0,)), ((), ())), preferred_element_type=F32
    )
    table_term = jnp.where(section == 0, table_term, 0.0).astype(BF)
    table_sum = lax.psum(table_term, "dp")
    table_grad = lax.psum_scatter(table_sum, "section", scatter_dimension=0, tiled=True).astype(F32)

    summed = lax.psum_scatter(
        sums.reshape(3, width, width), "dp", scatter_dimension=1, tiled=True
    ).astype(F32)
    order = jnp.arange(ranks) ^ tensor
    packed = jnp.concatenate(
        [jnp.take(vecs[0:ranks], order, axis=0), jnp.take(vecs[4 : 4 + ranks], order, axis=0)]
        + [vecs[row].reshape(ranks, width // ranks) for row in range(8, 14)],
        axis=1,
    )
    packed = lax.psum(packed, ("tensor", "dp"))
    mine = lax.dynamic_slice_in_dim(packed, tensor, 1, 0)

    def vector(start, count):
        return mine[:, start : start + count]

    share = width // ranks
    after = 2 * width
    return (
        layer_outputs,
        layer_input_grads,
        summed[2, :, 0:part][None],
        vector(width, part),
        summed[2, :, part : 2 * part][None],
        summed[2, :, 2 * part : 3 * part][None],
        vector(width + 2 * part, part),
        summed[2, :, 3 * part : 4 * part].T[None],
        vector(after, share),
        vector(after + 2 * share, share),
        vector(after + 3 * share, share),
        summed[1][None],
        vector(0, hidden),
        summed[0].T[None],
        vector(after + share, share),
        vector(after + 4 * share, share),
        vector(after + 5 * share, share),
        table_grad,
    )


def solution(mesh):
    return jax.shard_map(
        on_device,
        mesh=mesh,
        in_specs=(
            P(None, "dp", None, None),
            P(None, "dp", None, None),
            P(None, "dp", None),
            P(None, "dp", None),
            P(None, "dp", None),
            P(None, "dp", None),
            P(None, "dp"),
            P(),
            P("section", None, "tensor"),
            P("section", "tensor"),
            P("section", None, "tensor"),
            P("section", None, "tensor"),
            P("section", "tensor"),
            P("section", "tensor", None),
            P("section", None),
            P("section", None),
            P("section", None),
            P("section", None, "tensor"),
            P("section", "tensor"),
            P("section", "tensor", None),
            P("section", None),
            P("section", None),
            P("section", None),
        ),
        out_specs=(
            P("section", None, "dp", None, "tensor"),
            P("section", None, "dp", None, "tensor"),
            P("section", "dp", "tensor"),
            P("section", "tensor"),
            P("section", "dp", "tensor"),
            P("section", "dp", "tensor"),
            P("section", "tensor"),
            P("section", "tensor", "dp"),
            P("section", "tensor"),
            P("section", "tensor"),
            P("section", "tensor"),
            P("section", "dp", "tensor"),
            P("section", "tensor"),
            P("section", "tensor", "dp"),
            P("section", "tensor"),
            P("section", "tensor"),
            P("section", "tensor"),
            P("section", "tensor"),
        ),
        check_vma=False,
    )
```

```python
import functools

import jax
import jax.numpy as jnp
from jax import lax
from jax.experimental import pallas as pl
from jax.experimental.pallas import tpu as pltpu
from jax.sharding import PartitionSpec as P

HD = 64
COLS = 256
ROWS = 256
EPSILON = 1e-12
MASKED = -1e30
BF = jnp.bfloat16
F32 = jnp.float32
MESH = pl.DeviceIdType.MESH
VMEM_LIMIT = 60 * 1024 * 1024
STEP = 128


def nn(left, right):
    return lax.dot_general(left, right, (((1,), (0,)), ((), ())), preferred_element_type=F32)


def nt(left, right):
    return lax.dot_general(left, right, (((1,), (1,)), ((), ())), preferred_element_type=F32)


def tn(left, right):
    return lax.dot_general(left, right, (((0,), (0,)), ((), ())), preferred_element_type=F32)


def normalize(value):
    centered = value - jnp.mean(value, axis=-1, keepdims=True)
    variance = jnp.mean(centered * centered, axis=-1, keepdims=True)
    scale = lax.rsqrt(variance + EPSILON)
    return centered * scale, scale


def place():
    section = lax.axis_index("section")
    data = lax.axis_index("dp")
    tensor = lax.axis_index("tensor")
    beside = tensor + 1 - 2 * (tensor % 2)
    across = tensor + 2 - 4 * ((tensor // 2) % 2)
    return section, data, tensor, beside, across


def greet(partners):
    barrier = pltpu.get_barrier_semaphore()
    for partner in partners:
        pl.semaphore_signal(barrier, inc=1, device_id=partner, device_id_type=MESH)
    pl.semaphore_wait(barrier, len(partners))


def remote(src, dst, send, recv, device):
    return pltpu.make_async_remote_copy(
        src_ref=src, dst_ref=dst, send_sem=send, recv_sem=recv, device_id=device, device_id_type=MESH
    )


def forward_kernel(
    inputs_ref,
    ids_ref,
    table_ref,
    length_ref,
    wa_ref,
    wu_ref,
    wd_ref,
    bias_ref,
    vec_ref,
    wa_out,
    wu_out,
    wd_out,
    p_out,
    lse_out,
    act_out,
    slope_out,
    n1_out,
    n2_out,
    rs1_out,
    rs2_out,
    x_out,
    y_out,
    wa,
    wu,
    wd,
    bias,
    p,
    lse,
    act,
    slope,
    xf,
    xb,
    first,
    low,
    n1,
    n2,
    rs1,
    rs2,
    y,
    gather_send,
    gather_recv,
    relay_send,
    relay_recv,
    local_sem,
    out_sem,
):
    section, data, tensor, beside, across = place()
    length, width = xf.shape
    ranks = wa.shape[0]
    heads = wa.shape[1] // (4 * HD)
    part = heads * HD
    steps = length // STEP
    sequences = inputs_ref.shape[1]
    near = (section, data, beside)
    far = (section, data, across)
    other = (1 - section, data, tensor)
    greet((near, far, other))

    shards = ((wa_ref, wa), (bias_ref, bias), (wu_ref, wu), (wd_ref, wd))
    to_far = []
    to_near = []
    onward = []
    own = []
    for number, (source, target) in enumerate(shards):
        to_far.append(
            remote(source, target.at[2], gather_send.at[number, 0], gather_recv.at[number, 0], far)
        )
        to_near.append(
            remote(source, target.at[1], gather_send.at[number, 1], gather_recv.at[number, 1], near)
        )
        onward.append(
            remote(
                target.at[2], target.at[3], gather_send.at[number, 2], gather_recv.at[number, 2], near
            )
        )
        own.append(pltpu.make_async_copy(source, target.at[0], local_sem.at[number]))
    for copy in to_far:
        copy.start()
    for copy in to_near:
        copy.start()
    for copy in own:
        copy.start()

    def pass_on(number):
        to_far[number].wait_recv()
        onward[number].start()

    def ready(number):
        own[number].wait()
        to_near[number].wait_recv()
        onward[number].wait_recv()

    out_copies = []

    def put_out(source, target):
        copy = pltpu.make_async_copy(source, target, out_sem.at[len(out_copies)])
        copy.start()
        out_copies.append(copy)

    relays = [
        remote(
            y.at[pl.ds(step * STEP, STEP)],
            xb.at[pl.ds(step * STEP, STEP)],
            relay_send.at[step],
            relay_recv.at[step],
            other,
        )
        for step in range(steps)
    ]

    @pl.when(section == 0)
    def _():
        copy = pltpu.make_async_copy(
            inputs_ref.at[tensor // sequences, tensor % sequences], xb, local_sem.at[4]
        )
        copy.start()
        copy.wait()

        def embed(step, carry):
            rows = pl.ds(pl.multiple_of(step * STEP, STEP), STEP)
            lane = lax.broadcasted_iota(jnp.int32, (STEP, table_ref.shape[0]), 1)
            picks = jnp.zeros((STEP, table_ref.shape[0]), F32)
            for column in range(4):
                picks = picks + jnp.where(ids_ref[rows, column : column + 1] == lane, 1.0, 0.0)
            value = xb[rows, :].astype(F32) + nn(picks.astype(BF), table_ref[...])
            xf[rows, :] = value
            xb[rows, :] = value.astype(BF)
            return carry

        lax.fori_loop(0, steps, embed, 0)

    pass_on(0)
    pass_on(1)

    @pl.when(section != 0)
    def _():
        for relay in relays:
            relay.wait_recv()
        xf[...] = xb[...].astype(F32)

    ready(0)
    ready(1)
    put_out(wa, wa_out)
    put_out(xb, x_out)

    def project(rank, carry):
        columns = jnp.transpose(bias[rank], (1, 0))
        p[rank, 0 : 3 * part, :] = (
            nt(wa[rank, 0 : 3 * part, :], xb[...]) + columns[0 : 3 * part, 1:2]
        ).astype(BF)
        return carry

    lax.fori_loop(0, ranks, project, 0)
    pass_on(2)

    visible = lax.broadcasted_iota(jnp.int32, (length, length), 0) < length_ref[0, 0]

    def attend(head, carry):
        rank = head // heads
        base = (head % heads) * HD
        query = p[rank, pl.ds(pl.multiple_of(base, HD), HD), :]
        keys = p[rank, pl.ds(pl.multiple_of(part + base, HD), HD), :]
        values = p[rank, pl.ds(pl.multiple_of(2 * part + base, HD), HD), :]
        query = (query.astype(F32) * HD ** (-0.5)).astype(BF)
        scores = jnp.where(visible, tn(keys, query), MASKED)
        maximum = jnp.max(scores, axis=0, keepdims=True)
        raised = jnp.exp(scores - maximum)
        total = jnp.sum(raised, axis=0, keepdims=True)
        context = nn(values, raised.astype(BF)) / total
        p[rank, pl.ds(pl.multiple_of(3 * part + base, HD), HD), :] = context.astype(BF)
        lse[head] = maximum + jnp.log(total)
        return carry

    lax.fori_loop(0, ranks * heads, attend, 0)
    put_out(p, p_out)
    put_out(lse, lse_out)

    def first_norm(step, carry):
        rows = pl.ds(pl.multiple_of(step * STEP, STEP), STEP)
        total = xf[rows, :] + vec_ref[0:1, :]
        for rank in range(ranks):
            total = total + tn(p[rank, 3 * part : 4 * part, rows], wa[rank, 3 * part : 4 * part, :])
        normal, scale = normalize(total)
        value = normal * vec_ref[1:2, :] + vec_ref[2:3, :]
        first[rows, :] = value
        low[rows, :] = value.astype(BF)
        n1[rows, :] = normal.astype(BF)
        rs1[rows, :] = jnp.broadcast_to(scale, (STEP, 128))
        return carry

    lax.fori_loop(0, steps, first_norm, 0)
    put_out(n1, n1_out)
    put_out(rs1, rs1_out)
    ready(2)
    put_out(wu, wu_out)
    block = 256
    blocks = wu.shape[2] // block

    def widen(index, carry):
        rank = index // blocks
        columns = pl.ds(pl.multiple_of((index % blocks) * block, block), block)
        hidden = nn(low[...], wu[rank, :, columns]) + bias[rank, 0:1, columns]
        inner = 0.5 * (1.0 + lax.erf(hidden * (0.5**0.5)))
        act[rank, :, columns] = (hidden * inner).astype(BF)
        density = jnp.exp(hidden * hidden * (-0.5)) * 0.3989422804014327
        slope[rank, :, columns] = (inner + hidden * density).astype(BF)
        return carry

    lax.fori_loop(0, ranks * blocks, widen, 0)
    put_out(act, act_out)
    put_out(slope, slope_out)
    pass_on(3)
    ready(3)
    put_out(wd, wd_out)

    for step in range(steps):
        rows = pl.ds(step * STEP, STEP)
        total = first[rows, :] + vec_ref[3:4, :]
        for rank in range(ranks):
            total = total + nn(act[rank, rows, :], wd[rank])
        normal, scale = normalize(total)
        y[rows, :] = (normal * vec_ref[4:5, :] + vec_ref[5:6, :]).astype(BF)
        n2[rows, :] = normal.astype(BF)
        rs2[rows, :] = jnp.broadcast_to(scale, (STEP, 128))

        @pl.when(section == 0)
        def _():
            relays[step].start()

    put_out(n2, n2_out)
    put_out(rs2, rs2_out)
    put_out(y, y_out)
    for copy in out_copies:
        copy.wait()
    for group in (to_far, to_near, onward):
        for copy in group:
            copy.wait_send()

    @pl.when(section == 0)
    def _():
        for relay in relays:
            relay.wait_send()


def forward(inputs, ids, table, length_here, wa, wu, wd, bias, vectors, ranks):
    length, width = inputs.shape[2], inputs.shape[3]
    rows_a = wa.shape[0]
    hidden = wu.shape[1]
    heads = ranks * (rows_a // (4 * HD))
    steps = length // STEP
    shapes = dict(
        wa=((ranks, rows_a, width), BF),
        wu=((ranks, width, hidden), BF),
        wd=((ranks, hidden, width), BF),
        p=((ranks, rows_a, length), BF),
        lse=((heads, 1, length), F32),
        act=((ranks, length, hidden), BF),
        slope=((ranks, length, hidden), BF),
        n1=((length, width), BF),
        n2=((length, width), BF),
        rs1=((length, 128), F32),
        rs2=((length, 128), F32),
        x=((length, width), BF),
        y=((length, width), BF),
    )

    def buffer(name):
        return pltpu.VMEM(*shapes[name])

    outs = ("wa", "wu", "wd", "p", "lse", "act", "slope", "n1", "n2", "rs1", "rs2", "x", "y")
    anywhere = pl.BlockSpec(memory_space=pl.ANY)
    inside = pl.BlockSpec(memory_space=pltpu.VMEM)
    return pl.pallas_call(
        forward_kernel,
        name="forward_layer",
        out_shape=tuple(jax.ShapeDtypeStruct(*shapes[name]) for name in outs),
        in_specs=[
            anywhere,
            inside,
            inside,
            pl.BlockSpec(memory_space=pltpu.SMEM),
            anywhere,
            anywhere,
            anywhere,
            anywhere,
            inside,
        ],
        out_specs=tuple(anywhere for _ in outs),
        scratch_shapes=[
            buffer("wa"),
            buffer("wu"),
            buffer("wd"),
            pltpu.VMEM((ranks,) + bias.shape, F32),
            buffer("p"),
            buffer("lse"),
            buffer("act"),
            buffer("slope"),
            pltpu.VMEM((length, width), F32),
            buffer("x"),
            pltpu.VMEM((length, width), F32),
            pltpu.VMEM((length, width), BF),
            buffer("n1"),
            buffer("n2"),
            buffer("rs1"),
            buffer("rs2"),
            buffer("y"),
            pltpu.SemaphoreType.DMA((4, 3)),
            pltpu.SemaphoreType.DMA((4, 3)),
            pltpu.SemaphoreType.DMA((steps,)),
            pltpu.SemaphoreType.DMA((steps,)),
            pltpu.SemaphoreType.DMA((5,)),
            pltpu.SemaphoreType.DMA((len(outs),)),
        ],
        compiler_params=pltpu.CompilerParams(
            collective_id=0, has_side_effects=True, vmem_limit_bytes=VMEM_LIMIT
        ),
        cost_estimate=pl.CostEstimate(
            flops=8_000_000_000, bytes_accessed=60_000_000, transcendentals=6_000_000
        ),
    )(inputs, ids, table, length_here, wa, wu, wd, bias, vectors)


def backward_kernel(
    inner,
    cotangent_ref,
    wa_ref,
    wu_ref,
    wd_ref,
    p_ref,
    lse_ref,
    act_ref,
    slope_ref,
    n1_ref,
    n2_ref,
    rs1_ref,
    rs2_ref,
    x_ref,
    y_ref,
    length_ref,
    vec_ref,
    ids_ref,
    sums_out,
    dx_out,
    y_out,
    vec_out,
    table_out,
    wa,
    wu,
    wd,
    p,
    lse,
    act,
    slope,
    n1,
    n2,
    rs1,
    rs2,
    xb,
    y,
    g,
    dsum,
    low,
    low_t,
    out_t,
    first_t,
    x_t,
    dcontext,
    dx,
    dx_t,
    dx_in,
    y_t,
    near_out,
    near_in,
    far_in,
    depth_in,
    final,
    vec,
    vec_in,
    table,
    table_away,
    table_in,
    load_sem,
    near_send,
    near_recv,
    far_send,
    far_recv,
    depth_send,
    depth_recv,
    relay_send,
    relay_recv,
    dx_send,
    dx_recv,
    y_send,
    y_recv,
    vec_send,
    vec_recv,
    table_send,
    table_recv,
    out_sem,
):
    section, data, tensor, beside, across = place()
    diagonal = beside + 2 - 4 * ((beside // 2) % 2)
    length, width = g.shape
    ranks = wa.shape[0]
    heads = wa.shape[1] // (4 * HD)
    part = heads * HD
    steps = length // STEP
    sequences = cotangent_ref.shape[1]
    units = near_in.shape[1]
    share = near_in.shape[3]
    columns_each = width // ranks
    depth = lax.axis_size("dp")
    near = (section, data, beside)
    far = (section, data, across)
    corner = (section, data, diagonal)
    other = (1 - section, data, tensor)
    deep = []
    if inner:
        deep = [(section, (data + 1 + hop) % depth, tensor) for hop in range(depth - 1)]
    greet([near, far, corner, other] + deep)

    loads = {}
    for name, source, target in (
        ("y", y_ref, y),
        ("n2", n2_ref, n2),
        ("rs2", rs2_ref, rs2),
        ("wd", wd_ref, wd),
        ("slope", slope_ref, slope),
        ("wu", wu_ref, wu),
        ("act", act_ref, act),
        ("n1", n1_ref, n1),
        ("rs1", rs1_ref, rs1),
        ("wa", wa_ref, wa),
        ("p", p_ref, p),
        ("lse", lse_ref, lse),
        ("xb", x_ref, xb),
    ):
        loads[name] = pltpu.make_async_copy(source, target, load_sem.at[len(loads)])
    start_g = pltpu.make_async_copy(
        cotangent_ref.at[tensor // sequences, tensor % sequences], g, load_sem.at[len(loads)]
    )
    relays = [
        remote(
            dx.at[pl.ds(step * STEP, STEP)],
            g.at[pl.ds(step * STEP, STEP)],
            relay_send.at[step],
            relay_recv.at[step],
            other,
        )
        for step in range(steps)
    ]
    around = ((beside, near), (across, far), (diagonal, corner))
    y_copies = [
        remote(y_t.at[rank], y_out.at[tensor], y_send.at[number], y_recv.at[number], device)
        for number, (rank, device) in enumerate(around)
    ]
    y_own = pltpu.make_async_copy(y_t.at[tensor], y_out.at[tensor], out_sem.at[0])
    dx_copies = [
        remote(dx_t.at[rank], dx_in.at[tensor], dx_send.at[number], dx_recv.at[number], device)
        for number, (rank, device) in enumerate(around)
    ]

    def turn(source, target):
        def body(step, carry):
            rows = pl.ds(pl.multiple_of(step * STEP, STEP), STEP)
            value = jnp.transpose(source[rows, :].astype(F32), (1, 0)).astype(BF)
            for rank in range(ranks):
                target[rank, :, rows] = value[rank * columns_each : (rank + 1) * columns_each]
            return carry

        lax.fori_loop(0, steps, body, 0)

    def share_outputs():
        turn(y, y_t)
        for copy in y_copies:
            copy.start()
        y_own.start()

    @pl.when(section != 0)
    def _():
        start_g.start()

    for name in loads:
        loads[name].start()
    vec[0] = jnp.zeros(vec.shape[1:], F32)
    loads["y"].wait()

    @pl.when(section == 0)
    def _():
        share_outputs()

    loads["n2"].wait()
    loads["rs2"].wait()

    @pl.when(section != 0)
    def _():
        start_g.wait()

    def add_row(row, value):
        vec[0, row : row + 1, :] += jnp.sum(value, axis=0, keepdims=True)

    def norm_back(arriving, normal, scale, gain):
        scaled = arriving * gain
        return (
            scaled
            - jnp.mean(scaled, axis=-1, keepdims=True)
            - normal * jnp.mean(scaled * normal, axis=-1, keepdims=True)
        ) * scale

    for step in range(steps):
        rows = pl.ds(step * STEP, STEP)

        @pl.when(section == 0)
        def _():
            relays[step].wait_recv()

        arriving = g[rows, :].astype(F32)
        normal = n2[rows, :].astype(F32)
        add_row(12, arriving * normal)
        add_row(13, arriving)
        value = norm_back(arriving, normal, rs2[rows, 0:1], vec_ref[4:5, :])
        dsum[rows, :] = value
        value = value.astype(BF)
        low[rows, :] = value
        value = value.astype(F32)
        add_row(9, value)
        low_t[:, rows] = jnp.transpose(value, (1, 0)).astype(BF)

    def to_near(number, unit, which):
        return remote(
            near_out.at[unit, which],
            near_in.at[number, unit, which],
            near_send.at[unit, which],
            near_recv.at[number, unit, which],
            near,
        )

    def to_far(number, unit):
        return remote(
            near_in.at[number, unit, 1],
            far_in.at[number, unit],
            far_send.at[number, unit],
            far_recv.at[number, unit],
            far,
        )

    def to_depth(number, unit):
        return remote(
            near_in.at[number, unit, 0],
            depth_in.at[number, unit],
            depth_send.at[number, unit],
            depth_recv.at[number, unit],
            (section, (data + 1 + unit) % depth, tensor),
        )

    def gradient(number, unit, rank):
        at = (data + 1 + unit) % depth if inner else unit
        rows = pl.ds(pl.multiple_of(at * share, share), share)
        if number == 0:
            return nn(low_t[rows, :], act[rank])
        if number == 1:
            return nn(first_t[rows, :], slope[rank])
        main = nt(x_t[rows, :], p[rank])
        edge = (3 * part // 256) * 256
        tail = nt(out_t[rows, :], p[rank, edge : 4 * part, :])
        lane = lax.broadcasted_iota(jnp.int32, tail.shape, 1)
        tail = jnp.where(lane < 3 * part - edge, main[:, edge:], tail)
        return jnp.concatenate([main[:, :edge], tail], axis=1)

    def reduce_stage(number):
        def body(index, carry):
            @pl.when(index < units)
            def _():
                for which, rank in ((1, 3), (0, 1)):
                    if number > 0:
                        to_near(number - 1, index, which).wait_send()
                    near_out[index, which] = gradient(number, index, rank).astype(BF)
                    to_near(number, index, which).start()

            @pl.when(index > 0)
            def _():
                unit = index - 1
                for which, rank in ((1, 2), (0, 0)):
                    mine = gradient(number, unit, rank)
                    to_near(number, unit, which).wait_recv()
                    near_in[number, unit, which] = (
                        mine + near_in[number, unit, which].astype(F32)
                    ).astype(BF)
                    if which == 1:
                        to_far(number, unit).start()

            return carry

        lax.fori_loop(0, units + 1, body, 0)

    def finish(index):
        number = index // units
        unit = index % units
        to_far(number, unit).wait_recv()
        near_in[number, unit, 0] = (
            near_in[number, unit, 0].astype(F32) + far_in[number, unit].astype(F32)
        ).astype(BF)
        if inner:

            @pl.when(unit < units - 1)
            def _():
                to_depth(number, unit).start()

    loads["act"].wait()

    @pl.when(section == 0)
    def _():
        reduce_stage(0)

    loads["wd"].wait()
    loads["slope"].wait()
    block = 256
    blocks = wu.shape[2] // block

    def narrow(index, carry):
        rank = index // blocks
        columns = pl.ds(pl.multiple_of((index % blocks) * block, block), block)
        value = nt(low[...], wd[rank, columns, :]) * slope[rank, :, columns].astype(F32)
        value = value.astype(BF)
        slope[rank, :, columns] = value
        vec[0, pl.ds(rank, 1), columns] = jnp.sum(value.astype(F32), axis=0, keepdims=True)
        return carry

    lax.fori_loop(0, ranks * blocks, narrow, 0)
    loads["n1"].wait()
    loads["rs1"].wait()

    def first_transpose(step, carry):
        rows = pl.ds(pl.multiple_of(step * STEP, STEP), STEP)
        value = n1[rows, :].astype(F32) * vec_ref[1:2, :] + vec_ref[2:3, :]
        first_t[:, rows] = jnp.transpose(value, (1, 0)).astype(BF)
        return carry

    lax.fori_loop(0, steps, first_transpose, 0)

    @pl.when(section == 0)
    def _():
        reduce_stage(1)

    loads["wu"].wait()

    def first_back(step, carry):
        rows = pl.ds(pl.multiple_of(step * STEP, STEP), STEP)
        arriving = dsum[rows, :]
        for rank in range(ranks):
            arriving = arriving + nt(slope[rank, rows, :], wu[rank])
        normal = n1[rows, :].astype(F32)
        add_row(10, arriving * normal)
        add_row(11, arriving)
        value = norm_back(arriving, normal, rs1[rows, 0:1], vec_ref[1:2, :])
        dsum[rows, :] = value
        value = value.astype(BF)
        low[rows, :] = value
        value = value.astype(F32)
        add_row(8, value)
        out_t[:, rows] = jnp.transpose(value, (1, 0)).astype(BF)
        return carry

    lax.fori_loop(0, steps, first_back, 0)

    @pl.when(section == 0)
    def _():
        finish(0)
        finish(1)

    loads["wa"].wait()
    loads["p"].wait()
    loads["lse"].wait()

    def context_back(rank, carry):
        dcontext[rank] = nt(wa[rank, 3 * part : 4 * part, :], low[...]).astype(BF)
        return carry

    lax.fori_loop(0, ranks, context_back, 0)
    visible = lax.broadcasted_iota(jnp.int32, (length, length), 0) < length_ref[0, 0]

    def attend_back(head, carry):
        rank = head // heads
        base = (head % heads) * HD
        at_query = pl.ds(pl.multiple_of(base, HD), HD)
        at_keys = pl.ds(pl.multiple_of(part + base, HD), HD)
        at_values = pl.ds(pl.multiple_of(2 * part + base, HD), HD)
        query = (p[rank, at_query, :].astype(F32) * HD ** (-0.5)).astype(BF)
        keys = p[rank, at_keys, :]
        values = p[rank, at_values, :]
        dout = dcontext[rank, at_query, :]
        weights = jnp.where(visible, jnp.exp(tn(keys, query) - lse[head]), 0.0)
        dweights = tn(values, dout)
        inner_sum = jnp.sum(weights * dweights, axis=0, keepdims=True)
        dscores = (weights * (dweights - inner_sum)).astype(BF)
        p[rank, at_query, :] = (nn(keys, dscores) * HD ** (-0.5)).astype(BF)
        p[rank, at_keys, :] = nt(query, dscores).astype(BF)
        p[rank, at_values, :] = nt(dout, weights.astype(BF)).astype(BF)

        @pl.when((section == 0) & (head % 3 == 2))
        def _():
            finish(2 + head // 3)

        return carry

    lax.fori_loop(0, ranks * heads, attend_back, 0)
    early = 2 + ranks * heads // 3
    for rank in range(ranks):
        vec[0, 4 + rank : 5 + rank, :] = nt(jnp.ones((8, length), BF), p[rank])[0:1, :]
    vec_near = remote(vec.at[0], vec_in.at[0], vec_send.at[0], vec_recv.at[0], near)
    vec_near.start()
    loads["xb"].wait()

    for step in range(steps):
        rows = pl.ds(step * STEP, STEP)
        total = dsum[rows, :]
        for rank in range(ranks):
            total = total + tn(p[rank, 0 : 3 * part, rows], wa[rank, 0 : 3 * part, :])
        dx[rows, :] = total.astype(BF)

        @pl.when(section != 0)
        def _():
            relays[step].start()

    vec_near.wait_recv()

    def join(level, swap):
        for row in range(vec.shape[1]):
            pair = row ^ swap if row < 8 else row
            vec[level + 1, row : row + 1, :] = (
                vec[level, row : row + 1, :] + vec_in[level, pair : pair + 1, :]
            )

    join(0, 1)
    vec_far = remote(vec.at[1], vec_in.at[1], vec_send.at[1], vec_recv.at[1], far)
    vec_far.start()
    turn(dx, dx_t)
    for copy in dx_copies:
        copy.start()
    dx_in[tensor] = dx_t[tensor]

    @pl.when(section != 0)
    def _():
        reduce_stage(0)
        reduce_stage(1)

    def entering_transpose(step, carry):
        rows = pl.ds(pl.multiple_of(step * STEP, STEP), STEP)
        x_t[:, rows] = jnp.transpose(xb[rows, :].astype(F32), (1, 0)).astype(BF)
        return carry

    lax.fori_loop(0, steps, entering_transpose, 0)
    reduce_stage(2)

    vec_far.wait_recv()
    join(1, 2)
    vec_deep = [
        remote(vec.at[2], vec_in.at[2 + hop], vec_send.at[2 + hop], vec_recv.at[2 + hop], device)
        for hop, device in enumerate(deep)
    ]
    for copy in vec_deep:
        copy.start()

    @pl.when(section != 0)
    def _():
        share_outputs()
        lax.fori_loop(0, early, lambda index, carry: (finish(index), carry)[1], 0)

    for copy in dx_copies:
        copy.wait_recv()
    dx_done = pltpu.make_async_copy(dx_in, dx_out, out_sem.at[1])
    dx_done.start()
    half = table.shape[0]
    table_x = remote(table_away, table, table_send.at[0], table_recv.at[0], other)

    @pl.when(section == 0)
    def _():
        total = jnp.zeros((2 * half, columns_each), F32)
        for item in range(ranks):
            row = lax.broadcasted_iota(jnp.int32, (2 * half, length), 0)
            picks = jnp.zeros((2 * half, length), F32)
            for kind in range(4):
                at = 4 * item + kind
                picks = picks + jnp.where(ids_ref[at : at + 1, :] == row, 1.0, 0.0)
            total = total + nt(picks.astype(BF), dx_in[item])
        table[...] = total[:half].astype(BF)
        table_away[...] = total[half:].astype(BF)
        table_x.start()

    lax.fori_loop(early, 3 * units, lambda index, carry: (finish(index), carry)[1], 0)

    @pl.when(section != 0)
    def _():
        table_x.wait_recv()

    table_deep = [
        remote(
            table, table_in.at[hop], table_send.at[1 + hop], table_recv.at[1 + hop], device
        )
        for hop, device in enumerate(deep)
    ]
    for copy in table_deep:
        copy.start()

    copies = []
    if inner:
        for number in range(3):
            total = near_in[number, units - 1, 0].astype(F32)
            for unit in range(units - 1):
                to_depth(number, unit).wait_recv()
                total = total + depth_in[number, unit].astype(F32)
            final[number] = total
            copy = pltpu.make_async_copy(
                final.at[number], sums_out.at[number], out_sem.at[2 + number]
            )
            copy.start()
            copies.append(copy)
    else:
        copy = pltpu.make_async_copy(
            near_in.at[:, :, 0], sums_out, out_sem.at[2]
        )
        copy.start()
        copies.append(copy)
    total = vec[2]
    for hop, copy in enumerate(vec_deep):
        copy.wait_recv()
        total = total + vec_in[2 + hop]
    vec_out[...] = total
    total = table[...].astype(F32)
    for hop, copy in enumerate(table_deep):
        copy.wait_recv()
        total = total + table_in[hop].astype(F32)
    table_out[...] = total

    for copy in y_copies:
        copy.wait()
    y_own.wait()
    for copy in dx_copies:
        copy.wait_send()
    vec_near.wait_send()
    vec_far.wait_send()
    for copy in vec_deep + table_deep:
        copy.wait_send()
    for unit in range(units):
        for which in range(2):
            to_near(2, unit, which).wait_send()
    for number in range(3):
        for unit in range(units):
            to_far(number, unit).wait_send()
            if inner and unit < units - 1:
                to_depth(number, unit).wait_send()

    @pl.when(section != 0)
    def _():
        for relay in relays:
            relay.wait_send()

    @pl.when(section == 0)
    def _():
        table_x.wait_send()

    dx_done.wait()
    for copy in copies:
        copy.wait()


def backward(cotangent, saved, length_here, vectors, ids, half, inner):
    wa, wu, wd, p, lse, act, slope, n1, n2, rs1, rs2, x, y = saved
    ranks = wa.shape[0]
    length, width = x.shape
    steps = length // STEP
    depth = lax.axis_size("dp")
    units = depth if inner else 4
    hops = depth - 1 if inner else 0
    share = width // units
    anywhere = pl.BlockSpec(memory_space=pl.ANY)
    inside = pl.BlockSpec(memory_space=pltpu.VMEM)
    part = wa.shape[1] // 4
    each = width // ranks

    def like(value):
        return pltpu.VMEM(value.shape, value.dtype)

    plane = (length, width)
    turned = (width, length)
    chunk = (share, width)
    spread = (ranks, each, length)
    semaphores = pltpu.SemaphoreType.DMA
    sums = ((3,) + chunk, F32) if inner else ((3, units) + chunk, BF)
    return pl.pallas_call(
        functools.partial(backward_kernel, inner),
        name="backward_layer",
        out_shape=(
            jax.ShapeDtypeStruct(*sums),
            jax.ShapeDtypeStruct(spread, BF),
            jax.ShapeDtypeStruct(spread, BF),
            jax.ShapeDtypeStruct((16, width), F32),
            jax.ShapeDtypeStruct((half, each), F32),
        ),
        in_specs=[anywhere] * 14 + [pl.BlockSpec(memory_space=pltpu.SMEM), inside, inside],
        out_specs=(anywhere, anywhere, anywhere, inside, inside),
        scratch_shapes=[like(value) for value in saved]
        + [
            pltpu.VMEM(plane, BF),
            pltpu.VMEM(plane, F32),
            pltpu.VMEM(plane, BF),
            pltpu.VMEM(turned, BF),
            pltpu.VMEM(turned, BF),
            pltpu.VMEM(turned, BF),
            pltpu.VMEM(turned, BF),
            pltpu.VMEM((ranks, part, length), BF),
            pltpu.VMEM(plane, BF),
            pltpu.VMEM(spread, BF),
            pltpu.VMEM(spread, BF),
            pltpu.VMEM(spread, BF),
            pltpu.VMEM((units, 2) + chunk, BF),
            pltpu.VMEM((3, units, 2) + chunk, BF),
            pltpu.VMEM((3, units) + chunk, BF),
            pltpu.VMEM((3, max(hops, 1)) + (chunk if inner else (16, 128)), BF),
            pltpu.VMEM((3,) + (chunk if inner else (16, 128)), F32),
            pltpu.VMEM((3, 16, width), F32),
            pltpu.VMEM((2 + hops, 16, width), F32),
            pltpu.VMEM((half, each), BF),
            pltpu.VMEM((half, each), BF),
            pltpu.VMEM((max(hops, 1), half, each), BF),
            semaphores((14,)),
            semaphores((units, 2)),
            semaphores((3, units, 2)),
            semaphores((3, units)),
            semaphores((3, units)),
            semaphores((3, units)),
            semaphores((3, units)),
            semaphores((steps,)),
            semaphores((steps,)),
            semaphores((3,)),
            semaphores((3,)),
            semaphores((3,)),
            semaphores((3,)),
            semaphores((2 + hops,)),
            semaphores((2 + hops,)),
            semaphores((1 + hops,)),
            semaphores((1 + hops,)),
            semaphores((5,)),
        ],
        compiler_params=pltpu.CompilerParams(
            collective_id=1, has_side_effects=True, vmem_limit_bytes=VMEM_LIMIT
        ),
        cost_estimate=pl.CostEstimate(
            flops=17_000_000_000, bytes_accessed=60_000_000, transcendentals=3_000_000
        ),
    )(cotangent, *saved, length_here, vectors, ids)


def on_device(
    inputs,
    cotangent,
    segment_ids,
    column_ids,
    row_ids,
    answer_ids,
    lengths,
    type_table,
    query_weight,
    query_bias,
    key_weight,
    value_weight,
    value_bias,
    output_weight,
    output_bias,
    first_gain,
    first_shift,
    up_weight,
    up_bias,
    down_weight,
    down_bias,
    second_gain,
    second_shift,
):
    section = lax.axis_index("section")
    tensor = lax.axis_index("tensor")
    ranks = lax.axis_size("tensor")
    micro_count, sequences, length, width = inputs.shape
    items = micro_count * sequences
    type_count = 4 + COLS + ROWS
    padded_types = -(-type_count // 16) * 16
    part = query_weight.shape[2]
    hidden = up_weight.shape[2]

    ids = jnp.stack(
        [segment_ids, column_ids + 2, row_ids + 2 + COLS, answer_ids + 2 + COLS + ROWS], axis=-1
    ).reshape(items, length, 4)
    own_ids = lax.dynamic_index_in_dim(ids, tensor, 0, keepdims=False)
    length_here = lax.dynamic_slice_in_dim(lengths.reshape(items), tensor, 1, 0).reshape(1, 1)
    table = jnp.pad(type_table, ((0, padded_types - type_count), (0, 0)))
    wa = jnp.concatenate(
        [query_weight[0].T, key_weight[0].T, value_weight[0].T, output_weight[0]], axis=0
    )
    gap = jnp.zeros((part,), F32)
    bias = jnp.zeros((8, hidden), F32)
    bias = bias.at[0].set(up_bias[0].astype(F32))
    bias = bias.at[1].set(
        jnp.concatenate([query_bias[0].astype(F32), gap, value_bias[0].astype(F32), gap])
    )
    vectors = jnp.concatenate(
        [output_bias, first_gain, first_shift, down_bias, second_gain, second_shift]
    ).astype(F32)
    vectors = jnp.pad(vectors, ((0, 2), (0, 0)))

    saved = forward(
        inputs, own_ids, table, length_here, wa, up_weight[0], down_weight[0], bias, vectors, ranks
    )
    depth = lax.axis_size("dp")
    inner = depth <= 8 and width % (16 * depth) == 0
    type_half = type_count // lax.axis_size("section")
    half = -(-type_half // 16) * 16
    turned_ids = jnp.swapaxes(ids, 1, 2).reshape(items * 4, length)
    turned_ids = turned_ids + jnp.where(turned_ids >= type_half, half - type_half, 0)
    sums, dx, leaving, vecs, table_part = backward(
        cotangent, saved, length_here, vectors, turned_ids, half, inner
    )

    def in_columns(value):
        return jnp.swapaxes(value, 1, 2).reshape(
            1, micro_count, sequences, length, width // ranks
        )

    layer_outputs = in_columns(leaving)
    layer_input_grads = in_columns(dx).astype(F32)
    table_grad = table_part[:type_half]
    if inner:
        summed = sums
    else:
        summed = lax.psum_scatter(
            sums.reshape(3, width, width), "dp", scatter_dimension=1, tiled=True
        ).astype(F32)
        vecs = lax.psum(vecs, "dp")
        table_grad = lax.psum(table_grad.astype(BF), "dp").astype(F32)
    mine = lax.dynamic_slice_in_dim(
        vecs[8:14].reshape(6, ranks, width // ranks), tensor, 1, 1
    ).reshape(1, 6 * (width // ranks))
    mine = jnp.concatenate([vecs[0:1], vecs[4:5], mine], axis=1)

    def vector(start, count):
        return mine[:, start : start + count]

    share = width // ranks
    after = 2 * width
    return (
        layer_outputs,
        layer_input_grads,
        summed[2, :, 0:part][None],
        vector(width, part),
        summed[2, :, part : 2 * part][None],
        summed[2, :, 2 * part : 3 * part][None],
        vector(width + 2 * part, part),
        summed[2, :, 3 * part : 4 * part].T[None],
        vector(after, share),
        vector(after + 2 * share, share),
        vector(after + 3 * share, share),
        summed[1][None],
        vector(0, hidden),
        summed[0].T[None],
        vector(after + share, share),
        vector(after + 4 * share, share),
        vector(after + 5 * share, share),
        table_grad,
    )


def solution(mesh):
    return jax.shard_map(
        on_device,
        mesh=mesh,
        in_specs=(
            P(None, "dp", None, None),
            P(None, "dp", None, None),
            P(None, "dp", None),
            P(None, "dp", None),
            P(None, "dp", None),
            P(None, "dp", None),
            P(None, "dp"),
            P(),
            P("section", None, "tensor"),
            P("section", "tensor"),
            P("section", None, "tensor"),
            P("section", None, "tensor"),
            P("section", "tensor"),
            P("section", "tensor", None),
            P("section", None),
            P("section", None),
            P("section", None),
            P("section", None, "tensor"),
            P("section", "tensor"),
            P("section", "tensor", None),
            P("section", None),
            P("section", None),
            P("section", None),
        ),
        out_specs=(
            P("section", None, "dp", None, "tensor"),
            P("section", None, "dp", None, "tensor"),
            P("section", "dp", "tensor"),
            P("section", "tensor"),
            P("section", "dp", "tensor"),
            P("section", "dp", "tensor"),
            P("section", "tensor"),
            P("section", "tensor", "dp"),
            P("section", "tensor"),
            P("section", "tensor"),
            P("section", "tensor"),
            P("section", "dp", "tensor"),
            P("section", "tensor"),
            P("section", "tensor", "dp"),
            P("section", "tensor"),
            P("section", "tensor"),
            P("section", "tensor"),
            P("section", "tensor"),
        ),
        check_vma=False,
    )
```

```python
import functools

import jax
import jax.numpy as jnp
from jax import lax
from jax.experimental import pallas as pl
from jax.experimental.pallas import tpu as pltpu
from jax.sharding import PartitionSpec as P

HD = 64
COLS = 256
ROWS = 256
EPSILON = 1e-12
MASKED = -1e30
BF = jnp.bfloat16
F32 = jnp.float32
MESH = pl.DeviceIdType.MESH
VMEM_LIMIT = 60 * 1024 * 1024
STEP = 128


def nn(left, right):
    return lax.dot_general(left, right, (((1,), (0,)), ((), ())), preferred_element_type=F32)


def nt(left, right):
    return lax.dot_general(left, right, (((1,), (1,)), ((), ())), preferred_element_type=F32)


def tn(left, right):
    return lax.dot_general(left, right, (((0,), (0,)), ((), ())), preferred_element_type=F32)


def normalize(value):
    centered = value - jnp.mean(value, axis=-1, keepdims=True)
    variance = jnp.mean(centered * centered, axis=-1, keepdims=True)
    scale = lax.rsqrt(variance + EPSILON)
    return centered * scale, scale


def place():
    section = lax.axis_index("section")
    data = lax.axis_index("dp")
    tensor = lax.axis_index("tensor")
    beside = tensor + 1 - 2 * (tensor % 2)
    across = tensor + 2 - 4 * ((tensor // 2) % 2)
    return section, data, tensor, beside, across


def greet(partners):
    barrier = pltpu.get_barrier_semaphore()
    for partner in partners:
        pl.semaphore_signal(barrier, inc=1, device_id=partner, device_id_type=MESH)
    pl.semaphore_wait(barrier, len(partners))


def remote(src, dst, send, recv, device):
    return pltpu.make_async_remote_copy(
        src_ref=src, dst_ref=dst, send_sem=send, recv_sem=recv, device_id=device, device_id_type=MESH
    )


def forward_kernel(
    inputs_ref,
    segment_ref,
    column_ref,
    row_ref,
    answer_ref,
    table_ref,
    length_ref,
    wa_ref,
    wu_ref,
    wd_ref,
    query_bias_ref,
    value_bias_ref,
    up_bias_ref,
    output_bias_ref,
    first_gain_ref,
    first_shift_ref,
    down_bias_ref,
    second_gain_ref,
    second_shift_ref,
    wa_out,
    wu_out,
    wd_out,
    p_out,
    lse_out,
    act_out,
    slope_out,
    n1_out,
    n2_out,
    rs1_out,
    rs2_out,
    x_out,
    y_out,
    wa,
    wu,
    wd,
    bias,
    table,
    p,
    lse,
    act,
    slope,
    xf,
    xb,
    first,
    low,
    n1,
    n2,
    rs1,
    rs2,
    y,
    gather_send,
    gather_recv,
    chain_send,
    chain_recv,
    relay_send,
    relay_recv,
    local_sem,
    out_sem,
):
    section, data, tensor, beside, across = place()
    length, width = xf.shape
    ranks = wa.shape[0]
    heads = wa.shape[1] // (4 * HD)
    part = heads * HD
    steps = length // STEP
    sequences = inputs_ref.shape[1]
    near = (section, data, beside)
    far = (section, data, across)
    other = (1 - section, data, tensor)
    depth = lax.axis_size("dp")
    group = 4 if depth % 4 == 0 else 1
    spot = data % group
    before = (section, data - spot + (spot + group - 1) % group, tensor)
    after = (section, data - spot + (spot + 1) % group, tensor)
    greet([near, far, other] + ([before, after] if group > 1 else []))

    shards = ((wa_ref, wa), (wu_ref, wu), (wd_ref, wd))
    direct = wa.shape[1] // 3
    piece = 2 * direct // group

    def rows_of(number):
        return pl.ds(pl.multiple_of(direct + number * piece, piece), piece)

    to_far = []
    to_near = []
    onward = []
    own = []
    for number, (source, target) in enumerate(shards):
        to_far.append(
            [
                remote(
                    source.at[rows],
                    target.at[2, rows],
                    gather_send.at[number, which],
                    gather_recv.at[number, which],
                    far,
                )
                for which, rows in enumerate((rows_of(spot), pl.ds(0, direct)))
            ]
        )
        to_near.append(
            remote(source, target.at[1], gather_send.at[number, 2], gather_recv.at[number, 2], near)
        )
        onward.append(
            remote(
                target.at[2], target.at[3], gather_send.at[number, 3], gather_recv.at[number, 3], near
            )
        )
        own.append(pltpu.make_async_copy(source, target.at[0], local_sem.at[number]))
    to_far[0][0].start()
    for copy in to_near:
        copy.start()
    for copy in own:
        copy.start()
    bias[0] = jnp.zeros(bias.shape[1:], F32)
    bias[0, 0:1, :] = up_bias_ref[...].astype(F32)
    bias[0, 1:2, 0:part] = query_bias_ref[...].astype(F32)
    bias[0, 1:2, 2 * part : 3 * part] = value_bias_ref[...].astype(F32)
    bias_copies = [
        remote(bias.at[0], bias.at[1 + which], gather_send.at[3, which], gather_recv.at[3, which], to)
        for which, to in enumerate((near, far))
    ]
    bias_onward = remote(bias.at[2], bias.at[3], gather_send.at[3, 2], gather_recv.at[3, 2], near)
    for copy in bias_copies:
        copy.start()

    def chain(number, hop, up):
        rows = rows_of(spot - (hop - 1) if up else spot + (hop - 1))
        target = shards[number][1]
        at = 0 if up else 1
        return remote(
            target.at[2, rows],
            target.at[2, rows],
            chain_send.at[number, at, hop - 1],
            chain_recv.at[number, at, hop - 1],
            after if up else before,
        )

    def chained(number, hop, up):
        rows = rows_of(spot - hop if up else spot + hop)
        target = shards[number][1]
        at = 0 if up else 1
        return remote(
            target.at[2, rows],
            target.at[2, rows],
            chain_send.at[number, at, hop - 1],
            chain_recv.at[number, at, hop - 1],
            before if up else after,
        )

    def piece_in(number):
        to_far[number][0].wait_recv()

    def send_piece(number):
        to_far[number][0].start()

    def send_direct(number):
        to_far[number][1].start()

    def hand_on(number, hop):
        if group == 1 or hop == group:
            return
        if hop > 0:

            @pl.when(spot >= hop)
            def _():
                chained(number, hop, True).wait_recv()

            @pl.when(spot + hop < group)
            def _():
                chained(number, hop, False).wait_recv()

        if hop + 1 < group:

            @pl.when((spot >= hop) & (spot + 1 < group))
            def _():
                chain(number, hop + 1, True).start()

            @pl.when((spot + hop < group) & (spot >= 1))
            def _():
                chain(number, hop + 1, False).start()

    def pass_on(number):
        to_far[number][1].wait_recv()
        onward[number].start()

    def ready(number):
        own[number].wait()
        to_near[number].wait_recv()
        onward[number].wait_recv()

    def at_first(actions):
        @pl.when(section == 0)
        def _():
            for action, *values in actions:
                action(*values)

    out_copies = []

    def put_out(source, target):
        copy = pltpu.make_async_copy(source, target, out_sem.at[len(out_copies)])
        copy.start()
        out_copies.append(copy)

    relays = [
        remote(
            y.at[pl.ds(step * STEP, STEP)],
            xb.at[pl.ds(step * STEP, STEP)],
            relay_send.at[step],
            relay_recv.at[step],
            other,
        )
        for step in range(steps)
    ]

    @pl.when(section == 0)
    def _():
        copy = pltpu.make_async_copy(
            inputs_ref.at[tensor // sequences, tensor % sequences], xb, local_sem.at[4]
        )
        copy.start()
        copy.wait()

        types = table.shape[0]
        table[...] = jnp.zeros_like(table)
        table[0 : table_ref.shape[0], :] = table_ref[...]
        micro, item = tensor // sequences, tensor % sequences
        offset = 0
        row = lax.broadcasted_iota(jnp.int32, (types, length), 0)
        picks = jnp.zeros((types, length), F32)
        for ids_ref, count in (
            (segment_ref, 2),
            (column_ref, COLS),
            (row_ref, ROWS),
            (answer_ref, 2),
        ):
            ids = ids_ref[micro, pl.ds(item, 1), :] + offset
            picks = picks + jnp.where(ids == row, 1.0, 0.0)
            offset += count
        xf[...] = xb[...].astype(F32) + tn(picks.astype(BF), table[...])
        xb[...] = xf[...].astype(BF)

    piece_in(0)
    hand_on(0, 0)
    send_piece(1)
    bias_copies[1].wait_recv()
    bias_onward.start()
    hand_on(0, 1)
    piece_in(1)
    hand_on(1, 0)
    send_piece(2)
    hand_on(0, 2)
    piece_in(2)
    send_direct(0)
    hand_on(1, 1)
    hand_on(0, 3)
    pass_on(0)
    send_direct(1)

    @pl.when(section != 0)
    def _():
        hand_on(1, 2)
        hand_on(2, 0)
        hand_on(1, 3)
        hand_on(2, 1)
        pass_on(1)
        send_direct(2)
        hand_on(2, 2)
        hand_on(2, 3)
        pass_on(2)
        for relay in relays:
            relay.wait_recv()
        xf[...] = xb[...].astype(F32)

    ready(0)
    bias_copies[0].wait_recv()
    bias_onward.wait_recv()
    put_out(wa, wa_out)
    put_out(xb, x_out)

    def project(rank, carry):
        columns = jnp.transpose(bias[rank], (1, 0))
        p[rank, 0 : 3 * part, :] = (
            nt(wa[rank, 0 : 3 * part, :], xb[...]) + columns[0 : 3 * part, 1:2]
        ).astype(BF)
        return carry

    lax.fori_loop(0, ranks, project, 0)
    at_first([(hand_on, 1, 2), (hand_on, 2, 0)])

    here = length_ref[tensor // sequences, tensor % sequences]
    visible = lax.broadcasted_iota(jnp.int32, (length, length), 0) < here

    def attend(head, carry):
        rank = head // heads
        base = (head % heads) * HD
        query = p[rank, pl.ds(pl.multiple_of(base, HD), HD), :]
        keys = p[rank, pl.ds(pl.multiple_of(part + base, HD), HD), :]
        values = p[rank, pl.ds(pl.multiple_of(2 * part + base, HD), HD), :]
        query = (query.astype(F32) * HD ** (-0.5)).astype(BF)
        scores = jnp.where(visible, tn(keys, query), MASKED)
        maximum = jnp.max(scores, axis=0, keepdims=True)
        raised = jnp.exp(scores - maximum)
        total = jnp.sum(raised, axis=0, keepdims=True)
        context = nn(values, raised.astype(BF)) / total
        p[rank, pl.ds(pl.multiple_of(3 * part + base, HD), HD), :] = context.astype(BF)
        lse[head] = maximum + jnp.log(total)
        for at, action in (
            (2, (hand_on, 1, 3)),
            (4, (pass_on, 1)),
            (4, (send_direct, 2)),
            (5, (hand_on, 2, 1)),
            (9, (hand_on, 2, 2)),
        ):

            @pl.when((section == 0) & (head == at))
            def _():
                action[0](*action[1:])

        return carry

    lax.fori_loop(0, ranks * heads, attend, 0)
    put_out(p, p_out)
    put_out(lse, lse_out)

    def first_norm(step, carry):
        rows = pl.ds(pl.multiple_of(step * STEP, STEP), STEP)
        total = xf[rows, :] + output_bias_ref[...].astype(F32)
        for rank in range(ranks):
            total = total + tn(p[rank, 3 * part : 4 * part, rows], wa[rank, 3 * part : 4 * part, :])
        normal, scale = normalize(total)
        value = normal * first_gain_ref[...].astype(F32) + first_shift_ref[...].astype(F32)
        first[rows, :] = value
        low[rows, :] = value.astype(BF)
        n1[rows, :] = normal.astype(BF)
        rs1[rows, :] = jnp.broadcast_to(scale, (STEP, 128))
        return carry

    lax.fori_loop(0, steps, first_norm, 0)
    put_out(n1, n1_out)
    put_out(rs1, rs1_out)
    at_first([(hand_on, 2, 3)])
    ready(1)
    put_out(wu, wu_out)
    block = 256
    blocks = wu.shape[2] // block

    def widen(index, carry):
        rank = index // blocks
        columns = pl.ds(pl.multiple_of((index % blocks) * block, block), block)
        hidden = nn(low[...], wu[rank, :, columns]) + bias[rank, 0:1, columns]
        inner = 0.5 * (1.0 + lax.erf(hidden * (0.5**0.5)))
        act[rank, :, columns] = (hidden * inner).astype(BF)
        density = jnp.exp(hidden * hidden * (-0.5)) * 0.3989422804014327
        slope[rank, :, columns] = (inner + hidden * density).astype(BF)

        return carry

    lax.fori_loop(0, ranks * blocks, widen, 0)
    put_out(act, act_out)
    put_out(slope, slope_out)
    at_first([(pass_on, 2)])
    ready(2)
    put_out(wd, wd_out)

    for step in range(steps):
        rows = pl.ds(step * STEP, STEP)
        total = first[rows, :] + down_bias_ref[...].astype(F32)
        for rank in range(ranks):
            total = total + nn(act[rank, rows, :], wd[rank])
        normal, scale = normalize(total)
        y[rows, :] = (
            normal * second_gain_ref[...].astype(F32) + second_shift_ref[...].astype(F32)
        ).astype(BF)
        n2[rows, :] = normal.astype(BF)
        rs2[rows, :] = jnp.broadcast_to(scale, (STEP, 128))

        @pl.when(section == 0)
        def _():
            relays[step].start()

    put_out(n2, n2_out)
    put_out(rs2, rs2_out)
    put_out(y, y_out)
    for copy in out_copies:
        copy.wait()
    for copies in to_far + [to_near, onward, bias_copies, [bias_onward]]:
        for copy in copies:
            copy.wait_send()
    for number in range(3):
        for hop in range(group - 1):

            @pl.when((spot >= hop) & (spot + 1 < group))
            def _():
                chain(number, hop + 1, True).wait_send()

            @pl.when((spot + hop < group) & (spot >= 1))
            def _():
                chain(number, hop + 1, False).wait_send()


    @pl.when(section == 0)
    def _():
        for relay in relays:
            relay.wait_send()


def forward(inputs, ids, table, lengths, wa, wu, wd, vectors, ranks):
    length, width = inputs.shape[2], inputs.shape[3]
    rows_a = wa.shape[0]
    hidden = wu.shape[1]
    heads = ranks * (rows_a // (4 * HD))
    steps = length // STEP
    shapes = dict(
        wa=((ranks, rows_a, width), BF),
        wu=((ranks, width, hidden), BF),
        wd=((ranks, hidden, width), BF),
        p=((ranks, rows_a, length), BF),
        lse=((heads, 1, length), F32),
        act=((ranks, length, hidden), BF),
        slope=((ranks, length, hidden), BF),
        n1=((length, width), BF),
        n2=((length, width), BF),
        rs1=((length, 128), F32),
        rs2=((length, 128), F32),
        x=((length, width), BF),
        y=((length, width), BF),
    )

    def buffer(name):
        return pltpu.VMEM(*shapes[name])

    outs = ("wa", "wu", "wd", "p", "lse", "act", "slope", "n1", "n2", "rs1", "rs2", "x", "y")
    anywhere = pl.BlockSpec(memory_space=pl.ANY)
    inside = pl.BlockSpec(memory_space=pltpu.VMEM)
    return pl.pallas_call(
        forward_kernel,
        name="forward_layer",
        out_shape=tuple(jax.ShapeDtypeStruct(*shapes[name]) for name in outs),
        in_specs=[
            anywhere,
            inside,
            inside,
            inside,
            inside,
            inside,
            pl.BlockSpec(memory_space=pltpu.SMEM),
            anywhere,
            anywhere,
            anywhere,
        ]
        + [inside] * len(vectors),
        out_specs=tuple(anywhere for _ in outs),
        scratch_shapes=[
            buffer("wa"),
            buffer("wu"),
            buffer("wd"),
            pltpu.VMEM((ranks, 8, hidden), F32),
            pltpu.VMEM((-(-table.shape[0] // 16) * 16, width), BF),
            buffer("p"),
            buffer("lse"),
            buffer("act"),
            buffer("slope"),
            pltpu.VMEM((length, width), F32),
            buffer("x"),
            pltpu.VMEM((length, width), F32),
            pltpu.VMEM((length, width), BF),
            buffer("n1"),
            buffer("n2"),
            buffer("rs1"),
            buffer("rs2"),
            buffer("y"),
            pltpu.SemaphoreType.DMA((4, 4)),
            pltpu.SemaphoreType.DMA((4, 4)),
            pltpu.SemaphoreType.DMA((3, 2, 3)),
            pltpu.SemaphoreType.DMA((3, 2, 3)),
            pltpu.SemaphoreType.DMA((steps,)),
            pltpu.SemaphoreType.DMA((steps,)),
            pltpu.SemaphoreType.DMA((5,)),
            pltpu.SemaphoreType.DMA((len(outs),)),
        ],
        compiler_params=pltpu.CompilerParams(
            collective_id=0, has_side_effects=True, vmem_limit_bytes=VMEM_LIMIT
        ),
        cost_estimate=pl.CostEstimate(
            flops=8_000_000_000, bytes_accessed=60_000_000, transcendentals=6_000_000
        ),
    )(inputs, *ids, table, lengths, wa, wu, wd, *vectors)


def backward_kernel(
    inner,
    cotangent_ref,
    wa_ref,
    wu_ref,
    wd_ref,
    p_ref,
    lse_ref,
    act_ref,
    slope_ref,
    n1_ref,
    n2_ref,
    rs1_ref,
    rs2_ref,
    x_ref,
    y_ref,
    length_ref,
    first_gain_ref,
    first_shift_ref,
    second_gain_ref,
    segment_ref,
    column_ref,
    row_ref,
    answer_ref,
    sums_out,
    dx_out,
    y_out,
    vec_out,
    table_out,
    wa,
    wu,
    wd,
    p,
    lse,
    act,
    slope,
    n1,
    n2,
    rs1,
    rs2,
    xb,
    g,
    dsum,
    low,
    low_t,
    first_t,
    dcontext,
    dx,
    dx_t,
    dx_in,
    y_t,
    near_out,
    near_in,
    far_in,
    depth_in,
    final,
    vec,
    vec_in,
    table,
    table_away,
    table_in,
    table_sum,
    load_sem,
    near_send,
    near_recv,
    far_send,
    far_recv,
    depth_send,
    depth_recv,
    relay_send,
    relay_recv,
    dx_send,
    dx_recv,
    y_send,
    y_recv,
    vec_send,
    vec_recv,
    table_send,
    table_recv,
    out_sem,
):
    section, data, tensor, beside, across = place()
    diagonal = beside + 2 - 4 * ((beside // 2) % 2)
    length, width = g.shape
    ranks = wa.shape[0]
    heads = wa.shape[1] // (4 * HD)
    part = heads * HD
    steps = length // STEP
    sequences = cotangent_ref.shape[1]
    units = near_in.shape[1]
    share = near_in.shape[3]
    columns_each = width // ranks
    depth = lax.axis_size("dp")
    near = (section, data, beside)
    far = (section, data, across)
    corner = (section, data, diagonal)
    other = (1 - section, data, tensor)
    deep = []
    left = right = None
    if inner:
        deep = [(section, (data + 1 + hop) % depth, tensor) for hop in range(depth - 1)]
        left = (section, (data + depth - 1) % depth, tensor)
        right = (section, (data + 1) % depth, tensor)
    greet([near, far, corner, other] + deep)

    loads = {}
    for name, source, target in (
        ("y", y_ref, dx),
        ("n2", n2_ref, n2),
        ("rs2", rs2_ref, rs2),
        ("wd", wd_ref, wd),
        ("slope", slope_ref, slope),
        ("wu", wu_ref, wu),
        ("act", act_ref, act),
        ("n1", n1_ref, n1),
        ("rs1", rs1_ref, rs1),
        ("wa", wa_ref, wa),
        ("p", p_ref, p),
        ("lse", lse_ref, lse),
        ("xb", x_ref, xb),
    ):
        loads[name] = pltpu.make_async_copy(source, target, load_sem.at[len(loads)])
    start_g = pltpu.make_async_copy(
        cotangent_ref.at[tensor // sequences, tensor % sequences], g, load_sem.at[len(loads)]
    )

    def relay(step):
        rows = pl.ds(pl.multiple_of(step * STEP, STEP), STEP)
        return remote(dx.at[rows], g.at[rows], relay_send.at[step], relay_recv.at[step], other)

    around = ((beside, near), (across, far), (diagonal, corner))
    y_copies = [
        remote(y_t.at[rank], y_out.at[tensor], y_send.at[number], y_recv.at[number], device)
        for number, (rank, device) in enumerate(around)
    ]
    y_own = pltpu.make_async_copy(y_t.at[tensor], y_out.at[tensor], out_sem.at[0])
    dx_copies = [
        remote(dx_t.at[rank], dx_in.at[tensor], dx_send.at[number], dx_recv.at[number], device)
        for number, (rank, device) in enumerate(around)
    ]

    def turn(source, target):
        def body(step, carry):
            rows = pl.ds(pl.multiple_of(step * STEP, STEP), STEP)
            value = jnp.transpose(source[rows, :].astype(F32), (1, 0)).astype(BF)
            for rank in range(ranks):
                target[rank, :, rows] = value[rank * columns_each : (rank + 1) * columns_each]
            return carry

        lax.fori_loop(0, steps, body, 0)

    def share_outputs():
        turn(dx, y_t)
        for copy in y_copies:
            copy.start()
        y_own.start()

    @pl.when(section != 0)
    def _():
        start_g.start()

    for name in loads:
        loads[name].start()
    vec[0] = jnp.zeros(vec.shape[1:], F32)
    loads["y"].wait()
    share_outputs()
    loads["n2"].wait()
    loads["rs2"].wait()

    @pl.when(section != 0)
    def _():
        start_g.wait()

    def add_row(row, value):
        vec[0, row : row + 1, :] += jnp.sum(value, axis=0, keepdims=True)

    def norm_back(arriving, normal, scale, gain):
        scaled = arriving * gain
        return (
            scaled
            - jnp.mean(scaled, axis=-1, keepdims=True)
            - normal * jnp.mean(scaled * normal, axis=-1, keepdims=True)
        ) * scale

    def second_back(step, carry):
        rows = pl.ds(pl.multiple_of(step * STEP, STEP), STEP)

        @pl.when(section == 0)
        def _():
            relay(step).wait_recv()

        arriving = g[rows, :].astype(F32)
        normal = n2[rows, :].astype(F32)
        add_row(12, arriving * normal)
        add_row(13, arriving)
        value = norm_back(arriving, normal, rs2[rows, 0:1], second_gain_ref[...].astype(F32))
        dsum[rows, :] = value
        value = value.astype(BF)
        low[rows, :] = value
        value = value.astype(F32)
        add_row(9, value)
        low_t[:, rows] = jnp.transpose(value, (1, 0)).astype(BF)
        return carry

    lax.fori_loop(0, steps, second_back, 0)

    def to_near(number, unit, which):
        return remote(
            near_out.at[unit % 2, which],
            near_in.at[number, unit, which],
            near_send.at[unit % 2, which],
            near_recv.at[number, unit, which],
            near,
        )

    def to_far(number, unit):
        return remote(
            near_in.at[number, unit, 1],
            far_in.at[number, unit],
            far_send.at[number, unit],
            far_recv.at[number, unit],
            far,
        )

    factor = (depth - data) * (depth - data) * (depth - data) % (depth + 1)

    def owner(unit):
        return (factor * (unit + 1)) % (depth + 1) - 1

    def rightward(number, block, slot):
        return remote(
            near_in.at[number, slot, 0],
            depth_in.at[number, block],
            depth_send.at[number, slot],
            depth_recv.at[number, block],
            right,
        )

    def leftward(number, block, slot, landing):
        return remote(
            near_in.at[number, slot, 0],
            depth_in.at[number, landing],
            depth_send.at[number, slot],
            depth_recv.at[number, landing],
            left,
        )

    def gradient(number, unit, rank):
        at = owner(unit) if inner else unit
        rows = pl.ds(pl.multiple_of(at * share, share), share)
        if number == 0:
            return nn(low_t[rows, :], act[rank])
        if number == 1:
            return nn(first_t[rows, :], slope[rank])
        main = nt(first_t[rows, :], p[rank])
        edge = (3 * part // 256) * 256
        tail = nt(low_t[rows, :], p[rank, edge : 4 * part, :])
        lane = lax.broadcasted_iota(jnp.int32, tail.shape, 1)
        tail = jnp.where(lane < 3 * part - edge, main[:, edge:], tail)
        return jnp.concatenate([main[:, :edge], tail], axis=1)

    def reduce_stage(number):
        def body(index, carry):
            @pl.when(index < units)
            def _():
                for which, rank in ((1, 3), (0, 1)):

                    @pl.when((index >= 2) | (number > 0))
                    def _():
                        to_near(number, index, which).wait_send()

                    near_out[index % 2, which] = gradient(number, index, rank).astype(BF)
                    to_near(number, index, which).start()

            @pl.when(index > 0)
            def _():
                unit = index - 1
                for which, rank in ((1, 2), (0, 0)):
                    mine = gradient(number, unit, rank)
                    to_near(number, unit, which).wait_recv()
                    near_in[number, unit, which] = (
                        mine + near_in[number, unit, which].astype(F32)
                    ).astype(BF)
                    if which == 1 and number == 0:

                        @pl.when(unit < 2)
                        def _():
                            to_far(number, unit).start()

            return carry

        lax.fori_loop(0, units + 1, body, 0)

    def finish(index):
        number = index // units
        unit = index % units
        to_far(number, unit).wait_recv()
        near_in[number, unit, 0] = (
            near_in[number, unit, 0].astype(F32) + far_in[number, unit].astype(F32)
        ).astype(BF)
        if inner:
            block = owner(unit)

            @pl.when(((block > data) & (data > 0)) | ((block < data) & (data < depth - 1)))
            def _():
                rightward(number, block, unit).wait_recv()
                near_in[number, unit, 0] = (
                    near_in[number, unit, 0].astype(F32) + depth_in[number, block].astype(F32)
                ).astype(BF)

            @pl.when(block > data)
            def _():
                rightward(number, block, unit).start()

            @pl.when(block < data)
            def _():
                landing = block + (depth - block) * ((block + 1) // data)
                leftward(number, block, unit, landing).start()

        @pl.when(index + 2 < 3 * units)
        def _():
            to_far((index + 2) // units, (index + 2) % units).start()

    loads["act"].wait()

    @pl.when(section == 0)
    def _():
        reduce_stage(0)

    loads["wd"].wait()
    loads["slope"].wait()
    block = 256
    blocks = wu.shape[2] // block

    def narrow(index, carry):
        rank = index // blocks
        columns = pl.ds(pl.multiple_of((index % blocks) * block, block), block)
        value = nt(low[...], wd[rank, columns, :]) * slope[rank, :, columns].astype(F32)
        value = value.astype(BF)
        slope[rank, :, columns] = value
        vec[0, pl.ds(rank, 1), columns] = jnp.sum(value.astype(F32), axis=0, keepdims=True)
        return carry

    lax.fori_loop(0, ranks * blocks, narrow, 0)

    @pl.when(section == 0)
    def _():
        finish(0)

    loads["n1"].wait()
    loads["rs1"].wait()

    def first_transpose(step, carry):
        rows = pl.ds(pl.multiple_of(step * STEP, STEP), STEP)
        value = n1[rows, :].astype(F32) * first_gain_ref[...].astype(F32)
        value = value + first_shift_ref[...].astype(F32)
        first_t[:, rows] = jnp.transpose(value, (1, 0)).astype(BF)
        return carry

    lax.fori_loop(0, steps, first_transpose, 0)

    @pl.when(section == 0)
    def _():
        reduce_stage(1)
        finish(1)

    loads["wu"].wait()

    def first_back(step, carry):
        rows = pl.ds(pl.multiple_of(step * STEP, STEP), STEP)
        arriving = dsum[rows, :]
        for rank in range(ranks):
            arriving = arriving + nt(slope[rank, rows, :], wu[rank])
        normal = n1[rows, :].astype(F32)
        add_row(10, arriving * normal)
        add_row(11, arriving)
        value = norm_back(arriving, normal, rs1[rows, 0:1], first_gain_ref[...].astype(F32))
        dsum[rows, :] = value
        value = value.astype(BF)
        low[rows, :] = value
        add_row(8, value.astype(F32))
        return carry

    lax.fori_loop(0, steps, first_back, 0)

    @pl.when(section == 0)
    def _():
        finish(2)

    loads["wa"].wait()
    loads["p"].wait()
    loads["lse"].wait()

    def context_back(rank, carry):
        dcontext[rank] = nt(wa[rank, 3 * part : 4 * part, :], low[...]).astype(BF)
        return carry

    lax.fori_loop(0, ranks, context_back, 0)
    here = length_ref[tensor // sequences, tensor % sequences]
    visible = lax.broadcasted_iota(jnp.int32, (length, length), 0) < here

    def attend_back(head, carry):
        rank = head // heads
        base = (head % heads) * HD
        at_query = pl.ds(pl.multiple_of(base, HD), HD)
        at_keys = pl.ds(pl.multiple_of(part + base, HD), HD)
        at_values = pl.ds(pl.multiple_of(2 * part + base, HD), HD)
        query = (p[rank, at_query, :].astype(F32) * HD ** (-0.5)).astype(BF)
        keys = p[rank, at_keys, :]
        values = p[rank, at_values, :]
        dout = dcontext[rank, at_query, :]
        weights = jnp.where(visible, jnp.exp(tn(keys, query) - lse[head]), 0.0)
        dweights = tn(values, dout)
        inner_sum = jnp.sum(weights * dweights, axis=0, keepdims=True)
        dscores = (weights * (dweights - inner_sum)).astype(BF)
        p[rank, at_query, :] = (nn(keys, dscores) * HD ** (-0.5)).astype(BF)
        p[rank, at_keys, :] = nt(query, dscores).astype(BF)
        p[rank, at_values, :] = nt(dout, weights.astype(BF)).astype(BF)

        @pl.when((section == 0) & (head % 5 == 4))
        def _():
            finish(3 + head // 5)

        return carry

    lax.fori_loop(0, ranks * heads, attend_back, 0)
    early = 3 + ranks * heads // 5 + 1
    for rank in range(ranks):
        vec[0, 4 + rank : 5 + rank, :] = nt(jnp.ones((8, length), BF), p[rank])[0:1, :]
    vec_near = remote(vec.at[0], vec_in.at[0], vec_send.at[0], vec_recv.at[0], near)
    vec_near.start()
    loads["xb"].wait()

    def entering_back(step, carry):
        rows = pl.ds(pl.multiple_of(step * STEP, STEP), STEP)
        total = dsum[rows, :]
        for rank in range(ranks):
            total = total + tn(p[rank, 0 : 3 * part, rows], wa[rank, 0 : 3 * part, :])
        dx[rows, :] = total.astype(BF)

        @pl.when(section != 0)
        def _():
            relay(step).start()

        return carry

    lax.fori_loop(0, steps, entering_back, 0)
    vec_near.wait_recv()

    def join(level, swap):
        for row in range(vec.shape[1]):
            pair = row ^ swap if row < 8 else row
            vec[level + 1, row : row + 1, :] = (
                vec[level, row : row + 1, :] + vec_in[level, pair : pair + 1, :]
            )

    join(0, 1)
    vec_far = remote(vec.at[1], vec_in.at[1], vec_send.at[1], vec_recv.at[1], far)
    vec_far.start()
    turn(dx, dx_t)
    for copy in dx_copies:
        copy.start()
    dx_in[tensor] = dx_t[tensor]

    @pl.when(section == 0)
    def _():
        finish(early - 1)

    @pl.when(section != 0)
    def _():
        reduce_stage(0)
        reduce_stage(1)
        finish(0)

    def entering_transpose(step, carry):
        rows = pl.ds(pl.multiple_of(step * STEP, STEP), STEP)
        first_t[:, rows] = jnp.transpose(xb[rows, :].astype(F32), (1, 0)).astype(BF)
        low_t[:, rows] = jnp.transpose(low[rows, :].astype(F32), (1, 0)).astype(BF)
        return carry

    lax.fori_loop(0, steps, entering_transpose, 0)
    reduce_stage(2)

    vec_far.wait_recv()
    join(1, 2)
    vec_deep = [
        remote(vec.at[2], vec_in.at[2 + hop], vec_send.at[2 + hop], vec_recv.at[2 + hop], device)
        for hop, device in enumerate(deep)
    ]
    for copy in vec_deep:
        copy.start()

    @pl.when(section != 0)
    def _():
        lax.fori_loop(1, early, lambda index, carry: (finish(index), carry)[1], 0)

    lax.fori_loop(early, 2 * units, lambda index, carry: (finish(index), carry)[1], 0)
    for copy in dx_copies:
        copy.wait_recv()
    dx_done = pltpu.make_async_copy(dx_in, dx_out, out_sem.at[1])
    dx_done.start()
    half = table.shape[0]
    table_x = remote(table_away, table, table_send.at[0], table_recv.at[0], other)
    table_deep = [
        remote(table, table_in.at[hop], table_send.at[1 + hop], table_recv.at[1 + hop], device)
        for hop, device in enumerate(deep)
    ]

    @pl.when(section == 0)
    def _():
        types_each = table_out.shape[0]
        table_sum[...] = jnp.zeros_like(table_sum)

        def count(number, carry):
            row = lax.broadcasted_iota(jnp.int32, (2 * half, length), 0)
            picks = jnp.zeros((2 * half, length), F32)
            micro, item = number // sequences, number % sequences
            offset = 0
            for ids_ref, number_of in (
                (segment_ref, 2),
                (column_ref, COLS),
                (row_ref, ROWS),
                (answer_ref, 2),
            ):
                ids = ids_ref[micro, pl.ds(item, 1), :] + offset
                ids = ids + jnp.where(ids >= types_each, half - types_each, 0)
                picks = picks + jnp.where(ids == row, 1.0, 0.0)
                offset += number_of
            table_sum[...] += nt(picks.astype(BF), dx_in[number])
            return carry

        lax.fori_loop(0, ranks, count, 0)
        table[...] = table_sum[:half].astype(BF)
        table_away[...] = table_sum[half:].astype(BF)
        table_x.start()
        for copy in table_deep:
            copy.start()

    lax.fori_loop(2 * units, 3 * units - 1, lambda index, carry: (finish(index), carry)[1], 0)

    @pl.when(section != 0)
    def _():
        table_x.wait_recv()
        for copy in table_deep:
            copy.start()

    finish(3 * units - 1)
    copies = []
    if inner:
        for number in range(3):
            total = jnp.zeros(final.shape[1:], F32)
            for unit in range(units):
                keep = jnp.where(owner(unit) == data, 1.0, 0.0)
                total = total + near_in[number, unit, 0].astype(F32) * keep
            final[number] = total

            @pl.when(data > 0)
            def _():
                rightward(number, data, 0).wait_recv()
                final[number] = final[number] + depth_in[number, data].astype(F32)

            @pl.when(data < depth - 1)
            def _():
                leftward(number, data, 0, depth).wait_recv()
                final[number] = final[number] + depth_in[number, depth].astype(F32)

            copy = pltpu.make_async_copy(
                final.at[number], sums_out.at[number], out_sem.at[2 + number]
            )
            copy.start()
            copies.append(copy)
    else:
        copy = pltpu.make_async_copy(
            near_in.at[:, :, 0], sums_out, out_sem.at[2]
        )
        copy.start()
        copies.append(copy)
    total = vec[2]
    for hop, copy in enumerate(vec_deep):
        copy.wait_recv()
        total = total + vec_in[2 + hop]
    vec_out[...] = total
    total = table[...].astype(F32)
    for hop, copy in enumerate(table_deep):
        copy.wait_recv()
        total = total + table_in[hop].astype(F32)
    table_out[...] = total[: table_out.shape[0]]

    for copy in y_copies:
        copy.wait()
    y_own.wait()
    for copy in dx_copies:
        copy.wait_send()
    vec_near.wait_send()
    vec_far.wait_send()
    for copy in vec_deep + table_deep:
        copy.wait_send()
    for unit in range(2):
        for which in range(2):
            to_near(2, unit, which).wait_send()
    for number in range(3):
        for unit in range(units):
            to_far(number, unit).wait_send()
            if inner:

                @pl.when(owner(unit) != data)
                def _():
                    rightward(number, 0, unit).wait_send()

    @pl.when(section != 0)
    def _():
        for step in range(steps):
            relay(step).wait_send()

    @pl.when(section == 0)
    def _():
        table_x.wait_send()

    dx_done.wait()
    for copy in copies:
        copy.wait()


def backward(cotangent, saved, lengths, vectors, ids, type_half, inner):
    wa, wu, wd, p, lse, act, slope, n1, n2, rs1, rs2, x, y = saved
    ranks = wa.shape[0]
    length, width = x.shape
    steps = length // STEP
    depth = lax.axis_size("dp")
    units = depth if inner else 4
    hops = depth - 1 if inner else 0
    share = width // units
    anywhere = pl.BlockSpec(memory_space=pl.ANY)
    inside = pl.BlockSpec(memory_space=pltpu.VMEM)
    part = wa.shape[1] // 4
    each = width // ranks
    half = -(-type_half // 16) * 16

    def like(value):
        return pltpu.VMEM(value.shape, value.dtype)

    plane = (length, width)
    turned = (width, length)
    chunk = (share, width)
    spread = (ranks, each, length)
    semaphores = pltpu.SemaphoreType.DMA
    sums = ((3,) + chunk, F32) if inner else ((3, units) + chunk, BF)
    return pl.pallas_call(
        functools.partial(backward_kernel, inner),
        name="backward_layer",
        out_shape=(
            jax.ShapeDtypeStruct(*sums),
            jax.ShapeDtypeStruct(spread, BF),
            jax.ShapeDtypeStruct(spread, BF),
            jax.ShapeDtypeStruct((16, width), F32),
            jax.ShapeDtypeStruct((type_half, each), F32),
        ),
        in_specs=[anywhere] * 14
        + [pl.BlockSpec(memory_space=pltpu.SMEM)]
        + [inside] * (len(vectors) + len(ids)),
        out_specs=(anywhere, anywhere, anywhere, inside, inside),
        scratch_shapes=[like(value) for value in saved[:-1]]
        + [
            pltpu.VMEM(plane, BF),
            pltpu.VMEM(plane, F32),
            pltpu.VMEM(plane, BF),
            pltpu.VMEM(turned, BF),
            pltpu.VMEM(turned, BF),
            pltpu.VMEM((ranks, part, length), BF),
            pltpu.VMEM(plane, BF),
            pltpu.VMEM(spread, BF),
            pltpu.VMEM(spread, BF),
            pltpu.VMEM(spread, BF),
            pltpu.VMEM((2, 2) + chunk, BF),
            pltpu.VMEM((3, units, 2) + chunk, BF),
            pltpu.VMEM((3, units) + chunk, BF),
            pltpu.VMEM((3, units + 1) + (chunk if inner else (16, 128)), BF),
            pltpu.VMEM((3,) + (chunk if inner else (16, 128)), F32),
            pltpu.VMEM((3, 16, width), F32),
            pltpu.VMEM((2 + hops, 16, width), F32),
            pltpu.VMEM((half, each), BF),
            pltpu.VMEM((half, each), BF),
            pltpu.VMEM((max(hops, 1), half, each), BF),
            pltpu.VMEM((2 * half, each), F32),
            semaphores((14,)),
            semaphores((2, 2)),
            semaphores((3, units, 2)),
            semaphores((3, units)),
            semaphores((3, units)),
            semaphores((3, units)),
            semaphores((3, units + 1)),
            semaphores((steps,)),
            semaphores((steps,)),
            semaphores((3,)),
            semaphores((3,)),
            semaphores((3,)),
            semaphores((3,)),
            semaphores((2 + hops,)),
            semaphores((2 + hops,)),
            semaphores((1 + hops,)),
            semaphores((1 + hops,)),
            semaphores((5,)),
        ],
        compiler_params=pltpu.CompilerParams(
            collective_id=1, has_side_effects=True, vmem_limit_bytes=VMEM_LIMIT
        ),
        cost_estimate=pl.CostEstimate(
            flops=17_000_000_000, bytes_accessed=60_000_000, transcendentals=3_000_000
        ),
    )(cotangent, *saved, lengths, *vectors, *ids)


def on_device(
    inputs,
    cotangent,
    segment_ids,
    column_ids,
    row_ids,
    answer_ids,
    lengths,
    type_table,
    query_weight,
    query_bias,
    key_weight,
    value_weight,
    value_bias,
    output_weight,
    output_bias,
    first_gain,
    first_shift,
    up_weight,
    up_bias,
    down_weight,
    down_bias,
    second_gain,
    second_shift,
):
    tensor = lax.axis_index("tensor")
    ranks = lax.axis_size("tensor")
    micro_count, sequences, length, width = inputs.shape
    type_count = 4 + COLS + ROWS
    part = query_weight.shape[2]
    hidden = up_weight.shape[2]

    ids = (segment_ids, column_ids, row_ids, answer_ids)
    wa = jnp.concatenate(
        [query_weight[0].T, key_weight[0].T, value_weight[0].T, output_weight[0]], axis=0
    )
    vectors = (
        query_bias,
        value_bias,
        up_bias,
        output_bias,
        first_gain,
        first_shift,
        down_bias,
        second_gain,
        second_shift,
    )
    saved = forward(
        inputs, ids, type_table, lengths, wa, up_weight[0], down_weight[0], vectors, ranks
    )
    depth = lax.axis_size("dp")
    inner = depth == 4 and width % (16 * depth) == 0
    type_half = type_count // lax.axis_size("section")
    sums, dx, leaving, vecs, table_grad = backward(
        cotangent, saved, lengths, (first_gain, first_shift, second_gain), ids, type_half, inner
    )

    def in_columns(value):
        return jnp.swapaxes(value, 1, 2).reshape(
            1, micro_count, sequences, length, width // ranks
        )

    layer_outputs = in_columns(leaving)
    layer_input_grads = in_columns(dx).astype(F32)
    if inner:
        summed = sums
    else:
        summed = lax.psum_scatter(
            sums.reshape(3, width, width), "dp", scatter_dimension=1, tiled=True
        ).astype(F32)
        vecs = lax.psum(vecs, "dp")
        table_grad = lax.psum(table_grad.astype(BF), "dp").astype(F32)
    mine = lax.dynamic_slice_in_dim(
        vecs[8:14].reshape(6, ranks, width // ranks), tensor, 1, 1
    ).reshape(1, 6 * (width // ranks))
    mine = jnp.concatenate([vecs[0:1], vecs[4:5], mine], axis=1)

    def vector(start, count):
        return mine[:, start : start + count]

    share = width // ranks
    after = 2 * width
    return (
        layer_outputs,
        layer_input_grads,
        summed[2, :, 0:part][None],
        vector(width, part),
        summed[2, :, part : 2 * part][None],
        summed[2, :, 2 * part : 3 * part][None],
        vector(width + 2 * part, part),
        summed[2, :, 3 * part : 4 * part].T[None],
        vector(after, share),
        vector(after + 2 * share, share),
        vector(after + 3 * share, share),
        summed[1][None],
        vector(0, hidden),
        summed[0].T[None],
        vector(after + share, share),
        vector(after + 4 * share, share),
        vector(after + 5 * share, share),
        table_grad,
    )


def solution(mesh):
    return jax.shard_map(
        on_device,
        mesh=mesh,
        in_specs=(
            P(None, "dp", None, None),
            P(None, "dp", None, None),
            P(None, "dp", None),
            P(None, "dp", None),
            P(None, "dp", None),
            P(None, "dp", None),
            P(None, "dp"),
            P(),
            P("section", None, "tensor"),
            P("section", "tensor"),
            P("section", None, "tensor"),
            P("section", None, "tensor"),
            P("section", "tensor"),
            P("section", "tensor", None),
            P("section", None),
            P("section", None),
            P("section", None),
            P("section", None, "tensor"),
            P("section", "tensor"),
            P("section", "tensor", None),
            P("section", None),
            P("section", None),
            P("section", None),
        ),
        out_specs=(
            P("section", None, "dp", None, "tensor"),
            P("section", None, "dp", None, "tensor"),
            P("section", "dp", "tensor"),
            P("section", "tensor"),
            P("section", "dp", "tensor"),
            P("section", "dp", "tensor"),
            P("section", "tensor"),
            P("section", "tensor", "dp"),
            P("section", "tensor"),
            P("section", "tensor"),
            P("section", "tensor"),
            P("section", "dp", "tensor"),
            P("section", "tensor"),
            P("section", "tensor", "dp"),
            P("section", "tensor"),
            P("section", "tensor"),
            P("section", "tensor"),
            P("section", "tensor"),
        ),
        check_vma=False,
    )
```

```python
import functools

import jax
import jax.numpy as jnp
from jax import lax
from jax.experimental import pallas as pl
from jax.experimental.pallas import tpu as pltpu
from jax.sharding import PartitionSpec as P

HD = 64
COLS = 256
ROWS = 256
EPSILON = 1e-12
MASKED = -1e30
BF = jnp.bfloat16
F32 = jnp.float32
MESH = pl.DeviceIdType.MESH
VMEM_LIMIT = 60 * 1024 * 1024
STEP = 256
OUTS = ("wa", "wu", "wd", "p", "lse", "act", "slope", "n1", "n2", "rs1", "rs2", "x", "y")


def nn(left, right):
    return lax.dot_general(left, right, (((1,), (0,)), ((), ())), preferred_element_type=F32)


def nt(left, right):
    return lax.dot_general(left, right, (((1,), (1,)), ((), ())), preferred_element_type=F32)


def tn(left, right):
    return lax.dot_general(left, right, (((0,), (0,)), ((), ())), preferred_element_type=F32)


def normalize(value):
    centered = value - jnp.mean(value, axis=-1, keepdims=True)
    variance = jnp.mean(centered * centered, axis=-1, keepdims=True)
    scale = lax.rsqrt(variance + EPSILON)
    return centered * scale, scale


def place():
    section = lax.axis_index("section")
    data = lax.axis_index("dp")
    tensor = lax.axis_index("tensor")
    beside = tensor + 1 - 2 * (tensor % 2)
    across = tensor + 2 - 4 * ((tensor // 2) % 2)
    return section, data, tensor, beside, across


def greet(partners):
    barrier = pltpu.get_barrier_semaphore()
    for partner in partners:
        pl.semaphore_signal(barrier, inc=1, device_id=partner, device_id_type=MESH)
    pl.semaphore_wait(barrier, len(partners))


def remote(src, dst, send, recv, device):
    return pltpu.make_async_remote_copy(
        src_ref=src, dst_ref=dst, send_sem=send, recv_sem=recv, device_id=device, device_id_type=MESH
    )


def forward_kernel(
    inputs_ref,
    segment_ref,
    column_ref,
    row_ref,
    answer_ref,
    table_ref,
    length_ref,
    wa_ref,
    wu_ref,
    wd_ref,
    query_bias_ref,
    value_bias_ref,
    up_bias_ref,
    output_bias_ref,
    first_gain_ref,
    first_shift_ref,
    down_bias_ref,
    second_gain_ref,
    second_shift_ref,
    wa_out,
    wu_out,
    wd_out,
    p_out,
    lse_out,
    act_out,
    slope_out,
    n1_out,
    n2_out,
    rs1_out,
    rs2_out,
    x_out,
    y_out,
    wa,
    wu,
    wd,
    bias,
    table,
    p,
    lse,
    act,
    slope,
    xf,
    xb,
    first,
    low,
    n1,
    n2,
    rs1,
    rs2,
    y,
    gather_send,
    gather_recv,
    chain_send,
    chain_recv,
    relay_send,
    relay_recv,
    local_sem,
    out_sem,
    turn_sem,
):
    section, data, tensor, beside, across = place()
    length, width = xf.shape
    ranks = wa.shape[0]
    heads = wa.shape[1] // (4 * HD)
    part = heads * HD
    steps = length // STEP
    sequences = inputs_ref.shape[1]
    near = (section, data, beside)
    far = (section, data, across)
    other = (1 - section, data, tensor)
    depth = lax.axis_size("dp")
    group = 4 if depth % 4 == 0 else 1
    spot = data % group
    before = (section, data - spot + (spot + group - 1) % group, tensor)
    after = (section, data - spot + (spot + 1) % group, tensor)
    greet([near, far, other] + ([before, after] if group > 1 else []))

    shards = ((wa_ref, wa), (wu_ref, wu), (wd_ref, wd))
    direct = wa.shape[1] * 5 // 12
    piece = (wa.shape[1] - direct) // group

    def rows_of(number):
        return pl.ds(pl.multiple_of(direct + number * piece, 16), piece)

    to_far = []
    to_near = []
    onward = []
    own = []
    for number, (source, target) in enumerate(shards):
        to_far.append(
            [
                remote(
                    source.at[rows],
                    target.at[2, rows],
                    gather_send.at[number, which],
                    gather_recv.at[number, which],
                    far,
                )
                for which, rows in enumerate((rows_of(spot), pl.ds(0, direct)))
            ]
        )
        to_near.append(
            remote(source, target.at[1], gather_send.at[number, 2], gather_recv.at[number, 2], near)
        )
        onward.append(
            remote(
                target.at[2], target.at[3], gather_send.at[number, 3], gather_recv.at[number, 3], near
            )
        )
        own.append(pltpu.make_async_copy(source, target.at[0], local_sem.at[number]))
    to_far[0][0].start()
    for copy in to_near:
        copy.start()
    for copy in own:
        copy.start()
    bias[0] = jnp.zeros(bias.shape[1:], F32)
    bias[0, 0:1, :] = up_bias_ref[...].astype(F32)
    bias[0, 1:2, 0:part] = query_bias_ref[...].astype(F32)
    bias[0, 1:2, 2 * part : 3 * part] = value_bias_ref[...].astype(F32)
    bias_copies = [
        remote(bias.at[0], bias.at[1 + which], gather_send.at[3, which], gather_recv.at[3, which], to)
        for which, to in enumerate((near, far))
    ]
    bias_onward = remote(bias.at[2], bias.at[3], gather_send.at[3, 2], gather_recv.at[3, 2], near)
    for copy in bias_copies:
        copy.start()

    def chain(number, hop, up):
        rows = rows_of(spot - (hop - 1) if up else spot + (hop - 1))
        target = shards[number][1]
        at = 0 if up else 1
        return remote(
            target.at[2, rows],
            target.at[2, rows],
            chain_send.at[number, at, hop - 1],
            chain_recv.at[number, at, hop - 1],
            after if up else before,
        )

    def chained(number, hop, up):
        rows = rows_of(spot - hop if up else spot + hop)
        target = shards[number][1]
        at = 0 if up else 1
        return remote(
            target.at[2, rows],
            target.at[2, rows],
            chain_send.at[number, at, hop - 1],
            chain_recv.at[number, at, hop - 1],
            before if up else after,
        )

    def piece_in(number):
        to_far[number][0].wait_recv()

    def send_piece(number):
        to_far[number][0].start()

    def send_direct(number):
        to_far[number][1].start()

    def hand_on(number, hop):
        if group == 1 or hop == group:
            return
        if hop > 0:

            @pl.when(spot >= hop)
            def _():
                chained(number, hop, True).wait_recv()

            @pl.when(spot + hop < group)
            def _():
                chained(number, hop, False).wait_recv()

        if hop + 1 < group:

            @pl.when((spot >= hop) & (spot + 1 < group))
            def _():
                chain(number, hop + 1, True).start()

            @pl.when((spot + hop < group) & (spot >= 1))
            def _():
                chain(number, hop + 1, False).start()

    def pass_on(number):
        to_far[number][1].wait_recv()
        onward[number].start()

    def ready(number):
        own[number].wait()
        to_near[number].wait_recv()
        onward[number].wait_recv()

    def at_first(actions):
        @pl.when(section == 0)
        def _():
            for action, *values in actions:
                action(*values)

    out_copies = []

    wu_copy = pltpu.make_async_copy(wu, wu_out, out_sem.at[len(OUTS)])
    wd_copy = pltpu.make_async_copy(wd, wd_out, out_sem.at[len(OUTS) + 1])

    def put_out(source, target):
        copy = pltpu.make_async_copy(source, target, out_sem.at[len(out_copies)])
        copy.start()
        out_copies.append(copy)

    relays = [
        remote(
            y.at[pl.ds(step * STEP, STEP)],
            xb.at[pl.ds(step * STEP, STEP)],
            relay_send.at[step],
            relay_recv.at[step],
            other,
        )
        for step in range(steps)
    ]

    load_input = pltpu.make_async_copy(
        inputs_ref.at[tensor // sequences, tensor % sequences], xb, local_sem.at[3]
    )

    @pl.when(section == 0)
    def _():
        load_input.start()

    piece_in(0)
    hand_on(0, 0)
    send_piece(1)
    send_direct(0)
    bias_copies[1].wait_recv()
    bias_onward.start()

    @pl.when(section == 0)
    def _():
        load_input.wait()
        types = table.shape[0]
        table[...] = jnp.zeros_like(table)
        table[0 : table_ref.shape[0], :] = table_ref[...]
        micro, item = tensor // sequences, tensor % sequences
        offset = 0
        row = lax.broadcasted_iota(jnp.int32, (types, length), 0)
        picks = jnp.zeros((types, length), F32)
        for ids_ref, count in (
            (segment_ref, 2),
            (column_ref, COLS),
            (row_ref, ROWS),
            (answer_ref, 2),
        ):
            ids = ids_ref[micro, pl.ds(item, 1), :] + offset
            picks = picks + jnp.where(ids == row, 1.0, 0.0)
            offset += count
        xf[...] = xb[...].astype(F32) + tn(picks.astype(BF), table[...])
        xb[...] = xf[...].astype(BF)

    hand_on(0, 1)
    piece_in(1)
    hand_on(1, 0)
    send_piece(2)
    hand_on(0, 2)
    piece_in(2)
    hand_on(2, 0)
    send_direct(1)
    hand_on(1, 1)
    hand_on(0, 3)
    pass_on(0)
    ready(0)
    put_out(wa, wa_out)

    @pl.when(section != 0)
    def _():
        hand_on(1, 2)
        hand_on(2, 1)
        hand_on(1, 3)
        pass_on(1)
        send_direct(2)
        hand_on(2, 2)
        hand_on(2, 3)
        pass_on(2)
        ready(1)
        wu_copy.start()
        ready(2)
        wd_copy.start()
        for relay in relays:
            relay.wait_recv()
        xf[...] = xb[...].astype(F32)

    bias_copies[0].wait_recv()
    bias_onward.wait_recv()
    put_out(xb, x_out)

    def project(rank, carry):
        columns = jnp.transpose(bias[rank], (1, 0))
        p[rank, 0 : 3 * part, :] = (
            nt(wa[rank, 0 : 3 * part, :], xb[...]) + columns[0 : 3 * part, 1:2]
        ).astype(BF)
        return carry

    lax.fori_loop(0, ranks, project, 0)
    at_first([(hand_on, 1, 2), (hand_on, 2, 1)])

    here = length_ref[tensor // sequences, tensor % sequences]
    visible = lax.broadcasted_iota(jnp.int32, (length, length), 0) < here

    def attend(head, carry):
        rank = head // heads
        base = (head % heads) * HD
        query = p[rank, pl.ds(pl.multiple_of(base, HD), HD), :]
        keys = p[rank, pl.ds(pl.multiple_of(part + base, HD), HD), :]
        values = p[rank, pl.ds(pl.multiple_of(2 * part + base, HD), HD), :]
        query = (query.astype(F32) * HD ** (-0.5)).astype(BF)
        scores = jnp.where(visible, tn(keys, query), MASKED)
        maximum = jnp.max(scores, axis=0, keepdims=True)
        raised = jnp.exp(scores - maximum)
        total = jnp.sum(raised, axis=0, keepdims=True)
        context = nn(values, raised.astype(BF)) / total
        p[rank, pl.ds(pl.multiple_of(3 * part + base, HD), HD), :] = context.astype(BF)
        lse[head] = maximum + jnp.log(total)
        for at, action in (
            (2, (hand_on, 1, 3)),
            (2, (pass_on, 1)),
            (2, (send_direct, 2)),
            (4, (hand_on, 2, 2)),
            (8, (hand_on, 2, 3)),
        ):

            @pl.when((section == 0) & (head == at))
            def _():
                action[0](*action[1:])

        return carry

    lax.fori_loop(0, ranks * heads, attend, 0)
    put_out(p, p_out)
    put_out(lse, lse_out)

    def first_norm(step, carry):
        rows = pl.ds(pl.multiple_of(step * STEP, STEP), STEP)
        total = xf[rows, :] + output_bias_ref[...].astype(F32)
        for rank in range(ranks):
            total = total + tn(p[rank, 3 * part : 4 * part, rows], wa[rank, 3 * part : 4 * part, :])
        normal, scale = normalize(total)
        value = normal * first_gain_ref[...].astype(F32) + first_shift_ref[...].astype(F32)
        first[rows, :] = value
        low[rows, :] = value.astype(BF)
        n1[rows, :] = normal.astype(BF)
        rs1[rows, :] = jnp.broadcast_to(scale, (STEP, 128))
        return carry

    lax.fori_loop(0, steps, first_norm, 0)
    put_out(n1, n1_out)
    put_out(rs1, rs1_out)
    at_first([(pass_on, 2), (ready, 1), (wu_copy.start,)])
    block = 256
    blocks = wu.shape[2] // block

    def widen(index, carry):
        rank = index // blocks
        columns = pl.ds(pl.multiple_of((index % blocks) * block, block), block)
        hidden = nn(low[...], wu[rank, :, columns]) + bias[rank, 0:1, columns]
        inner = 0.5 * (1.0 + lax.erf(hidden * (0.5**0.5)))
        act[rank, :, columns] = (hidden * inner).astype(BF)
        density = jnp.exp(hidden * hidden * (-0.5)) * 0.3989422804014327
        slope[rank, :, columns] = (inner + hidden * density).astype(BF)

        return carry

    lax.fori_loop(0, ranks * blocks, widen, 0)
    put_out(act, act_out)
    put_out(slope, slope_out)
    at_first([(ready, 2), (wd_copy.start,)])

    for step in range(steps):
        rows = pl.ds(step * STEP, STEP)
        total = first[rows, :] + down_bias_ref[...].astype(F32)
        for rank in range(ranks):
            total = total + nn(act[rank, rows, :], wd[rank])
        normal, scale = normalize(total)
        y[rows, :] = (
            normal * second_gain_ref[...].astype(F32) + second_shift_ref[...].astype(F32)
        ).astype(BF)
        n2[rows, :] = normal.astype(BF)
        rs2[rows, :] = jnp.broadcast_to(scale, (STEP, 128))

        @pl.when((section == 0) & (tensor % 2 == 0))
        def _():
            relays[step].start()

    put_out(n2, n2_out)
    put_out(rs2, rs2_out)
    put_out(y, y_out)

    @pl.when((section == 0) & (tensor % 2 == 0))
    def _():
        for relay in relays:
            relay.wait_send()
        pl.semaphore_signal(turn_sem, inc=1, device_id=near, device_id_type=MESH)

    @pl.when((section == 0) & (tensor % 2 == 1))
    def _():
        pl.semaphore_wait(turn_sem, 1)
        for relay in relays:
            relay.start()
        for relay in relays:
            relay.wait_send()

    for copy in out_copies + [wu_copy, wd_copy]:
        copy.wait()
    for copies in to_far + [to_near, onward, bias_copies, [bias_onward]]:
        for copy in copies:
            copy.wait_send()
    for number in range(3):
        for hop in range(group - 1):

            @pl.when((spot >= hop) & (spot + 1 < group))
            def _():
                chain(number, hop + 1, True).wait_send()

            @pl.when((spot + hop < group) & (spot >= 1))
            def _():
                chain(number, hop + 1, False).wait_send()


def forward(inputs, ids, table, lengths, wa, wu, wd, vectors, ranks):
    length, width = inputs.shape[2], inputs.shape[3]
    rows_a = wa.shape[0]
    hidden = wu.shape[1]
    heads = ranks * (rows_a // (4 * HD))
    steps = length // STEP
    shapes = dict(
        wa=((ranks, rows_a, width), BF),
        wu=((ranks, width, hidden), BF),
        wd=((ranks, hidden, width), BF),
        p=((ranks, rows_a, length), BF),
        lse=((heads, 1, length), F32),
        act=((ranks, length, hidden), BF),
        slope=((ranks, length, hidden), BF),
        n1=((length, width), BF),
        n2=((length, width), BF),
        rs1=((length, 128), F32),
        rs2=((length, 128), F32),
        x=((length, width), BF),
        y=((length, width), BF),
    )

    def buffer(name):
        return pltpu.VMEM(*shapes[name])

    anywhere = pl.BlockSpec(memory_space=pl.ANY)
    inside = pl.BlockSpec(memory_space=pltpu.VMEM)
    return pl.pallas_call(
        forward_kernel,
        name="forward_layer",
        out_shape=tuple(jax.ShapeDtypeStruct(*shapes[name]) for name in OUTS),
        in_specs=[
            anywhere,
            inside,
            inside,
            inside,
            inside,
            inside,
            pl.BlockSpec(memory_space=pltpu.SMEM),
            anywhere,
            anywhere,
            anywhere,
        ]
        + [inside] * len(vectors),
        out_specs=tuple(anywhere for _ in OUTS),
        scratch_shapes=[
            buffer("wa"),
            buffer("wu"),
            buffer("wd"),
            pltpu.VMEM((ranks, 8, hidden), F32),
            pltpu.VMEM((-(-table.shape[0] // 16) * 16, width), BF),
            buffer("p"),
            buffer("lse"),
            buffer("act"),
            buffer("slope"),
            pltpu.VMEM((length, width), F32),
            buffer("x"),
            pltpu.VMEM((length, width), F32),
            pltpu.VMEM((length, width), BF),
            buffer("n1"),
            buffer("n2"),
            buffer("rs1"),
            buffer("rs2"),
            buffer("y"),
            pltpu.SemaphoreType.DMA((4, 4)),
            pltpu.SemaphoreType.DMA((4, 4)),
            pltpu.SemaphoreType.DMA((3, 2, 3)),
            pltpu.SemaphoreType.DMA((3, 2, 3)),
            pltpu.SemaphoreType.DMA((steps,)),
            pltpu.SemaphoreType.DMA((steps,)),
            pltpu.SemaphoreType.DMA((5,)),
            pltpu.SemaphoreType.DMA((len(OUTS) + 2,)),
            pltpu.SemaphoreType.REGULAR,
        ],
        compiler_params=pltpu.CompilerParams(
            collective_id=0, has_side_effects=True, vmem_limit_bytes=VMEM_LIMIT
        ),
        cost_estimate=pl.CostEstimate(
            flops=8_000_000_000, bytes_accessed=60_000_000, transcendentals=6_000_000
        ),
    )(inputs, *ids, table, lengths, wa, wu, wd, *vectors)


def backward_kernel(
    inner,
    cotangent_ref,
    wa_ref,
    wu_ref,
    wd_ref,
    p_ref,
    lse_ref,
    act_ref,
    slope_ref,
    n1_ref,
    n2_ref,
    rs1_ref,
    rs2_ref,
    x_ref,
    y_ref,
    length_ref,
    first_gain_ref,
    first_shift_ref,
    second_gain_ref,
    segment_ref,
    column_ref,
    row_ref,
    answer_ref,
    sums_out,
    dx_out,
    y_out,
    vec_out,
    table_out,
    wa,
    wu,
    wd,
    p,
    lse,
    act,
    slope,
    n1,
    n2,
    rs1,
    rs2,
    xb,
    g,
    dsum,
    low,
    low_t,
    first_t,
    dcontext,
    dx,
    dx_t,
    dx_in,
    y_t,
    near_out,
    near_in,
    far_in,
    depth_in,
    final,
    vec,
    vec_in,
    table,
    table_away,
    table_in,
    table_sum,
    load_sem,
    near_send,
    near_recv,
    far_send,
    far_recv,
    depth_send,
    depth_recv,
    relay_send,
    relay_recv,
    dx_send,
    dx_recv,
    y_send,
    y_recv,
    vec_send,
    vec_recv,
    table_send,
    table_recv,
    out_sem,
):
    section, data, tensor, beside, across = place()
    diagonal = beside + 2 - 4 * ((beside // 2) % 2)
    length, width = g.shape
    ranks = wa.shape[0]
    heads = wa.shape[1] // (4 * HD)
    part = heads * HD
    steps = length // STEP
    sequences = cotangent_ref.shape[1]
    units = near_in.shape[1]
    share = near_in.shape[3]
    columns_each = width // ranks
    depth = lax.axis_size("dp")
    near = (section, data, beside)
    far = (section, data, across)
    corner = (section, data, diagonal)
    other = (1 - section, data, tensor)
    deep = []
    left = right = None
    if inner:
        deep = [(section, (data + 1 + hop) % depth, tensor) for hop in range(depth - 1)]
        left = (section, (data + depth - 1) % depth, tensor)
        right = (section, (data + 1) % depth, tensor)
    partners = [near, far, corner, other] + deep
    barrier = pltpu.get_barrier_semaphore()
    for partner in partners:
        pl.semaphore_signal(barrier, inc=1, device_id=partner, device_id_type=MESH)

    @pl.when(section == 0)
    def _():
        pl.semaphore_wait(barrier, len(partners))

    loads = {}
    for name, source, target in (
        ("n2", n2_ref, n2),
        ("rs2", rs2_ref, rs2),
        ("wd", wd_ref, wd),
        ("slope", slope_ref, slope),
        ("wu", wu_ref, wu),
        ("act", act_ref, act),
        ("n1", n1_ref, n1),
        ("rs1", rs1_ref, rs1),
        ("wa", wa_ref, wa),
        ("p", p_ref, p),
        ("lse", lse_ref, lse),
        ("xb", x_ref, xb),
    ):
        loads[name] = pltpu.make_async_copy(source, target, load_sem.at[len(loads)])
    start_g = pltpu.make_async_copy(
        cotangent_ref.at[tensor // sequences, tensor % sequences], g, load_sem.at[len(loads)]
    )
    first_y = pltpu.make_async_copy(y_ref, dx, load_sem.at[len(loads) + 1])
    later_y = pltpu.make_async_copy(y_ref, g, load_sem.at[len(loads) + 1])
    waves = (("n2", "rs2"), ("wd", "slope"), ("wu", "n1", "rs1"), ("wa", "p", "lse"), ("act", "xb"))

    def begin(wave):
        for name in waves[wave]:
            loads[name].start()

    def arrived(wave):
        for name in waves[wave]:
            loads[name].wait()
        if wave + 1 < len(waves):

            @pl.when(section != 0)
            def _():
                begin(wave + 1)


    def relay(step):
        rows = pl.ds(pl.multiple_of(step * STEP, STEP), STEP)
        return remote(dx.at[rows], g.at[rows], relay_send.at[step], relay_recv.at[step], other)

    around = ((beside, near), (across, far), (diagonal, corner))
    y_copies = [
        remote(y_t.at[rank], y_out.at[tensor], y_send.at[number], y_recv.at[number], device)
        for number, (rank, device) in enumerate(around)
    ]
    y_own = pltpu.make_async_copy(y_t.at[tensor], y_out.at[tensor], out_sem.at[0])
    dx_copies = [
        remote(dx_t.at[rank], dx_in.at[tensor], dx_send.at[number], dx_recv.at[number], device)
        for number, (rank, device) in enumerate(around)
    ]

    def turn(source, target):
        def body(step, carry):
            rows = pl.ds(pl.multiple_of(step * STEP, STEP), STEP)
            value = jnp.transpose(source[rows, :].astype(F32), (1, 0)).astype(BF)
            for rank in range(ranks):
                target[rank, :, rows] = value[rank * columns_each : (rank + 1) * columns_each]
            return carry

        lax.fori_loop(0, steps, body, 0)

    def share_outputs(source):
        turn(source, y_t)
        for copy in y_copies:
            copy.start()
        y_own.start()

    begin(0)
    vec[0] = jnp.zeros(vec.shape[1:], F32)

    @pl.when(section == 0)
    def _():
        first_y.start()
        for wave in range(1, len(waves)):
            begin(wave)
        first_y.wait()
        share_outputs(dx)

    @pl.when(section != 0)
    def _():
        start_g.start()
        start_g.wait()

    arrived(0)

    def add_row(row, value):
        vec[0, row : row + 1, :] += jnp.sum(value, axis=0, keepdims=True)

    def norm_back(arriving, normal, scale, gain):
        scaled = arriving * gain
        return (
            scaled
            - jnp.mean(scaled, axis=-1, keepdims=True)
            - normal * jnp.mean(scaled * normal, axis=-1, keepdims=True)
        ) * scale

    def second_back(step, carry):
        rows = pl.ds(pl.multiple_of(step * STEP, STEP), STEP)

        @pl.when(section == 0)
        def _():
            relay(step).wait_recv()

        arriving = g[rows, :].astype(F32)
        normal = n2[rows, :].astype(F32)
        add_row(12, arriving * normal)
        add_row(13, arriving)
        value = norm_back(arriving, normal, rs2[rows, 0:1], second_gain_ref[...].astype(F32))
        dsum[rows, :] = value
        value = value.astype(BF)
        low[rows, :] = value
        value = value.astype(F32)
        add_row(9, value)
        low_t[:, rows] = jnp.transpose(value, (1, 0)).astype(BF)
        return carry

    lax.fori_loop(0, steps, second_back, 0)

    def to_near(number, unit, which):
        return remote(
            near_out.at[unit % 2, which],
            near_in.at[number, unit, which],
            near_send.at[unit % 2, which],
            near_recv.at[number, unit, which],
            near,
        )

    def to_far(number, unit):
        return remote(
            near_in.at[number, unit, 1],
            far_in.at[number, unit],
            far_send.at[number, unit],
            far_recv.at[number, unit],
            far,
        )

    factor = (depth - data) * (depth - data) * (depth - data) % (depth + 1)

    def owner(unit):
        return (factor * (unit + 1)) % (depth + 1) - 1

    def rightward(number, block, slot):
        return remote(
            near_in.at[number, slot, 0],
            depth_in.at[number, block],
            depth_send.at[number, slot],
            depth_recv.at[number, block],
            right,
        )

    def leftward(number, block, slot, landing):
        return remote(
            near_in.at[number, slot, 0],
            depth_in.at[number, landing],
            depth_send.at[number, slot],
            depth_recv.at[number, landing],
            left,
        )

    def gradient(number, unit, rank):
        at = owner(unit) if inner else unit
        rows = pl.ds(pl.multiple_of(at * share, share), share)
        if number == 0:
            return nn(low_t[rows, :], act[rank])
        if number == 1:
            return nn(first_t[rows, :], slope[rank])
        main = nt(first_t[rows, :], p[rank])
        edge = (3 * part // 256) * 256
        tail = nt(low_t[rows, :], p[rank, edge : 4 * part, :])
        lane = lax.broadcasted_iota(jnp.int32, tail.shape, 1)
        tail = jnp.where(lane < 3 * part - edge, main[:, edge:], tail)
        return jnp.concatenate([main[:, :edge], tail], axis=1)

    def reduce_stage(number):
        def body(index, carry):
            @pl.when(index < units)
            def _():
                for which, rank in ((1, 3), (0, 1)):

                    @pl.when((index >= 2) | (number > 0))
                    def _():
                        to_near(number, index, which).wait_send()

                    near_out[index % 2, which] = gradient(number, index, rank).astype(BF)
                    to_near(number, index, which).start()

            @pl.when(index > 0)
            def _():
                unit = index - 1
                for which, rank in ((1, 2), (0, 0)):
                    mine = gradient(number, unit, rank)
                    to_near(number, unit, which).wait_recv()
                    near_in[number, unit, which] = (
                        mine + near_in[number, unit, which].astype(F32)
                    ).astype(BF)
                    if which == 1 and number == 0:

                        @pl.when(unit < 2)
                        def _():
                            to_far(number, unit).start()

            return carry

        lax.fori_loop(0, units + 1, body, 0)

    def finish(index):
        number = index // units
        unit = index % units
        to_far(number, unit).wait_recv()
        near_in[number, unit, 0] = (
            near_in[number, unit, 0].astype(F32) + far_in[number, unit].astype(F32)
        ).astype(BF)
        if inner:
            block = owner(unit)

            @pl.when(((block > data) & (data > 0)) | ((block < data) & (data < depth - 1)))
            def _():
                rightward(number, block, unit).wait_recv()
                near_in[number, unit, 0] = (
                    near_in[number, unit, 0].astype(F32) + depth_in[number, block].astype(F32)
                ).astype(BF)

            @pl.when(block > data)
            def _():
                rightward(number, block, unit).start()

            @pl.when(block < data)
            def _():
                landing = block + (depth - block) * ((block + 1) // data)
                leftward(number, block, unit, landing).start()

        @pl.when(index + 2 < 3 * units)
        def _():
            to_far((index + 2) // units, (index + 2) % units).start()


    @pl.when(section == 0)
    def _():
        arrived(4)
        reduce_stage(0)

    @pl.when(section != 0)
    def _():
        later_y.start()

    arrived(1)
    block = 256
    blocks = wu.shape[2] // block

    def narrow(index, carry):
        rank = index // blocks
        columns = pl.ds(pl.multiple_of((index % blocks) * block, block), block)
        value = nt(low[...], wd[rank, columns, :]) * slope[rank, :, columns].astype(F32)
        value = value.astype(BF)
        slope[rank, :, columns] = value
        vec[0, pl.ds(rank, 1), columns] = jnp.sum(value.astype(F32), axis=0, keepdims=True)
        return carry

    lax.fori_loop(0, ranks * blocks, narrow, 0)

    @pl.when(section == 0)
    def _():
        finish(0)

    arrived(2)

    def first_transpose(step, carry):
        rows = pl.ds(pl.multiple_of(step * STEP, STEP), STEP)
        value = n1[rows, :].astype(F32) * first_gain_ref[...].astype(F32)
        value = value + first_shift_ref[...].astype(F32)
        first_t[:, rows] = jnp.transpose(value, (1, 0)).astype(BF)
        return carry

    def up_gradients():
        lax.fori_loop(0, steps, first_transpose, 0)
        reduce_stage(1)

    @pl.when(section == 0)
    def _():
        up_gradients()
        finish(1)

    def first_back(step, carry):
        rows = pl.ds(pl.multiple_of(step * STEP, STEP), STEP)
        arriving = dsum[rows, :]
        for rank in range(ranks):
            arriving = arriving + nt(slope[rank, rows, :], wu[rank])
        normal = n1[rows, :].astype(F32)
        add_row(10, arriving * normal)
        add_row(11, arriving)
        value = norm_back(arriving, normal, rs1[rows, 0:1], first_gain_ref[...].astype(F32))
        dsum[rows, :] = value
        value = value.astype(BF)
        low[rows, :] = value
        add_row(8, value.astype(F32))
        return carry

    lax.fori_loop(0, steps, first_back, 0)

    @pl.when(section == 0)
    def _():
        finish(2)

    @pl.when(section != 0)
    def _():
        later_y.wait()
        pl.semaphore_wait(barrier, len(partners))
        share_outputs(g)

    arrived(3)

    def context_back(rank, carry):
        dcontext[rank] = nt(wa[rank, 3 * part : 4 * part, :], low[...]).astype(BF)
        return carry

    lax.fori_loop(0, ranks, context_back, 0)
    here = length_ref[tensor // sequences, tensor % sequences]
    visible = lax.broadcasted_iota(jnp.int32, (length, length), 0) < here

    def attend_back(head, carry):
        rank = head // heads
        base = (head % heads) * HD
        at_query = pl.ds(pl.multiple_of(base, HD), HD)
        at_keys = pl.ds(pl.multiple_of(part + base, HD), HD)
        at_values = pl.ds(pl.multiple_of(2 * part + base, HD), HD)
        query = (p[rank, at_query, :].astype(F32) * HD ** (-0.5)).astype(BF)
        keys = p[rank, at_keys, :]
        values = p[rank, at_values, :]
        dout = dcontext[rank, at_query, :]
        weights = jnp.where(visible, jnp.exp(tn(keys, query) - lse[head]), 0.0)
        dweights = tn(values, dout)
        inner_sum = jnp.sum(weights * dweights, axis=0, keepdims=True)
        dscores = (weights * (dweights - inner_sum)).astype(BF)
        p[rank, at_query, :] = (nn(keys, dscores) * HD ** (-0.5)).astype(BF)
        p[rank, at_keys, :] = nt(query, dscores).astype(BF)
        p[rank, at_values, :] = nt(dout, weights.astype(BF)).astype(BF)

        @pl.when((section == 0) & (head % 5 == 4))
        def _():
            finish(3 + head // 5)

        return carry

    lax.fori_loop(0, ranks * heads, attend_back, 0)
    early = 3 + ranks * heads // 5 + 1
    for rank in range(ranks):
        vec[0, 4 + rank : 5 + rank, :] = nt(jnp.ones((8, length), BF), p[rank])[0:1, :]

    @pl.when(section != 0)
    def _():
        arrived(4)

    vec_near = remote(vec.at[0], vec_in.at[0], vec_send.at[0], vec_recv.at[0], near)
    vec_near.start()

    def entering_back(step, carry):
        rows = pl.ds(pl.multiple_of(step * STEP, STEP), STEP)
        total = dsum[rows, :]
        for rank in range(ranks):
            total = total + tn(p[rank, 0 : 3 * part, rows], wa[rank, 0 : 3 * part, :])
        dx[rows, :] = total.astype(BF)

        @pl.when(section != 0)
        def _():
            relay(step).start()

        return carry

    lax.fori_loop(0, steps, entering_back, 0)
    vec_near.wait_recv()

    def join(level, swap):
        for row in range(vec.shape[1]):
            pair = row ^ swap if row < 8 else row
            vec[level + 1, row : row + 1, :] = (
                vec[level, row : row + 1, :] + vec_in[level, pair : pair + 1, :]
            )

    join(0, 1)
    vec_far = remote(vec.at[1], vec_in.at[1], vec_send.at[1], vec_recv.at[1], far)
    vec_far.start()
    turn(dx, dx_t)
    for copy in dx_copies:
        copy.start()
    dx_in[tensor] = dx_t[tensor]

    @pl.when(section == 0)
    def _():
        finish(early - 1)

    @pl.when(section != 0)
    def _():
        reduce_stage(0)
        up_gradients()
        finish(0)

    def entering_transpose(step, carry):
        rows = pl.ds(pl.multiple_of(step * STEP, STEP), STEP)
        first_t[:, rows] = jnp.transpose(xb[rows, :].astype(F32), (1, 0)).astype(BF)
        low_t[:, rows] = jnp.transpose(low[rows, :].astype(F32), (1, 0)).astype(BF)
        return carry

    lax.fori_loop(0, steps, entering_transpose, 0)
    reduce_stage(2)

    vec_far.wait_recv()
    join(1, 2)
    vec_deep = [
        remote(vec.at[2], vec_in.at[2 + hop], vec_send.at[2 + hop], vec_recv.at[2 + hop], device)
        for hop, device in enumerate(deep)
    ]
    for copy in vec_deep:
        copy.start()

    @pl.when(section != 0)
    def _():
        lax.fori_loop(1, early, lambda index, carry: (finish(index), carry)[1], 0)

    lax.fori_loop(early, 2 * units, lambda index, carry: (finish(index), carry)[1], 0)
    for copy in dx_copies:
        copy.wait_recv()
    dx_done = pltpu.make_async_copy(dx_in, dx_out, out_sem.at[1])
    dx_done.start()
    half = table.shape[0]
    table_x = remote(table_away, table, table_send.at[0], table_recv.at[0], other)
    table_deep = [
        remote(table, table_in.at[hop], table_send.at[1 + hop], table_recv.at[1 + hop], device)
        for hop, device in enumerate(deep)
    ]

    @pl.when(section == 0)
    def _():
        types_each = table_out.shape[0]
        table_sum[...] = jnp.zeros_like(table_sum)

        def count(number, carry):
            row = lax.broadcasted_iota(jnp.int32, (2 * half, length), 0)
            picks = jnp.zeros((2 * half, length), F32)
            micro, item = number // sequences, number % sequences
            offset = 0
            for ids_ref, number_of in (
                (segment_ref, 2),
                (column_ref, COLS),
                (row_ref, ROWS),
                (answer_ref, 2),
            ):
                ids = ids_ref[micro, pl.ds(item, 1), :] + offset
                ids = ids + jnp.where(ids >= types_each, half - types_each, 0)
                picks = picks + jnp.where(ids == row, 1.0, 0.0)
                offset += number_of
            table_sum[...] += nt(picks.astype(BF), dx_in[number])
            return carry

        lax.fori_loop(0, ranks, count, 0)
        table[...] = table_sum[:half].astype(BF)
        table_away[...] = table_sum[half:].astype(BF)
        table_x.start()
        for copy in table_deep:
            copy.start()

    lax.fori_loop(2 * units, 3 * units - 1, lambda index, carry: (finish(index), carry)[1], 0)

    @pl.when(section != 0)
    def _():
        table_x.wait_recv()
        for copy in table_deep:
            copy.start()

    finish(3 * units - 1)
    copies = []
    if inner:
        for number in range(3):
            total = jnp.zeros(final.shape[1:], F32)
            for unit in range(units):
                keep = jnp.where(owner(unit) == data, 1.0, 0.0)
                total = total + near_in[number, unit, 0].astype(F32) * keep
            final[number] = total

            @pl.when(data > 0)
            def _():
                rightward(number, data, 0).wait_recv()
                final[number] = final[number] + depth_in[number, data].astype(F32)

            @pl.when(data < depth - 1)
            def _():
                leftward(number, data, 0, depth).wait_recv()
                final[number] = final[number] + depth_in[number, depth].astype(F32)

            copy = pltpu.make_async_copy(
                final.at[number], sums_out.at[number], out_sem.at[2 + number]
            )
            copy.start()
            copies.append(copy)
    else:
        copy = pltpu.make_async_copy(
            near_in.at[:, :, 0], sums_out, out_sem.at[2]
        )
        copy.start()
        copies.append(copy)
    total = vec[2]
    for hop, copy in enumerate(vec_deep):
        copy.wait_recv()
        total = total + vec_in[2 + hop]
    vec_out[...] = total
    total = table[...].astype(F32)
    for hop, copy in enumerate(table_deep):
        copy.wait_recv()
        total = total + table_in[hop].astype(F32)
    table_out[...] = total[: table_out.shape[0]]

    for copy in y_copies:
        copy.wait()
    y_own.wait()
    for copy in dx_copies:
        copy.wait_send()
    vec_near.wait_send()
    vec_far.wait_send()
    for copy in vec_deep + table_deep:
        copy.wait_send()
    for unit in range(2):
        for which in range(2):
            to_near(2, unit, which).wait_send()
    for number in range(3):
        for unit in range(units):
            to_far(number, unit).wait_send()
            if inner:

                @pl.when(owner(unit) != data)
                def _():
                    rightward(number, 0, unit).wait_send()

    @pl.when(section != 0)
    def _():
        for step in range(steps):
            relay(step).wait_send()

    @pl.when(section == 0)
    def _():
        table_x.wait_send()

    dx_done.wait()
    for copy in copies:
        copy.wait()


def backward(cotangent, saved, lengths, vectors, ids, type_half, inner):
    wa, wu, wd, p, lse, act, slope, n1, n2, rs1, rs2, x, y = saved
    ranks = wa.shape[0]
    length, width = x.shape
    steps = length // STEP
    depth = lax.axis_size("dp")
    units = depth if inner else 4
    hops = depth - 1 if inner else 0
    share = width // units
    anywhere = pl.BlockSpec(memory_space=pl.ANY)
    inside = pl.BlockSpec(memory_space=pltpu.VMEM)
    part = wa.shape[1] // 4
    each = width // ranks
    half = -(-type_half // 16) * 16

    def like(value):
        return pltpu.VMEM(value.shape, value.dtype)

    plane = (length, width)
    turned = (width, length)
    chunk = (share, width)
    spread = (ranks, each, length)
    semaphores = pltpu.SemaphoreType.DMA
    sums = ((3,) + chunk, F32) if inner else ((3, units) + chunk, BF)
    return pl.pallas_call(
        functools.partial(backward_kernel, inner),
        name="backward_layer",
        out_shape=(
            jax.ShapeDtypeStruct(*sums),
            jax.ShapeDtypeStruct(spread, BF),
            jax.ShapeDtypeStruct(spread, BF),
            jax.ShapeDtypeStruct((16, width), F32),
            jax.ShapeDtypeStruct((type_half, each), F32),
        ),
        in_specs=[anywhere] * 14
        + [pl.BlockSpec(memory_space=pltpu.SMEM)]
        + [inside] * (len(vectors) + len(ids)),
        out_specs=(anywhere, anywhere, anywhere, inside, inside),
        scratch_shapes=[like(value) for value in saved[:-1]]
        + [
            pltpu.VMEM(plane, BF),
            pltpu.VMEM(plane, F32),
            pltpu.VMEM(plane, BF),
            pltpu.VMEM(turned, BF),
            pltpu.VMEM(turned, BF),
            pltpu.VMEM((ranks, part, length), BF),
            pltpu.VMEM(plane, BF),
            pltpu.VMEM(spread, BF),
            pltpu.VMEM(spread, BF),
            pltpu.VMEM(spread, BF),
            pltpu.VMEM((2, 2) + chunk, BF),
            pltpu.VMEM((3, units, 2) + chunk, BF),
            pltpu.VMEM((3, units) + chunk, BF),
            pltpu.VMEM((3, units + 1) + (chunk if inner else (16, 128)), BF),
            pltpu.VMEM((3,) + (chunk if inner else (16, 128)), F32),
            pltpu.VMEM((3, 16, width), F32),
            pltpu.VMEM((2 + hops, 16, width), F32),
            pltpu.VMEM((half, each), BF),
            pltpu.VMEM((half, each), BF),
            pltpu.VMEM((max(hops, 1), half, each), BF),
            pltpu.VMEM((2 * half, each), F32),
            semaphores((15,)),
            semaphores((2, 2)),
            semaphores((3, units, 2)),
            semaphores((3, units)),
            semaphores((3, units)),
            semaphores((3, units)),
            semaphores((3, units + 1)),
            semaphores((steps,)),
            semaphores((steps,)),
            semaphores((3,)),
            semaphores((3,)),
            semaphores((3,)),
            semaphores((3,)),
            semaphores((2 + hops,)),
            semaphores((2 + hops,)),
            semaphores((1 + hops,)),
            semaphores((1 + hops,)),
            semaphores((5,)),
        ],
        compiler_params=pltpu.CompilerParams(
            collective_id=1, has_side_effects=True, vmem_limit_bytes=VMEM_LIMIT
        ),
        cost_estimate=pl.CostEstimate(
            flops=17_000_000_000, bytes_accessed=60_000_000, transcendentals=3_000_000
        ),
    )(cotangent, *saved, lengths, *vectors, *ids)


def on_device(
    inputs,
    cotangent,
    segment_ids,
    column_ids,
    row_ids,
    answer_ids,
    lengths,
    type_table,
    query_weight,
    query_bias,
    key_weight,
    value_weight,
    value_bias,
    output_weight,
    output_bias,
    first_gain,
    first_shift,
    up_weight,
    up_bias,
    down_weight,
    down_bias,
    second_gain,
    second_shift,
):
    tensor = lax.axis_index("tensor")
    ranks = lax.axis_size("tensor")
    micro_count, sequences, length, width = inputs.shape
    type_count = 4 + COLS + ROWS
    part = query_weight.shape[2]
    hidden = up_weight.shape[2]

    ids = (segment_ids, column_ids, row_ids, answer_ids)
    wa = jnp.concatenate(
        [query_weight[0].T, key_weight[0].T, value_weight[0].T, output_weight[0]], axis=0
    )
    vectors = (
        query_bias,
        value_bias,
        up_bias,
        output_bias,
        first_gain,
        first_shift,
        down_bias,
        second_gain,
        second_shift,
    )
    saved = forward(
        inputs, ids, type_table, lengths, wa, up_weight[0], down_weight[0], vectors, ranks
    )
    depth = lax.axis_size("dp")
    inner = depth == 4 and width % (16 * depth) == 0
    type_half = type_count // lax.axis_size("section")
    sums, dx, leaving, vecs, table_grad = backward(
        cotangent, saved, lengths, (first_gain, first_shift, second_gain), ids, type_half, inner
    )

    def in_columns(value):
        return jnp.swapaxes(value, 1, 2).reshape(
            1, micro_count, sequences, length, width // ranks
        )

    layer_outputs = in_columns(leaving)
    layer_input_grads = in_columns(dx).astype(F32)
    if inner:
        summed = sums
    else:
        summed = lax.psum_scatter(
            sums.reshape(3, width, width), "dp", scatter_dimension=1, tiled=True
        ).astype(F32)
        vecs = lax.psum(vecs, "dp")
        table_grad = lax.psum(table_grad.astype(BF), "dp").astype(F32)
    mine = lax.dynamic_slice_in_dim(
        vecs[8:14].reshape(6, ranks, width // ranks), tensor, 1, 1
    ).reshape(1, 6 * (width // ranks))
    mine = jnp.concatenate([vecs[0:1], vecs[4:5], mine], axis=1)

    def vector(start, count):
        return mine[:, start : start + count]

    share = width // ranks
    after = 2 * width
    return (
        layer_outputs,
        layer_input_grads,
        summed[2, :, 0:part][None],
        vector(width, part),
        summed[2, :, part : 2 * part][None],
        summed[2, :, 2 * part : 3 * part][None],
        vector(width + 2 * part, part),
        summed[2, :, 3 * part : 4 * part].T[None],
        vector(after, share),
        vector(after + 2 * share, share),
        vector(after + 3 * share, share),
        summed[1][None],
        vector(0, hidden),
        summed[0].T[None],
        vector(after + share, share),
        vector(after + 4 * share, share),
        vector(after + 5 * share, share),
        table_grad,
    )


def solution(mesh):
    return jax.shard_map(
        on_device,
        mesh=mesh,
        in_specs=(
            P(None, "dp", None, None),
            P(None, "dp", None, None),
            P(None, "dp", None),
            P(None, "dp", None),
            P(None, "dp", None),
            P(None, "dp", None),
            P(None, "dp"),
            P(),
            P("section", None, "tensor"),
            P("section", "tensor"),
            P("section", None, "tensor"),
            P("section", None, "tensor"),
            P("section", "tensor"),
            P("section", "tensor", None),
            P("section", None),
            P("section", None),
            P("section", None),
            P("section", None, "tensor"),
            P("section", "tensor"),
            P("section", "tensor", None),
            P("section", None),
            P("section", None),
            P("section", None),
        ),
        out_specs=(
            P("section", None, "dp", None, "tensor"),
            P("section", None, "dp", None, "tensor"),
            P("section", "dp", "tensor"),
            P("section", "tensor"),
            P("section", "dp", "tensor"),
            P("section", "dp", "tensor"),
            P("section", "tensor"),
            P("section", "tensor", "dp"),
            P("section", "tensor"),
            P("section", "tensor"),
            P("section", "tensor"),
            P("section", "dp", "tensor"),
            P("section", "tensor"),
            P("section", "tensor", "dp"),
            P("section", "tensor"),
            P("section", "tensor"),
            P("section", "tensor"),
            P("section", "tensor"),
        ),
        check_vma=False,
    )
```

```python
import functools

import jax
import jax.numpy as jnp
from jax import lax
from jax.experimental import pallas as pl
from jax.experimental.pallas import tpu as pltpu
from jax.sharding import PartitionSpec as P

HD = 64
COLS = 256
ROWS = 256
EPSILON = 1e-12
MASKED = -1e30
BF = jnp.bfloat16
F32 = jnp.float32
MESH = pl.DeviceIdType.MESH
VMEM_LIMIT = 60 * 1024 * 1024
STEP = 256
OUTS = ("wa", "wu", "wd", "p", "lse", "act", "slope", "n1", "n2", "rs1", "rs2", "x", "y")


def nn(left, right):
    return lax.dot_general(left, right, (((1,), (0,)), ((), ())), preferred_element_type=F32)


def nt(left, right):
    return lax.dot_general(left, right, (((1,), (1,)), ((), ())), preferred_element_type=F32)


def tn(left, right):
    return lax.dot_general(left, right, (((0,), (0,)), ((), ())), preferred_element_type=F32)


def normalize(value):
    centered = value - jnp.mean(value, axis=-1, keepdims=True)
    variance = jnp.mean(centered * centered, axis=-1, keepdims=True)
    scale = lax.rsqrt(variance + EPSILON)
    return centered * scale, scale


def place():
    section = lax.axis_index("section")
    data = lax.axis_index("dp")
    tensor = lax.axis_index("tensor")
    beside = tensor + 1 - 2 * (tensor % 2)
    across = tensor + 2 - 4 * ((tensor // 2) % 2)
    return section, data, tensor, beside, across


def greet(partners):
    barrier = pltpu.get_barrier_semaphore()
    for partner in partners:
        pl.semaphore_signal(barrier, inc=1, device_id=partner, device_id_type=MESH)
    pl.semaphore_wait(barrier, len(partners))


def remote(src, dst, send, recv, device):
    return pltpu.make_async_remote_copy(
        src_ref=src, dst_ref=dst, send_sem=send, recv_sem=recv, device_id=device, device_id_type=MESH
    )


def forward_kernel(
    inputs_ref,
    segment_ref,
    column_ref,
    row_ref,
    answer_ref,
    table_ref,
    length_ref,
    wa_ref,
    wu_ref,
    wd_ref,
    query_bias_ref,
    value_bias_ref,
    up_bias_ref,
    output_bias_ref,
    first_gain_ref,
    first_shift_ref,
    down_bias_ref,
    second_gain_ref,
    second_shift_ref,
    wa_out,
    wu_out,
    wd_out,
    p_out,
    lse_out,
    act_out,
    slope_out,
    n1_out,
    n2_out,
    rs1_out,
    rs2_out,
    x_out,
    y_out,
    wa,
    wu,
    wd,
    bias,
    table,
    p,
    lse,
    act,
    slope,
    xf,
    xb,
    first,
    low,
    n1,
    n2,
    rs1,
    rs2,
    y,
    gather_send,
    gather_recv,
    chain_send,
    chain_recv,
    relay_send,
    relay_recv,
    local_sem,
    out_sem,
    turn_sem,
):
    section, data, tensor, beside, across = place()
    length, width = xf.shape
    ranks = wa.shape[0]
    heads = wa.shape[1] // (4 * HD)
    part = heads * HD
    steps = length // STEP
    sequences = inputs_ref.shape[1]
    near = (section, data, beside)
    far = (section, data, across)
    other = (1 - section, data, tensor)
    depth = lax.axis_size("dp")
    group = 4 if depth % 4 == 0 else 1
    spot = data % group
    before = (section, data - spot + (spot + group - 1) % group, tensor)
    after = (section, data - spot + (spot + 1) % group, tensor)
    greet([near, far, other] + ([before, after] if group > 1 else []))

    shards = ((wa_ref, wa), (wu_ref, wu), (wd_ref, wd))
    direct = wa.shape[1] * 5 // 12
    piece = (wa.shape[1] - direct) // group

    def rows_of(number):
        return pl.ds(pl.multiple_of(direct + number * piece, 16), piece)

    to_far = []
    to_near = []
    onward = []
    own = []
    for number, (source, target) in enumerate(shards):
        to_far.append(
            [
                remote(
                    source.at[rows],
                    target.at[2, rows],
                    gather_send.at[number, which],
                    gather_recv.at[number, which],
                    far,
                )
                for which, rows in enumerate((rows_of(spot), pl.ds(0, direct)))
            ]
        )
        to_near.append(
            remote(source, target.at[1], gather_send.at[number, 2], gather_recv.at[number, 2], near)
        )
        rest = wa.shape[1] - direct
        onward.append(
            [
                remote(
                    target.at[2, rows],
                    target.at[3, rows],
                    gather_send.at[number, 3 + which],
                    gather_recv.at[number, 3 + which],
                    near,
                )
                for which, rows in enumerate((pl.ds(0, direct), pl.ds(direct, rest)))
            ]
        )
        own.append(pltpu.make_async_copy(source, target.at[0], local_sem.at[number]))
    to_far[0][0].start()
    for copy in to_near:
        copy.start()
    for copy in own:
        copy.start()
    bias[0] = jnp.zeros(bias.shape[1:], F32)
    bias[0, 0:1, :] = up_bias_ref[...].astype(F32)
    bias[0, 1:2, 0:part] = query_bias_ref[...].astype(F32)
    bias[0, 1:2, 2 * part : 3 * part] = value_bias_ref[...].astype(F32)
    bias_copies = [
        remote(bias.at[0], bias.at[1 + which], gather_send.at[3, which], gather_recv.at[3, which], to)
        for which, to in enumerate((near, far))
    ]
    bias_onward = remote(bias.at[2], bias.at[3], gather_send.at[3, 2], gather_recv.at[3, 2], near)
    for copy in bias_copies:
        copy.start()

    def chain(number, hop, up):
        rows = rows_of(spot - (hop - 1) if up else spot + (hop - 1))
        target = shards[number][1]
        at = 0 if up else 1
        return remote(
            target.at[2, rows],
            target.at[2, rows],
            chain_send.at[number, at, hop - 1],
            chain_recv.at[number, at, hop - 1],
            after if up else before,
        )

    def chained(number, hop, up):
        rows = rows_of(spot - hop if up else spot + hop)
        target = shards[number][1]
        at = 0 if up else 1
        return remote(
            target.at[2, rows],
            target.at[2, rows],
            chain_send.at[number, at, hop - 1],
            chain_recv.at[number, at, hop - 1],
            before if up else after,
        )

    def piece_in(number):
        to_far[number][0].wait_recv()

    def send_piece(number):
        to_far[number][0].start()

    def send_direct(number):
        to_far[number][1].start()

    def hand_on(number, hop):
        if group == 1 or hop == group:
            return
        if hop > 0:

            @pl.when(spot >= hop)
            def _():
                chained(number, hop, True).wait_recv()

            @pl.when(spot + hop < group)
            def _():
                chained(number, hop, False).wait_recv()

        if hop + 1 < group:

            @pl.when((spot >= hop) & (spot + 1 < group))
            def _():
                chain(number, hop + 1, True).start()

            @pl.when((spot + hop < group) & (spot >= 1))
            def _():
                chain(number, hop + 1, False).start()

    def direct_in(number):
        to_far[number][1].wait_recv()
        onward[number][0].start()

    def pass_on(number):
        onward[number][1].start()

    def ready(number):
        own[number].wait()
        to_near[number].wait_recv()
        for copy in onward[number]:
            copy.wait_recv()

    def at_first(actions):
        @pl.when(section == 0)
        def _():
            for action, *values in actions:
                action(*values)

    out_copies = []

    wu_copy = pltpu.make_async_copy(wu, wu_out, out_sem.at[len(OUTS)])
    wd_copy = pltpu.make_async_copy(wd, wd_out, out_sem.at[len(OUTS) + 1])

    def put_out(source, target):
        copy = pltpu.make_async_copy(source, target, out_sem.at[len(out_copies)])
        copy.start()
        out_copies.append(copy)

    relays = [
        remote(
            y.at[pl.ds(step * STEP, STEP)],
            xb.at[pl.ds(step * STEP, STEP)],
            relay_send.at[step],
            relay_recv.at[step],
            other,
        )
        for step in range(steps)
    ]

    load_input = pltpu.make_async_copy(
        inputs_ref.at[tensor // sequences, tensor % sequences], xb, local_sem.at[3]
    )

    @pl.when(section == 0)
    def _():
        load_input.start()

    piece_in(0)
    hand_on(0, 0)
    send_piece(1)
    send_direct(0)
    bias_copies[1].wait_recv()
    bias_onward.start()

    @pl.when(section == 0)
    def _():
        load_input.wait()
        types = table.shape[0]
        table[...] = jnp.zeros_like(table)
        table[0 : table_ref.shape[0], :] = table_ref[...]
        micro, item = tensor // sequences, tensor % sequences
        offset = 0
        row = lax.broadcasted_iota(jnp.int32, (types, length), 0)
        picks = jnp.zeros((types, length), F32)
        for ids_ref, count in (
            (segment_ref, 2),
            (column_ref, COLS),
            (row_ref, ROWS),
            (answer_ref, 2),
        ):
            ids = ids_ref[micro, pl.ds(item, 1), :] + offset
            picks = picks + jnp.where(ids == row, 1.0, 0.0)
            offset += count
        xf[...] = xb[...].astype(F32) + tn(picks.astype(BF), table[...])
        xb[...] = xf[...].astype(BF)

    hand_on(0, 1)
    hand_on(0, 2)
    piece_in(1)
    hand_on(1, 0)
    send_piece(2)
    direct_in(0)
    send_direct(1)
    hand_on(0, 3)
    pass_on(0)
    hand_on(1, 1)
    ready(0)
    put_out(wa, wa_out)

    @pl.when(section != 0)
    def _():
        piece_in(2)
        hand_on(2, 0)
        hand_on(1, 2)
        hand_on(2, 1)
        hand_on(1, 3)
        direct_in(1)
        pass_on(1)
        send_direct(2)
        hand_on(2, 2)
        hand_on(2, 3)
        direct_in(2)
        pass_on(2)
        ready(1)
        wu_copy.start()
        ready(2)
        wd_copy.start()
        for relay in relays:
            relay.wait_recv()
        xf[...] = xb[...].astype(F32)

    bias_copies[0].wait_recv()
    bias_onward.wait_recv()
    put_out(xb, x_out)

    def project(rank, carry):
        columns = jnp.transpose(bias[rank], (1, 0))
        p[rank, 0 : 3 * part, :] = (
            nt(wa[rank, 0 : 3 * part, :], xb[...]) + columns[0 : 3 * part, 1:2]
        ).astype(BF)
        return carry

    lax.fori_loop(0, ranks, project, 0)
    at_first([(piece_in, 2), (hand_on, 2, 0)])

    here = length_ref[tensor // sequences, tensor % sequences]
    visible = lax.broadcasted_iota(jnp.int32, (length, length), 0) < here

    def attend(head, carry):
        rank = head // heads
        base = (head % heads) * HD
        query = p[rank, pl.ds(pl.multiple_of(base, HD), HD), :]
        keys = p[rank, pl.ds(pl.multiple_of(part + base, HD), HD), :]
        values = p[rank, pl.ds(pl.multiple_of(2 * part + base, HD), HD), :]
        query = (query.astype(F32) * HD ** (-0.5)).astype(BF)
        scores = jnp.where(visible, tn(keys, query), MASKED)
        maximum = jnp.max(scores, axis=0, keepdims=True)
        raised = jnp.exp(scores - maximum)
        total = jnp.sum(raised, axis=0, keepdims=True)
        context = nn(values, raised.astype(BF)) / total
        p[rank, pl.ds(pl.multiple_of(3 * part + base, HD), HD), :] = context.astype(BF)
        lse[head] = maximum + jnp.log(total)
        for at, action in (
            (2, (hand_on, 1, 2)),
            (7, (hand_on, 2, 1)),
            (7, (direct_in, 1)),
            (7, (send_direct, 2)),
            (11, (hand_on, 1, 3)),
            (11, (pass_on, 1)),
        ):

            @pl.when((section == 0) & (head == at))
            def _():
                action[0](*action[1:])

        return carry

    lax.fori_loop(0, ranks * heads, attend, 0)
    put_out(p, p_out)
    put_out(lse, lse_out)

    def first_norm(step, carry):
        rows = pl.ds(pl.multiple_of(step * STEP, STEP), STEP)
        total = xf[rows, :] + output_bias_ref[...].astype(F32)
        for rank in range(ranks):
            total = total + tn(p[rank, 3 * part : 4 * part, rows], wa[rank, 3 * part : 4 * part, :])
        normal, scale = normalize(total)
        value = normal * first_gain_ref[...].astype(F32) + first_shift_ref[...].astype(F32)
        first[rows, :] = value
        low[rows, :] = value.astype(BF)
        n1[rows, :] = normal.astype(BF)
        rs1[rows, :] = jnp.broadcast_to(scale, (STEP, 128))
        return carry

    lax.fori_loop(0, steps, first_norm, 0)
    put_out(n1, n1_out)
    put_out(rs1, rs1_out)
    at_first([(hand_on, 2, 2), (ready, 1), (wu_copy.start,)])
    block = 256
    blocks = wu.shape[2] // block

    def widen(index, carry):
        rank = index // blocks
        columns = pl.ds(pl.multiple_of((index % blocks) * block, block), block)
        hidden = nn(low[...], wu[rank, :, columns]) + bias[rank, 0:1, columns]
        inner = 0.5 * (1.0 + lax.erf(hidden * (0.5**0.5)))
        act[rank, :, columns] = (hidden * inner).astype(BF)
        density = jnp.exp(hidden * hidden * (-0.5)) * 0.3989422804014327
        slope[rank, :, columns] = (inner + hidden * density).astype(BF)

        @pl.when((section == 0) & (index == ranks * blocks - 4))
        def _():
            direct_in(2)
            hand_on(2, 3)
            pass_on(2)

        return carry

    lax.fori_loop(0, ranks * blocks, widen, 0)
    put_out(act, act_out)
    put_out(slope, slope_out)
    at_first([(ready, 2), (wd_copy.start,)])

    for step in range(steps):
        rows = pl.ds(step * STEP, STEP)
        total = first[rows, :] + down_bias_ref[...].astype(F32)
        for rank in range(ranks):
            total = total + nn(act[rank, rows, :], wd[rank])
        normal, scale = normalize(total)
        y[rows, :] = (
            normal * second_gain_ref[...].astype(F32) + second_shift_ref[...].astype(F32)
        ).astype(BF)
        n2[rows, :] = normal.astype(BF)
        rs2[rows, :] = jnp.broadcast_to(scale, (STEP, 128))

        @pl.when((section == 0) & (tensor % 2 == 0))
        def _():
            relays[step].start()

    put_out(n2, n2_out)
    put_out(rs2, rs2_out)
    put_out(y, y_out)

    @pl.when((section == 0) & (tensor % 2 == 0))
    def _():
        for relay in relays:
            relay.wait_send()
        pl.semaphore_signal(turn_sem, inc=1, device_id=near, device_id_type=MESH)

    @pl.when((section == 0) & (tensor % 2 == 1))
    def _():
        pl.semaphore_wait(turn_sem, 1)
        for relay in relays:
            relay.start()
        for relay in relays:
            relay.wait_send()

    for copy in out_copies + [wu_copy, wd_copy]:
        copy.wait()
    for copies in to_far + onward + [to_near, bias_copies, [bias_onward]]:
        for copy in copies:
            copy.wait_send()
    for number in range(3):
        for hop in range(group - 1):

            @pl.when((spot >= hop) & (spot + 1 < group))
            def _():
                chain(number, hop + 1, True).wait_send()

            @pl.when((spot + hop < group) & (spot >= 1))
            def _():
                chain(number, hop + 1, False).wait_send()


def forward(inputs, ids, table, lengths, wa, wu, wd, vectors, ranks):
    length, width = inputs.shape[2], inputs.shape[3]
    rows_a = wa.shape[0]
    hidden = wu.shape[1]
    heads = ranks * (rows_a // (4 * HD))
    steps = length // STEP
    shapes = dict(
        wa=((ranks, rows_a, width), BF),
        wu=((ranks, width, hidden), BF),
        wd=((ranks, hidden, width), BF),
        p=((ranks, rows_a, length), BF),
        lse=((heads, 1, length), F32),
        act=((ranks, length, hidden), BF),
        slope=((ranks, length, hidden), BF),
        n1=((length, width), BF),
        n2=((length, width), BF),
        rs1=((length, 128), F32),
        rs2=((length, 128), F32),
        x=((length, width), BF),
        y=((length, width), BF),
    )

    def buffer(name):
        return pltpu.VMEM(*shapes[name])

    anywhere = pl.BlockSpec(memory_space=pl.ANY)
    inside = pl.BlockSpec(memory_space=pltpu.VMEM)
    return pl.pallas_call(
        forward_kernel,
        name="forward_layer",
        out_shape=tuple(jax.ShapeDtypeStruct(*shapes[name]) for name in OUTS),
        in_specs=[
            anywhere,
            inside,
            inside,
            inside,
            inside,
            inside,
            pl.BlockSpec(memory_space=pltpu.SMEM),
            anywhere,
            anywhere,
            anywhere,
        ]
        + [inside] * len(vectors),
        out_specs=tuple(anywhere for _ in OUTS),
        scratch_shapes=[
            buffer("wa"),
            buffer("wu"),
            buffer("wd"),
            pltpu.VMEM((ranks, 8, hidden), F32),
            pltpu.VMEM((-(-table.shape[0] // 16) * 16, width), BF),
            buffer("p"),
            buffer("lse"),
            buffer("act"),
            buffer("slope"),
            pltpu.VMEM((length, width), F32),
            buffer("x"),
            pltpu.VMEM((length, width), F32),
            pltpu.VMEM((length, width), BF),
            buffer("n1"),
            buffer("n2"),
            buffer("rs1"),
            buffer("rs2"),
            buffer("y"),
            pltpu.SemaphoreType.DMA((4, 5)),
            pltpu.SemaphoreType.DMA((4, 5)),
            pltpu.SemaphoreType.DMA((3, 2, 3)),
            pltpu.SemaphoreType.DMA((3, 2, 3)),
            pltpu.SemaphoreType.DMA((steps,)),
            pltpu.SemaphoreType.DMA((steps,)),
            pltpu.SemaphoreType.DMA((5,)),
            pltpu.SemaphoreType.DMA((len(OUTS) + 2,)),
            pltpu.SemaphoreType.REGULAR,
        ],
        compiler_params=pltpu.CompilerParams(
            collective_id=0, has_side_effects=True, vmem_limit_bytes=VMEM_LIMIT
        ),
        cost_estimate=pl.CostEstimate(
            flops=8_000_000_000, bytes_accessed=60_000_000, transcendentals=6_000_000
        ),
    )(inputs, *ids, table, lengths, wa, wu, wd, *vectors)


def backward_kernel(
    inner,
    cotangent_ref,
    wa_ref,
    wu_ref,
    wd_ref,
    p_ref,
    lse_ref,
    act_ref,
    slope_ref,
    n1_ref,
    n2_ref,
    rs1_ref,
    rs2_ref,
    x_ref,
    y_ref,
    length_ref,
    first_gain_ref,
    first_shift_ref,
    second_gain_ref,
    segment_ref,
    column_ref,
    row_ref,
    answer_ref,
    sums_out,
    dx_out,
    y_out,
    vec_out,
    table_out,
    wa,
    wu,
    wd,
    p,
    lse,
    act,
    slope,
    n1,
    n2,
    rs1,
    rs2,
    xb,
    g,
    dsum,
    low,
    low_t,
    first_t,
    dcontext,
    dx,
    dx_t,
    dx_in,
    y_t,
    near_out,
    near_in,
    far_in,
    depth_in,
    final,
    vec,
    vec_in,
    table,
    table_away,
    table_in,
    table_sum,
    load_sem,
    near_send,
    near_recv,
    far_send,
    far_recv,
    depth_send,
    depth_recv,
    relay_send,
    relay_recv,
    dx_send,
    dx_recv,
    y_send,
    y_recv,
    vec_send,
    vec_recv,
    table_send,
    table_recv,
    out_sem,
):
    section, data, tensor, beside, across = place()
    diagonal = beside + 2 - 4 * ((beside // 2) % 2)
    length, width = g.shape
    ranks = wa.shape[0]
    heads = wa.shape[1] // (4 * HD)
    part = heads * HD
    steps = length // STEP
    sequences = cotangent_ref.shape[1]
    units = near_in.shape[1]
    share = near_in.shape[3]
    columns_each = width // ranks
    depth = lax.axis_size("dp")
    near = (section, data, beside)
    far = (section, data, across)
    corner = (section, data, diagonal)
    other = (1 - section, data, tensor)
    deep = []
    left = right = None
    if inner:
        deep = [(section, (data + 1 + hop) % depth, tensor) for hop in range(depth - 1)]
        left = (section, (data + depth - 1) % depth, tensor)
        right = (section, (data + 1) % depth, tensor)
    partners = [near, far, corner, other] + deep
    barrier = pltpu.get_barrier_semaphore()
    for partner in partners:
        pl.semaphore_signal(barrier, inc=1, device_id=partner, device_id_type=MESH)

    @pl.when(section == 0)
    def _():
        pl.semaphore_wait(barrier, len(partners))

    loads = {}
    for name, source, target in (
        ("n2", n2_ref, n2),
        ("rs2", rs2_ref, rs2),
        ("wd", wd_ref, wd),
        ("slope", slope_ref, slope),
        ("wu", wu_ref, wu),
        ("act", act_ref, act),
        ("n1", n1_ref, n1),
        ("rs1", rs1_ref, rs1),
        ("wa", wa_ref, wa),
        ("p", p_ref, p),
        ("lse", lse_ref, lse),
        ("xb", x_ref, xb),
    ):
        loads[name] = pltpu.make_async_copy(source, target, load_sem.at[len(loads)])
    start_g = pltpu.make_async_copy(
        cotangent_ref.at[tensor // sequences, tensor % sequences], g, load_sem.at[len(loads)]
    )
    first_y = pltpu.make_async_copy(y_ref, dx, load_sem.at[len(loads) + 1])
    later_y = pltpu.make_async_copy(y_ref, g, load_sem.at[len(loads) + 1])
    waves = (("n2", "rs2"), ("wd", "slope"), ("wu", "n1", "rs1"), ("wa", "p", "lse"), ("act", "xb"))

    def begin(wave):
        for name in waves[wave]:
            loads[name].start()

    def arrived(wave):
        for name in waves[wave]:
            loads[name].wait()
        if wave + 1 < len(waves):

            @pl.when(section != 0)
            def _():
                begin(wave + 1)


    def relay(step):
        rows = pl.ds(pl.multiple_of(step * STEP, STEP), STEP)
        return remote(dx.at[rows], g.at[rows], relay_send.at[step], relay_recv.at[step], other)

    around = ((beside, near), (across, far), (diagonal, corner))
    y_copies = [
        remote(y_t.at[rank], y_out.at[tensor], y_send.at[number], y_recv.at[number], device)
        for number, (rank, device) in enumerate(around)
    ]
    y_own = pltpu.make_async_copy(y_t.at[tensor], y_out.at[tensor], out_sem.at[0])
    dx_copies = [
        remote(dx_t.at[rank], dx_in.at[tensor], dx_send.at[number], dx_recv.at[number], device)
        for number, (rank, device) in enumerate(around)
    ]

    def turn(source, target):
        def body(step, carry):
            rows = pl.ds(pl.multiple_of(step * STEP, STEP), STEP)
            value = jnp.transpose(source[rows, :].astype(F32), (1, 0)).astype(BF)
            for rank in range(ranks):
                target[rank, :, rows] = value[rank * columns_each : (rank + 1) * columns_each]
            return carry

        lax.fori_loop(0, steps, body, 0)

    def share_outputs(source):
        turn(source, y_t)
        for copy in y_copies:
            copy.start()
        y_own.start()

    begin(0)
    vec[0] = jnp.zeros(vec.shape[1:], F32)

    @pl.when(section == 0)
    def _():
        first_y.start()
        for wave in range(1, len(waves)):
            begin(wave)
        first_y.wait()
        share_outputs(dx)

    @pl.when(section != 0)
    def _():
        start_g.start()
        start_g.wait()

    arrived(0)

    def add_row(row, value):
        vec[0, row : row + 1, :] += jnp.sum(value, axis=0, keepdims=True)

    def norm_back(arriving, normal, scale, gain):
        scaled = arriving * gain
        return (
            scaled
            - jnp.mean(scaled, axis=-1, keepdims=True)
            - normal * jnp.mean(scaled * normal, axis=-1, keepdims=True)
        ) * scale

    def second_back(step, carry):
        rows = pl.ds(pl.multiple_of(step * STEP, STEP), STEP)

        @pl.when(section == 0)
        def _():
            relay(step).wait_recv()

        arriving = g[rows, :].astype(F32)
        normal = n2[rows, :].astype(F32)
        add_row(12, arriving * normal)
        add_row(13, arriving)
        value = norm_back(arriving, normal, rs2[rows, 0:1], second_gain_ref[...].astype(F32))
        dsum[rows, :] = value
        value = value.astype(BF)
        low[rows, :] = value
        value = value.astype(F32)
        add_row(9, value)
        low_t[:, rows] = jnp.transpose(value, (1, 0)).astype(BF)
        return carry

    lax.fori_loop(0, steps, second_back, 0)

    def to_near(number, unit, which):
        return remote(
            near_out.at[unit % 2, which],
            near_in.at[number, unit, which],
            near_send.at[unit % 2, which],
            near_recv.at[number, unit, which],
            near,
        )

    def to_far(number, unit):
        return remote(
            near_in.at[number, unit, 1],
            far_in.at[number, unit],
            far_send.at[number, unit],
            far_recv.at[number, unit],
            far,
        )

    factor = (depth - data) * (depth - data) * (depth - data) % (depth + 1)

    def owner(unit):
        return (factor * (unit + 1)) % (depth + 1) - 1

    def rightward(number, block, slot):
        return remote(
            near_in.at[number, slot, 0],
            depth_in.at[number, block],
            depth_send.at[number, slot],
            depth_recv.at[number, block],
            right,
        )

    def leftward(number, block, slot, landing):
        return remote(
            near_in.at[number, slot, 0],
            depth_in.at[number, landing],
            depth_send.at[number, slot],
            depth_recv.at[number, landing],
            left,
        )

    def gradient(number, unit, rank):
        at = owner(unit) if inner else unit
        rows = pl.ds(pl.multiple_of(at * share, share), share)
        if number == 0:
            return nn(low_t[rows, :], act[rank])
        if number == 1:
            return nn(first_t[rows, :], slope[rank])
        main = nt(first_t[rows, :], p[rank])
        edge = (3 * part // 256) * 256
        tail = nt(low_t[rows, :], p[rank, edge : 4 * part, :])
        lane = lax.broadcasted_iota(jnp.int32, tail.shape, 1)
        tail = jnp.where(lane < 3 * part - edge, main[:, edge:], tail)
        return jnp.concatenate([main[:, :edge], tail], axis=1)

    def reduce_stage(number):
        def body(index, carry):
            @pl.when(index < units)
            def _():
                for which, rank in ((1, 3), (0, 1)):

                    @pl.when((index >= 2) | (number > 0))
                    def _():
                        to_near(number, index, which).wait_send()

                    near_out[index % 2, which] = gradient(number, index, rank).astype(BF)
                    to_near(number, index, which).start()

            @pl.when(index > 0)
            def _():
                unit = index - 1
                for which, rank in ((1, 2), (0, 0)):
                    mine = gradient(number, unit, rank)
                    to_near(number, unit, which).wait_recv()
                    near_in[number, unit, which] = (
                        mine + near_in[number, unit, which].astype(F32)
                    ).astype(BF)
                    if which == 1 and number == 0:

                        @pl.when(unit < 2)
                        def _():
                            to_far(number, unit).start()

            return carry

        lax.fori_loop(0, units + 1, body, 0)

    def finish(index):
        number = index // units
        unit = index % units
        to_far(number, unit).wait_recv()
        near_in[number, unit, 0] = (
            near_in[number, unit, 0].astype(F32) + far_in[number, unit].astype(F32)
        ).astype(BF)
        if inner:
            block = owner(unit)

            @pl.when(((block > data) & (data > 0)) | ((block < data) & (data < depth - 1)))
            def _():
                rightward(number, block, unit).wait_recv()
                near_in[number, unit, 0] = (
                    near_in[number, unit, 0].astype(F32) + depth_in[number, block].astype(F32)
                ).astype(BF)

            @pl.when(block > data)
            def _():
                rightward(number, block, unit).start()

            @pl.when(block < data)
            def _():
                landing = block + (depth - block) * ((block + 1) // data)
                leftward(number, block, unit, landing).start()

        @pl.when(index + 2 < 3 * units)
        def _():
            to_far((index + 2) // units, (index + 2) % units).start()


    @pl.when(section == 0)
    def _():
        arrived(4)
        reduce_stage(0)

    @pl.when(section != 0)
    def _():
        later_y.start()

    arrived(1)
    block = 256
    blocks = wu.shape[2] // block

    def narrow(index, carry):
        rank = index // blocks
        columns = pl.ds(pl.multiple_of((index % blocks) * block, block), block)
        value = nt(low[...], wd[rank, columns, :]) * slope[rank, :, columns].astype(F32)
        value = value.astype(BF)
        slope[rank, :, columns] = value
        vec[0, pl.ds(rank, 1), columns] = jnp.sum(value.astype(F32), axis=0, keepdims=True)
        return carry

    lax.fori_loop(0, ranks * blocks, narrow, 0)

    @pl.when(section == 0)
    def _():
        finish(0)

    arrived(2)

    def first_transpose(step, carry):
        rows = pl.ds(pl.multiple_of(step * STEP, STEP), STEP)
        value = n1[rows, :].astype(F32) * first_gain_ref[...].astype(F32)
        value = value + first_shift_ref[...].astype(F32)
        first_t[:, rows] = jnp.transpose(value, (1, 0)).astype(BF)
        return carry

    def up_gradients():
        lax.fori_loop(0, steps, first_transpose, 0)
        reduce_stage(1)

    @pl.when(section == 0)
    def _():
        up_gradients()
        finish(1)

    def first_back(step, carry):
        rows = pl.ds(pl.multiple_of(step * STEP, STEP), STEP)
        arriving = dsum[rows, :]
        for rank in range(ranks):
            arriving = arriving + nt(slope[rank, rows, :], wu[rank])
        normal = n1[rows, :].astype(F32)
        add_row(10, arriving * normal)
        add_row(11, arriving)
        value = norm_back(arriving, normal, rs1[rows, 0:1], first_gain_ref[...].astype(F32))
        dsum[rows, :] = value
        value = value.astype(BF)
        low[rows, :] = value
        add_row(8, value.astype(F32))
        return carry

    lax.fori_loop(0, steps, first_back, 0)

    @pl.when(section == 0)
    def _():
        finish(2)

    @pl.when(section != 0)
    def _():
        later_y.wait()
        pl.semaphore_wait(barrier, len(partners))
        share_outputs(g)

    arrived(3)

    def context_back(rank, carry):
        dcontext[rank] = nt(wa[rank, 3 * part : 4 * part, :], low[...]).astype(BF)
        return carry

    lax.fori_loop(0, ranks, context_back, 0)
    here = length_ref[tensor // sequences, tensor % sequences]
    visible = lax.broadcasted_iota(jnp.int32, (length, length), 0) < here

    def attend_back(head, carry):
        rank = head // heads
        base = (head % heads) * HD
        at_query = pl.ds(pl.multiple_of(base, HD), HD)
        at_keys = pl.ds(pl.multiple_of(part + base, HD), HD)
        at_values = pl.ds(pl.multiple_of(2 * part + base, HD), HD)
        query = (p[rank, at_query, :].astype(F32) * HD ** (-0.5)).astype(BF)
        keys = p[rank, at_keys, :]
        values = p[rank, at_values, :]
        dout = dcontext[rank, at_query, :]
        weights = jnp.where(visible, jnp.exp(tn(keys, query) - lse[head]), 0.0)
        dweights = tn(values, dout)
        inner_sum = jnp.sum(weights * dweights, axis=0, keepdims=True)
        dscores = (weights * (dweights - inner_sum)).astype(BF)
        p[rank, at_query, :] = (nn(keys, dscores) * HD ** (-0.5)).astype(BF)
        p[rank, at_keys, :] = nt(query, dscores).astype(BF)
        p[rank, at_values, :] = nt(dout, weights.astype(BF)).astype(BF)

        @pl.when((section == 0) & (head % 5 == 4))
        def _():
            finish(3 + head // 5)

        return carry

    lax.fori_loop(0, ranks * heads, attend_back, 0)
    early = 3 + ranks * heads // 5 + 1
    for rank in range(ranks):
        vec[0, 4 + rank : 5 + rank, :] = nt(jnp.ones((8, length), BF), p[rank])[0:1, :]

    @pl.when(section != 0)
    def _():
        arrived(4)

    vec_near = remote(vec.at[0], vec_in.at[0], vec_send.at[0], vec_recv.at[0], near)
    vec_near.start()

    def entering_back(step, carry):
        rows = pl.ds(pl.multiple_of(step * STEP, STEP), STEP)
        total = dsum[rows, :]
        for rank in range(ranks):
            total = total + tn(p[rank, 0 : 3 * part, rows], wa[rank, 0 : 3 * part, :])
        dx[rows, :] = total.astype(BF)

        @pl.when(section != 0)
        def _():
            relay(step).start()

        return carry

    lax.fori_loop(0, steps, entering_back, 0)
    vec_near.wait_recv()

    def join(level, swap):
        for row in range(vec.shape[1]):
            pair = row ^ swap if row < 8 else row
            vec[level + 1, row : row + 1, :] = (
                vec[level, row : row + 1, :] + vec_in[level, pair : pair + 1, :]
            )

    join(0, 1)
    vec_far = remote(vec.at[1], vec_in.at[1], vec_send.at[1], vec_recv.at[1], far)
    vec_far.start()
    turn(dx, dx_t)
    for copy in dx_copies:
        copy.start()
    dx_in[tensor] = dx_t[tensor]

    @pl.when(section == 0)
    def _():
        finish(early - 1)

    @pl.when(section != 0)
    def _():
        reduce_stage(0)
        up_gradients()
        finish(0)

    def entering_transpose(step, carry):
        rows = pl.ds(pl.multiple_of(step * STEP, STEP), STEP)
        first_t[:, rows] = jnp.transpose(xb[rows, :].astype(F32), (1, 0)).astype(BF)
        low_t[:, rows] = jnp.transpose(low[rows, :].astype(F32), (1, 0)).astype(BF)
        return carry

    lax.fori_loop(0, steps, entering_transpose, 0)
    reduce_stage(2)

    vec_far.wait_recv()
    join(1, 2)
    vec_deep = [
        remote(vec.at[2], vec_in.at[2 + hop], vec_send.at[2 + hop], vec_recv.at[2 + hop], device)
        for hop, device in enumerate(deep)
    ]
    for copy in vec_deep:
        copy.start()

    @pl.when(section != 0)
    def _():
        lax.fori_loop(1, early, lambda index, carry: (finish(index), carry)[1], 0)

    lax.fori_loop(early, 2 * units, lambda index, carry: (finish(index), carry)[1], 0)
    for copy in dx_copies:
        copy.wait_recv()
    dx_done = pltpu.make_async_copy(dx_in, dx_out, out_sem.at[1])
    dx_done.start()
    half = table.shape[0]
    table_x = remote(table_away, table, table_send.at[0], table_recv.at[0], other)
    table_deep = [
        remote(table, table_in.at[hop], table_send.at[1 + hop], table_recv.at[1 + hop], device)
        for hop, device in enumerate(deep)
    ]

    @pl.when(section == 0)
    def _():
        types_each = table_out.shape[0]
        table_sum[...] = jnp.zeros_like(table_sum)

        def count(number, carry):
            row = lax.broadcasted_iota(jnp.int32, (2 * half, length), 0)
            picks = jnp.zeros((2 * half, length), F32)
            micro, item = number // sequences, number % sequences
            offset = 0
            for ids_ref, number_of in (
                (segment_ref, 2),
                (column_ref, COLS),
                (row_ref, ROWS),
                (answer_ref, 2),
            ):
                ids = ids_ref[micro, pl.ds(item, 1), :] + offset
                ids = ids + jnp.where(ids >= types_each, half - types_each, 0)
                picks = picks + jnp.where(ids == row, 1.0, 0.0)
                offset += number_of
            table_sum[...] += nt(picks.astype(BF), dx_in[number])
            return carry

        lax.fori_loop(0, ranks, count, 0)
        table[...] = table_sum[:half].astype(BF)
        table_away[...] = table_sum[half:].astype(BF)
        table_x.start()
        for copy in table_deep:
            copy.start()

    lax.fori_loop(2 * units, 3 * units - 1, lambda index, carry: (finish(index), carry)[1], 0)

    @pl.when(section != 0)
    def _():
        table_x.wait_recv()
        for copy in table_deep:
            copy.start()

    finish(3 * units - 1)
    copies = []
    if inner:
        for number in range(3):
            total = jnp.zeros(final.shape[1:], F32)
            for unit in range(units):
                keep = jnp.where(owner(unit) == data, 1.0, 0.0)
                total = total + near_in[number, unit, 0].astype(F32) * keep
            final[number] = total

            @pl.when(data > 0)
            def _():
                rightward(number, data, 0).wait_recv()
                final[number] = final[number] + depth_in[number, data].astype(F32)

            @pl.when(data < depth - 1)
            def _():
                leftward(number, data, 0, depth).wait_recv()
                final[number] = final[number] + depth_in[number, depth].astype(F32)

            copy = pltpu.make_async_copy(
                final.at[number], sums_out.at[number], out_sem.at[2 + number]
            )
            copy.start()
            copies.append(copy)
    else:
        copy = pltpu.make_async_copy(
            near_in.at[:, :, 0], sums_out, out_sem.at[2]
        )
        copy.start()
        copies.append(copy)
    total = vec[2]
    for hop, copy in enumerate(vec_deep):
        copy.wait_recv()
        total = total + vec_in[2 + hop]
    vec_out[...] = total
    total = table[...].astype(F32)
    for hop, copy in enumerate(table_deep):
        copy.wait_recv()
        total = total + table_in[hop].astype(F32)
    table_out[...] = total[: table_out.shape[0]]

    for copy in y_copies:
        copy.wait()
    y_own.wait()
    for copy in dx_copies:
        copy.wait_send()
    vec_near.wait_send()
    vec_far.wait_send()
    for copy in vec_deep + table_deep:
        copy.wait_send()
    for unit in range(2):
        for which in range(2):
            to_near(2, unit, which).wait_send()
    for number in range(3):
        for unit in range(units):
            to_far(number, unit).wait_send()
            if inner:

                @pl.when(owner(unit) != data)
                def _():
                    rightward(number, 0, unit).wait_send()

    @pl.when(section != 0)
    def _():
        for step in range(steps):
            relay(step).wait_send()

    @pl.when(section == 0)
    def _():
        table_x.wait_send()

    dx_done.wait()
    for copy in copies:
        copy.wait()


def backward(cotangent, saved, lengths, vectors, ids, type_half, inner):
    wa, wu, wd, p, lse, act, slope, n1, n2, rs1, rs2, x, y = saved
    ranks = wa.shape[0]
    length, width = x.shape
    steps = length // STEP
    depth = lax.axis_size("dp")
    units = depth if inner else 4
    hops = depth - 1 if inner else 0
    share = width // units
    anywhere = pl.BlockSpec(memory_space=pl.ANY)
    inside = pl.BlockSpec(memory_space=pltpu.VMEM)
    part = wa.shape[1] // 4
    each = width // ranks
    half = -(-type_half // 16) * 16

    def like(value):
        return pltpu.VMEM(value.shape, value.dtype)

    plane = (length, width)
    turned = (width, length)
    chunk = (share, width)
    spread = (ranks, each, length)
    semaphores = pltpu.SemaphoreType.DMA
    sums = ((3,) + chunk, F32) if inner else ((3, units) + chunk, BF)
    return pl.pallas_call(
        functools.partial(backward_kernel, inner),
        name="backward_layer",
        out_shape=(
            jax.ShapeDtypeStruct(*sums),
            jax.ShapeDtypeStruct(spread, BF),
            jax.ShapeDtypeStruct(spread, BF),
            jax.ShapeDtypeStruct((16, width), F32),
            jax.ShapeDtypeStruct((type_half, each), F32),
        ),
        in_specs=[anywhere] * 14
        + [pl.BlockSpec(memory_space=pltpu.SMEM)]
        + [inside] * (len(vectors) + len(ids)),
        out_specs=(anywhere, anywhere, anywhere, inside, inside),
        scratch_shapes=[like(value) for value in saved[:-1]]
        + [
            pltpu.VMEM(plane, BF),
            pltpu.VMEM(plane, F32),
            pltpu.VMEM(plane, BF),
            pltpu.VMEM(turned, BF),
            pltpu.VMEM(turned, BF),
            pltpu.VMEM((ranks, part, length), BF),
            pltpu.VMEM(plane, BF),
            pltpu.VMEM(spread, BF),
            pltpu.VMEM(spread, BF),
            pltpu.VMEM(spread, BF),
            pltpu.VMEM((2, 2) + chunk, BF),
            pltpu.VMEM((3, units, 2) + chunk, BF),
            pltpu.VMEM((3, units) + chunk, BF),
            pltpu.VMEM((3, units + 1) + (chunk if inner else (16, 128)), BF),
            pltpu.VMEM((3,) + (chunk if inner else (16, 128)), F32),
            pltpu.VMEM((3, 16, width), F32),
            pltpu.VMEM((2 + hops, 16, width), F32),
            pltpu.VMEM((half, each), BF),
            pltpu.VMEM((half, each), BF),
            pltpu.VMEM((max(hops, 1), half, each), BF),
            pltpu.VMEM((2 * half, each), F32),
            semaphores((15,)),
            semaphores((2, 2)),
            semaphores((3, units, 2)),
            semaphores((3, units)),
            semaphores((3, units)),
            semaphores((3, units)),
            semaphores((3, units + 1)),
            semaphores((steps,)),
            semaphores((steps,)),
            semaphores((3,)),
            semaphores((3,)),
            semaphores((3,)),
            semaphores((3,)),
            semaphores((2 + hops,)),
            semaphores((2 + hops,)),
            semaphores((1 + hops,)),
            semaphores((1 + hops,)),
            semaphores((5,)),
        ],
        compiler_params=pltpu.CompilerParams(
            collective_id=1, has_side_effects=True, vmem_limit_bytes=VMEM_LIMIT
        ),
        cost_estimate=pl.CostEstimate(
            flops=17_000_000_000, bytes_accessed=60_000_000, transcendentals=3_000_000
        ),
    )(cotangent, *saved, lengths, *vectors, *ids)


def on_device(
    inputs,
    cotangent,
    segment_ids,
    column_ids,
    row_ids,
    answer_ids,
    lengths,
    type_table,
    query_weight,
    query_bias,
    key_weight,
    value_weight,
    value_bias,
    output_weight,
    output_bias,
    first_gain,
    first_shift,
    up_weight,
    up_bias,
    down_weight,
    down_bias,
    second_gain,
    second_shift,
):
    tensor = lax.axis_index("tensor")
    ranks = lax.axis_size("tensor")
    micro_count, sequences, length, width = inputs.shape
    type_count = 4 + COLS + ROWS
    part = query_weight.shape[2]
    hidden = up_weight.shape[2]

    ids = (segment_ids, column_ids, row_ids, answer_ids)
    wa = jnp.concatenate(
        [query_weight[0].T, key_weight[0].T, value_weight[0].T, output_weight[0]], axis=0
    )
    vectors = (
        query_bias,
        value_bias,
        up_bias,
        output_bias,
        first_gain,
        first_shift,
        down_bias,
        second_gain,
        second_shift,
    )
    saved = forward(
        inputs, ids, type_table, lengths, wa, up_weight[0], down_weight[0], vectors, ranks
    )
    depth = lax.axis_size("dp")
    inner = depth == 4 and width % (16 * depth) == 0
    type_half = type_count // lax.axis_size("section")
    sums, dx, leaving, vecs, table_grad = backward(
        cotangent, saved, lengths, (first_gain, first_shift, second_gain), ids, type_half, inner
    )

    def in_columns(value):
        return jnp.swapaxes(value, 1, 2).reshape(
            1, micro_count, sequences, length, width // ranks
        )

    layer_outputs = in_columns(leaving)
    layer_input_grads = in_columns(dx).astype(F32)
    if inner:
        summed = sums
    else:
        summed = lax.psum_scatter(
            sums.reshape(3, width, width), "dp", scatter_dimension=1, tiled=True
        ).astype(F32)
        vecs = lax.psum(vecs, "dp")
        table_grad = lax.psum(table_grad.astype(BF), "dp").astype(F32)
    mine = lax.dynamic_slice_in_dim(
        vecs[8:14].reshape(6, ranks, width // ranks), tensor, 1, 1
    ).reshape(1, 6 * (width // ranks))
    mine = jnp.concatenate([vecs[0:1], vecs[4:5], mine], axis=1)

    def vector(start, count):
        return mine[:, start : start + count]

    share = width // ranks
    after = 2 * width
    return (
        layer_outputs,
        layer_input_grads,
        summed[2, :, 0:part][None],
        vector(width, part),
        summed[2, :, part : 2 * part][None],
        summed[2, :, 2 * part : 3 * part][None],
        vector(width + 2 * part, part),
        summed[2, :, 3 * part : 4 * part].T[None],
        vector(after, share),
        vector(after + 2 * share, share),
        vector(after + 3 * share, share),
        summed[1][None],
        vector(0, hidden),
        summed[0].T[None],
        vector(after + share, share),
        vector(after + 4 * share, share),
        vector(after + 5 * share, share),
        table_grad,
    )


def solution(mesh):
    return jax.shard_map(
        on_device,
        mesh=mesh,
        in_specs=(
            P(None, "dp", None, None),
            P(None, "dp", None, None),
            P(None, "dp", None),
            P(None, "dp", None),
            P(None, "dp", None),
            P(None, "dp", None),
            P(None, "dp"),
            P(),
            P("section", None, "tensor"),
            P("section", "tensor"),
            P("section", None, "tensor"),
            P("section", None, "tensor"),
            P("section", "tensor"),
            P("section", "tensor", None),
            P("section", None),
            P("section", None),
            P("section", None),
            P("section", None, "tensor"),
            P("section", "tensor"),
            P("section", "tensor", None),
            P("section", None),
            P("section", None),
            P("section", None),
        ),
        out_specs=(
            P("section", None, "dp", None, "tensor"),
            P("section", None, "dp", None, "tensor"),
            P("section", "dp", "tensor"),
            P("section", "tensor"),
            P("section", "dp", "tensor"),
            P("section", "dp", "tensor"),
            P("section", "tensor"),
            P("section", "tensor", "dp"),
            P("section", "tensor"),
            P("section", "tensor"),
            P("section", "tensor"),
            P("section", "dp", "tensor"),
            P("section", "tensor"),
            P("section", "tensor", "dp"),
            P("section", "tensor"),
            P("section", "tensor"),
            P("section", "tensor"),
            P("section", "tensor"),
        ),
        check_vma=False,
    )
```

```python
import functools

import jax
import jax.numpy as jnp
from jax import lax
from jax.experimental import pallas as pl
from jax.experimental.pallas import tpu as pltpu
from jax.sharding import PartitionSpec as P

HD = 64
COLS = 256
ROWS = 256
EPSILON = 1e-12
MASKED = -1e30
BF = jnp.bfloat16
F32 = jnp.float32
MESH = pl.DeviceIdType.MESH
VMEM_LIMIT = 60 * 1024 * 1024
STEP = 256
SHARES = (5, 5, 5)
OUTS = ("wa", "wu", "wd", "p", "lse", "act", "slope", "n1", "n2", "rs1", "rs2", "x", "y")


def nn(left, right):
    return lax.dot_general(left, right, (((1,), (0,)), ((), ())), preferred_element_type=F32)


def nt(left, right):
    return lax.dot_general(left, right, (((1,), (1,)), ((), ())), preferred_element_type=F32)


def tn(left, right):
    return lax.dot_general(left, right, (((0,), (0,)), ((), ())), preferred_element_type=F32)


def normalize(value):
    centered = value - jnp.mean(value, axis=-1, keepdims=True)
    variance = jnp.mean(centered * centered, axis=-1, keepdims=True)
    scale = lax.rsqrt(variance + EPSILON)
    return centered * scale, scale


def place():
    section = lax.axis_index("section")
    data = lax.axis_index("dp")
    tensor = lax.axis_index("tensor")
    beside = tensor + 1 - 2 * (tensor % 2)
    across = tensor + 2 - 4 * ((tensor // 2) % 2)
    return section, data, tensor, beside, across


def greet(partners):
    barrier = pltpu.get_barrier_semaphore()
    for partner in partners:
        pl.semaphore_signal(barrier, inc=1, device_id=partner, device_id_type=MESH)
    pl.semaphore_wait(barrier, len(partners))


def remote(src, dst, send, recv, device):
    return pltpu.make_async_remote_copy(
        src_ref=src, dst_ref=dst, send_sem=send, recv_sem=recv, device_id=device, device_id_type=MESH
    )


def forward_kernel(
    inputs_ref,
    segment_ref,
    column_ref,
    row_ref,
    answer_ref,
    table_ref,
    length_ref,
    wa_ref,
    wu_ref,
    wd_ref,
    query_bias_ref,
    value_bias_ref,
    up_bias_ref,
    output_bias_ref,
    first_gain_ref,
    first_shift_ref,
    down_bias_ref,
    second_gain_ref,
    second_shift_ref,
    wa_out,
    wu_out,
    wd_out,
    p_out,
    lse_out,
    act_out,
    slope_out,
    n1_out,
    n2_out,
    rs1_out,
    rs2_out,
    x_out,
    y_out,
    wa,
    wu,
    wd,
    bias,
    table,
    p,
    lse,
    act,
    slope,
    xf,
    xb,
    first,
    low,
    n1,
    n2,
    rs1,
    rs2,
    y,
    gather_send,
    gather_recv,
    chain_send,
    chain_recv,
    relay_send,
    relay_recv,
    local_sem,
    out_sem,
    turn_sem,
):
    section, data, tensor, beside, across = place()
    length, width = xf.shape
    ranks = wa.shape[0]
    heads = wa.shape[1] // (4 * HD)
    part = heads * HD
    steps = length // STEP
    sequences = inputs_ref.shape[1]
    near = (section, data, beside)
    far = (section, data, across)
    other = (1 - section, data, tensor)
    depth = lax.axis_size("dp")
    group = 4 if depth % 4 == 0 else 1
    spot = data % group
    before = (section, data - spot + (spot + group - 1) % group, tensor)
    after = (section, data - spot + (spot + 1) % group, tensor)
    greet([near, far, other] + ([before, after] if group > 1 else []))

    shards = ((wa_ref, wa), (wu_ref, wu), (wd_ref, wd))
    direct = [wa.shape[1] * count // 12 for count in SHARES]
    piece = [(wa.shape[1] - count) // group for count in direct]

    def rows_of(number, part_at):
        start = direct[number] + part_at * piece[number]
        return pl.ds(pl.multiple_of(start, 16), piece[number])

    to_far = []
    to_near = []
    onward = []
    own = []
    for number, (source, target) in enumerate(shards):
        to_far.append(
            [
                remote(
                    source.at[rows],
                    target.at[2, rows],
                    gather_send.at[number, which],
                    gather_recv.at[number, which],
                    far,
                )
                for which, rows in enumerate((rows_of(number, spot), pl.ds(0, direct[number])))
            ]
        )
        to_near.append(
            remote(source, target.at[1], gather_send.at[number, 2], gather_recv.at[number, 2], near)
        )
        rest = wa.shape[1] - direct[number]
        onward.append(
            [
                remote(
                    target.at[2, rows],
                    target.at[3, rows],
                    gather_send.at[number, 3 + which],
                    gather_recv.at[number, 3 + which],
                    near,
                )
                for which, rows in enumerate(
                    (pl.ds(0, direct[number]), pl.ds(direct[number], rest))
                )
            ]
        )
        own.append(pltpu.make_async_copy(source, target.at[0], local_sem.at[number]))
    to_far[0][0].start()
    for copy in to_near:
        copy.start()
    for copy in own:
        copy.start()
    bias[0] = jnp.zeros(bias.shape[1:], F32)
    bias[0, 0:1, :] = up_bias_ref[...].astype(F32)
    bias[0, 1:2, 0:part] = query_bias_ref[...].astype(F32)
    bias[0, 1:2, 2 * part : 3 * part] = value_bias_ref[...].astype(F32)
    bias_copies = [
        remote(bias.at[0], bias.at[1 + which], gather_send.at[3, which], gather_recv.at[3, which], to)
        for which, to in enumerate((near, far))
    ]
    bias_onward = remote(bias.at[2], bias.at[3], gather_send.at[3, 2], gather_recv.at[3, 2], near)
    for copy in bias_copies:
        copy.start()

    def chain(number, hop, up):
        rows = rows_of(number, spot - (hop - 1) if up else spot + (hop - 1))
        target = shards[number][1]
        at = 0 if up else 1
        return remote(
            target.at[2, rows],
            target.at[2, rows],
            chain_send.at[number, at, hop - 1],
            chain_recv.at[number, at, hop - 1],
            after if up else before,
        )

    def chained(number, hop, up):
        rows = rows_of(number, spot - hop if up else spot + hop)
        target = shards[number][1]
        at = 0 if up else 1
        return remote(
            target.at[2, rows],
            target.at[2, rows],
            chain_send.at[number, at, hop - 1],
            chain_recv.at[number, at, hop - 1],
            before if up else after,
        )

    def piece_in(number):
        to_far[number][0].wait_recv()

    def send_piece(number):
        to_far[number][0].start()

    def send_direct(number):
        to_far[number][1].start()

    def hand_on(number, hop):
        if group == 1 or hop == group:
            return
        if hop > 0:

            @pl.when(spot >= hop)
            def _():
                chained(number, hop, True).wait_recv()

            @pl.when(spot + hop < group)
            def _():
                chained(number, hop, False).wait_recv()

        if hop + 1 < group:

            @pl.when((spot >= hop) & (spot + 1 < group))
            def _():
                chain(number, hop + 1, True).start()

            @pl.when((spot + hop < group) & (spot >= 1))
            def _():
                chain(number, hop + 1, False).start()

    def direct_in(number):
        to_far[number][1].wait_recv()
        onward[number][0].start()

    def pass_on(number):
        onward[number][1].start()

    def ready(number):
        own[number].wait()
        to_near[number].wait_recv()
        for copy in onward[number]:
            copy.wait_recv()

    def at_first(actions):
        @pl.when(section == 0)
        def _():
            for action, *values in actions:
                action(*values)

    out_copies = []

    wu_copy = pltpu.make_async_copy(wu, wu_out, out_sem.at[len(OUTS)])
    wd_copy = pltpu.make_async_copy(wd, wd_out, out_sem.at[len(OUTS) + 1])

    def put_out(source, target):
        copy = pltpu.make_async_copy(source, target, out_sem.at[len(out_copies)])
        copy.start()
        out_copies.append(copy)

    relays = [
        remote(
            y.at[pl.ds(step * STEP, STEP)],
            xb.at[pl.ds(step * STEP, STEP)],
            relay_send.at[step],
            relay_recv.at[step],
            other,
        )
        for step in range(steps)
    ]

    load_input = pltpu.make_async_copy(
        inputs_ref.at[tensor // sequences, tensor % sequences], xb, local_sem.at[3]
    )

    @pl.when(section == 0)
    def _():
        load_input.start()

    piece_in(0)
    hand_on(0, 0)
    send_piece(1)
    send_direct(0)
    bias_copies[1].wait_recv()
    bias_onward.start()

    @pl.when(section == 0)
    def _():
        load_input.wait()
        types = table.shape[0]
        table[...] = jnp.zeros_like(table)
        table[0 : table_ref.shape[0], :] = table_ref[...]
        micro, item = tensor // sequences, tensor % sequences
        offset = 0
        row = lax.broadcasted_iota(jnp.int32, (types, length), 0)
        picks = jnp.zeros((types, length), F32)
        for ids_ref, count in (
            (segment_ref, 2),
            (column_ref, COLS),
            (row_ref, ROWS),
            (answer_ref, 2),
        ):
            ids = ids_ref[micro, pl.ds(item, 1), :] + offset
            picks = picks + jnp.where(ids == row, 1.0, 0.0)
            offset += count
        xf[...] = xb[...].astype(F32) + tn(picks.astype(BF), table[...])
        xb[...] = xf[...].astype(BF)

    hand_on(0, 1)
    hand_on(0, 2)
    piece_in(1)
    hand_on(1, 0)
    send_piece(2)
    direct_in(0)
    send_direct(1)
    hand_on(0, 3)
    pass_on(0)
    hand_on(1, 1)
    ready(0)
    put_out(wa, wa_out)

    @pl.when(section != 0)
    def _():
        piece_in(2)
        hand_on(2, 0)
        hand_on(1, 2)
        hand_on(2, 1)
        hand_on(1, 3)
        direct_in(1)
        pass_on(1)
        send_direct(2)
        hand_on(2, 2)
        hand_on(2, 3)
        direct_in(2)
        pass_on(2)
        ready(1)
        wu_copy.start()
        ready(2)
        wd_copy.start()
        for relay in relays:
            relay.wait_recv()
        xf[...] = xb[...].astype(F32)

    bias_copies[0].wait_recv()
    bias_onward.wait_recv()
    put_out(xb, x_out)

    def project(rank, carry):
        columns = jnp.transpose(bias[rank], (1, 0))
        p[rank, 0 : 3 * part, :] = (
            nt(wa[rank, 0 : 3 * part, :], xb[...]) + columns[0 : 3 * part, 1:2]
        ).astype(BF)
        return carry

    lax.fori_loop(0, ranks, project, 0)
    at_first([(piece_in, 2), (hand_on, 2, 0)])

    here = length_ref[tensor // sequences, tensor % sequences]
    visible = lax.broadcasted_iota(jnp.int32, (length, length), 0) < here

    def attend(head, carry):
        rank = head // heads
        base = (head % heads) * HD
        query = p[rank, pl.ds(pl.multiple_of(base, HD), HD), :]
        keys = p[rank, pl.ds(pl.multiple_of(part + base, HD), HD), :]
        values = p[rank, pl.ds(pl.multiple_of(2 * part + base, HD), HD), :]
        query = (query.astype(F32) * HD ** (-0.5)).astype(BF)
        scores = jnp.where(visible, tn(keys, query), MASKED)
        maximum = jnp.max(scores, axis=0, keepdims=True)
        raised = jnp.exp(scores - maximum)
        total = jnp.sum(raised, axis=0, keepdims=True)
        context = nn(values, raised.astype(BF)) / total
        p[rank, pl.ds(pl.multiple_of(3 * part + base, HD), HD), :] = context.astype(BF)
        lse[head] = maximum + jnp.log(total)
        for at, action in (
            (2, (hand_on, 1, 2)),
            (7, (hand_on, 2, 1)),
            (7, (direct_in, 1)),
            (7, (send_direct, 2)),
            (11, (hand_on, 1, 3)),
            (11, (pass_on, 1)),
        ):

            @pl.when((section == 0) & (head == at))
            def _():
                action[0](*action[1:])

        return carry

    lax.fori_loop(0, ranks * heads, attend, 0)
    put_out(p, p_out)
    put_out(lse, lse_out)

    def first_norm(step, carry):
        rows = pl.ds(pl.multiple_of(step * STEP, STEP), STEP)
        total = xf[rows, :] + output_bias_ref[...].astype(F32)
        for rank in range(ranks):
            total = total + tn(p[rank, 3 * part : 4 * part, rows], wa[rank, 3 * part : 4 * part, :])
        normal, scale = normalize(total)
        value = normal * first_gain_ref[...].astype(F32) + first_shift_ref[...].astype(F32)
        first[rows, :] = value
        low[rows, :] = value.astype(BF)
        n1[rows, :] = normal.astype(BF)
        rs1[rows, :] = jnp.broadcast_to(scale, (STEP, 128))
        return carry

    lax.fori_loop(0, steps, first_norm, 0)
    put_out(n1, n1_out)
    put_out(rs1, rs1_out)
    at_first([(hand_on, 2, 2), (ready, 1), (wu_copy.start,)])
    block = 256
    blocks = wu.shape[2] // block

    def widen(index, carry):
        rank = index // blocks
        columns = pl.ds(pl.multiple_of((index % blocks) * block, block), block)
        hidden = nn(low[...], wu[rank, :, columns]) + bias[rank, 0:1, columns]
        inner = 0.5 * (1.0 + lax.erf(hidden * (0.5**0.5)))
        act[rank, :, columns] = (hidden * inner).astype(BF)
        density = jnp.exp(hidden * hidden * (-0.5)) * 0.3989422804014327
        slope[rank, :, columns] = (inner + hidden * density).astype(BF)

        @pl.when((section == 0) & (index == ranks * blocks - 4))
        def _():
            direct_in(2)
            hand_on(2, 3)
            pass_on(2)

        return carry

    lax.fori_loop(0, ranks * blocks, widen, 0)
    put_out(act, act_out)
    put_out(slope, slope_out)
    at_first([(ready, 2), (wd_copy.start,)])

    for step in range(steps):
        rows = pl.ds(step * STEP, STEP)
        total = first[rows, :] + down_bias_ref[...].astype(F32)
        for rank in range(ranks):
            total = total + nn(act[rank, rows, :], wd[rank])
        normal, scale = normalize(total)
        y[rows, :] = (
            normal * second_gain_ref[...].astype(F32) + second_shift_ref[...].astype(F32)
        ).astype(BF)
        n2[rows, :] = normal.astype(BF)
        rs2[rows, :] = jnp.broadcast_to(scale, (STEP, 128))

        @pl.when((section == 0) & (tensor % 2 == 0))
        def _():
            relays[step].start()

    put_out(n2, n2_out)
    put_out(rs2, rs2_out)
    put_out(y, y_out)

    @pl.when((section == 0) & (tensor % 2 == 0))
    def _():
        for relay in relays:
            relay.wait_send()
        pl.semaphore_signal(turn_sem, inc=1, device_id=near, device_id_type=MESH)

    @pl.when((section == 0) & (tensor % 2 == 1))
    def _():
        pl.semaphore_wait(turn_sem, 1)
        for relay in relays:
            relay.start()
        for relay in relays:
            relay.wait_send()

    for copy in out_copies + [wu_copy, wd_copy]:
        copy.wait()
    for copies in to_far + onward + [to_near, bias_copies, [bias_onward]]:
        for copy in copies:
            copy.wait_send()
    for number in range(3):
        for hop in range(group - 1):

            @pl.when((spot >= hop) & (spot + 1 < group))
            def _():
                chain(number, hop + 1, True).wait_send()

            @pl.when((spot + hop < group) & (spot >= 1))
            def _():
                chain(number, hop + 1, False).wait_send()


def forward(inputs, ids, table, lengths, wa, wu, wd, vectors, ranks):
    length, width = inputs.shape[2], inputs.shape[3]
    rows_a = wa.shape[0]
    hidden = wu.shape[1]
    heads = ranks * (rows_a // (4 * HD))
    steps = length // STEP
    shapes = dict(
        wa=((ranks, rows_a, width), BF),
        wu=((ranks, width, hidden), BF),
        wd=((ranks, hidden, width), BF),
        p=((ranks, rows_a, length), BF),
        lse=((heads, 1, length), F32),
        act=((ranks, length, hidden), BF),
        slope=((ranks, length, hidden), BF),
        n1=((length, width), BF),
        n2=((length, width), BF),
        rs1=((length, 128), F32),
        rs2=((length, 128), F32),
        x=((length, width), BF),
        y=((length, width), BF),
    )

    def buffer(name):
        return pltpu.VMEM(*shapes[name])

    anywhere = pl.BlockSpec(memory_space=pl.ANY)
    inside = pl.BlockSpec(memory_space=pltpu.VMEM)
    return pl.pallas_call(
        forward_kernel,
        name="forward_layer",
        out_shape=tuple(jax.ShapeDtypeStruct(*shapes[name]) for name in OUTS),
        in_specs=[
            anywhere,
            inside,
            inside,
            inside,
            inside,
            inside,
            pl.BlockSpec(memory_space=pltpu.SMEM),
            anywhere,
            anywhere,
            anywhere,
        ]
        + [inside] * len(vectors),
        out_specs=tuple(anywhere for _ in OUTS),
        scratch_shapes=[
            buffer("wa"),
            buffer("wu"),
            buffer("wd"),
            pltpu.VMEM((ranks, 8, hidden), F32),
            pltpu.VMEM((-(-table.shape[0] // 16) * 16, width), BF),
            buffer("p"),
            buffer("lse"),
            buffer("act"),
            buffer("slope"),
            pltpu.VMEM((length, width), F32),
            buffer("x"),
            pltpu.VMEM((length, width), F32),
            pltpu.VMEM((length, width), BF),
            buffer("n1"),
            buffer("n2"),
            buffer("rs1"),
            buffer("rs2"),
            buffer("y"),
            pltpu.SemaphoreType.DMA((4, 5)),
            pltpu.SemaphoreType.DMA((4, 5)),
            pltpu.SemaphoreType.DMA((3, 2, 3)),
            pltpu.SemaphoreType.DMA((3, 2, 3)),
            pltpu.SemaphoreType.DMA((steps,)),
            pltpu.SemaphoreType.DMA((steps,)),
            pltpu.SemaphoreType.DMA((5,)),
            pltpu.SemaphoreType.DMA((len(OUTS) + 2,)),
            pltpu.SemaphoreType.REGULAR,
        ],
        compiler_params=pltpu.CompilerParams(
            collective_id=0, has_side_effects=True, vmem_limit_bytes=VMEM_LIMIT
        ),
        cost_estimate=pl.CostEstimate(
            flops=8_000_000_000, bytes_accessed=60_000_000, transcendentals=6_000_000
        ),
    )(inputs, *ids, table, lengths, wa, wu, wd, *vectors)


def backward_kernel(
    inner,
    cotangent_ref,
    wa_ref,
    wu_ref,
    wd_ref,
    p_ref,
    lse_ref,
    act_ref,
    slope_ref,
    n1_ref,
    n2_ref,
    rs1_ref,
    rs2_ref,
    x_ref,
    y_ref,
    length_ref,
    first_gain_ref,
    first_shift_ref,
    second_gain_ref,
    segment_ref,
    column_ref,
    row_ref,
    answer_ref,
    sums_out,
    dx_out,
    y_out,
    vec_out,
    table_out,
    wa,
    wu,
    wd,
    p,
    lse,
    act,
    slope,
    n1,
    n2,
    rs1,
    rs2,
    xb,
    g,
    dsum,
    low,
    low_t,
    first_t,
    dcontext,
    dx,
    dx_t,
    dx_in,
    y_t,
    near_out,
    near_in,
    far_in,
    depth_in,
    final,
    vec,
    vec_in,
    table,
    table_away,
    table_in,
    table_sum,
    load_sem,
    near_send,
    near_recv,
    far_send,
    far_recv,
    depth_send,
    depth_recv,
    relay_send,
    relay_recv,
    dx_send,
    dx_recv,
    y_send,
    y_recv,
    vec_send,
    vec_recv,
    table_send,
    table_recv,
    out_sem,
):
    section, data, tensor, beside, across = place()
    diagonal = beside + 2 - 4 * ((beside // 2) % 2)
    length, width = g.shape
    ranks = wa.shape[0]
    heads = wa.shape[1] // (4 * HD)
    part = heads * HD
    steps = length // STEP
    sequences = cotangent_ref.shape[1]
    units = near_in.shape[1]
    share = near_in.shape[3]
    columns_each = width // ranks
    depth = lax.axis_size("dp")
    near = (section, data, beside)
    far = (section, data, across)
    corner = (section, data, diagonal)
    other = (1 - section, data, tensor)
    deep = []
    left = right = None
    if inner:
        deep = [(section, (data + 1 + hop) % depth, tensor) for hop in range(depth - 1)]
        left = (section, (data + depth - 1) % depth, tensor)
        right = (section, (data + 1) % depth, tensor)
    partners = [near, far, corner, other] + deep
    barrier = pltpu.get_barrier_semaphore()
    for partner in partners:
        pl.semaphore_signal(barrier, inc=1, device_id=partner, device_id_type=MESH)

    @pl.when(section == 0)
    def _():
        pl.semaphore_wait(barrier, len(partners))

    loads = {}
    for name, source, target in (
        ("n2", n2_ref, n2),
        ("rs2", rs2_ref, rs2),
        ("wd", wd_ref, wd),
        ("slope", slope_ref, slope),
        ("wu", wu_ref, wu),
        ("act", act_ref, act),
        ("n1", n1_ref, n1),
        ("rs1", rs1_ref, rs1),
        ("wa", wa_ref, wa),
        ("p", p_ref, p),
        ("lse", lse_ref, lse),
        ("xb", x_ref, xb),
    ):
        loads[name] = pltpu.make_async_copy(source, target, load_sem.at[len(loads)])
    start_g = pltpu.make_async_copy(
        cotangent_ref.at[tensor // sequences, tensor % sequences], g, load_sem.at[len(loads)]
    )
    first_y = pltpu.make_async_copy(y_ref, dx, load_sem.at[len(loads) + 1])
    later_y = pltpu.make_async_copy(y_ref, g, load_sem.at[len(loads) + 1])
    waves = (("n2", "rs2"), ("wd", "slope"), ("wu", "n1", "rs1"), ("wa", "p", "lse"), ("act", "xb"))

    def begin(wave):
        for name in waves[wave]:
            loads[name].start()

    def arrived(wave):
        for name in waves[wave]:
            loads[name].wait()
        if wave + 1 < len(waves):

            @pl.when(section != 0)
            def _():
                begin(wave + 1)


    def relay(step):
        rows = pl.ds(pl.multiple_of(step * STEP, STEP), STEP)
        return remote(dx.at[rows], g.at[rows], relay_send.at[step], relay_recv.at[step], other)

    around = ((beside, near), (across, far), (diagonal, corner))
    y_copies = [
        remote(y_t.at[rank], y_out.at[tensor], y_send.at[number], y_recv.at[number], device)
        for number, (rank, device) in enumerate(around)
    ]
    y_own = pltpu.make_async_copy(y_t.at[tensor], y_out.at[tensor], out_sem.at[0])
    dx_copies = [
        remote(dx_t.at[rank], dx_in.at[tensor], dx_send.at[number], dx_recv.at[number], device)
        for number, (rank, device) in enumerate(around)
    ]

    def turn(source, target):
        def body(step, carry):
            rows = pl.ds(pl.multiple_of(step * STEP, STEP), STEP)
            value = jnp.transpose(source[rows, :].astype(F32), (1, 0)).astype(BF)
            for rank in range(ranks):
                target[rank, :, rows] = value[rank * columns_each : (rank + 1) * columns_each]
            return carry

        lax.fori_loop(0, steps, body, 0)

    def share_outputs(source):
        turn(source, y_t)
        for copy in y_copies:
            copy.start()
        y_own.start()

    begin(0)
    vec[0] = jnp.zeros(vec.shape[1:], F32)

    @pl.when(section == 0)
    def _():
        first_y.start()
        for wave in range(1, len(waves)):
            begin(wave)
        first_y.wait()
        share_outputs(dx)

    @pl.when(section != 0)
    def _():
        start_g.start()
        start_g.wait()

    arrived(0)

    def add_row(row, value):
        vec[0, row : row + 1, :] += jnp.sum(value, axis=0, keepdims=True)

    def norm_back(arriving, normal, scale, gain):
        scaled = arriving * gain
        return (
            scaled
            - jnp.mean(scaled, axis=-1, keepdims=True)
            - normal * jnp.mean(scaled * normal, axis=-1, keepdims=True)
        ) * scale

    def second_back(step, carry):
        rows = pl.ds(pl.multiple_of(step * STEP, STEP), STEP)

        @pl.when(section == 0)
        def _():
            relay(step).wait_recv()

        arriving = g[rows, :].astype(F32)
        normal = n2[rows, :].astype(F32)
        add_row(12, arriving * normal)
        add_row(13, arriving)
        value = norm_back(arriving, normal, rs2[rows, 0:1], second_gain_ref[...].astype(F32))
        dsum[rows, :] = value
        value = value.astype(BF)
        low[rows, :] = value
        value = value.astype(F32)
        add_row(9, value)
        low_t[:, rows] = jnp.transpose(value, (1, 0)).astype(BF)
        return carry

    lax.fori_loop(0, steps, second_back, 0)

    def to_near(number, unit, which):
        return remote(
            near_out.at[unit % 2, which],
            near_in.at[number, unit, which],
            near_send.at[unit % 2, which],
            near_recv.at[number, unit, which],
            near,
        )

    def to_far(number, unit):
        return remote(
            near_in.at[number, unit, 1],
            far_in.at[number, unit],
            far_send.at[number, unit],
            far_recv.at[number, unit],
            far,
        )

    factor = (depth - data) * (depth - data) * (depth - data) % (depth + 1)

    def owner(unit):
        return (factor * (unit + 1)) % (depth + 1) - 1

    def rightward(number, block, slot):
        return remote(
            near_in.at[number, slot, 0],
            depth_in.at[number, block],
            depth_send.at[number, slot],
            depth_recv.at[number, block],
            right,
        )

    def leftward(number, block, slot, landing):
        return remote(
            near_in.at[number, slot, 0],
            depth_in.at[number, landing],
            depth_send.at[number, slot],
            depth_recv.at[number, landing],
            left,
        )

    def gradient(number, unit, rank):
        at = owner(unit) if inner else unit
        rows = pl.ds(pl.multiple_of(at * share, share), share)
        if number == 0:
            return nn(low_t[rows, :], act[rank])
        if number == 1:
            return nn(first_t[rows, :], slope[rank])
        main = nt(first_t[rows, :], p[rank])
        edge = (3 * part // 256) * 256
        tail = nt(low_t[rows, :], p[rank, edge : 4 * part, :])
        lane = lax.broadcasted_iota(jnp.int32, tail.shape, 1)
        tail = jnp.where(lane < 3 * part - edge, main[:, edge:], tail)
        return jnp.concatenate([main[:, :edge], tail], axis=1)

    def reduce_stage(number):
        def body(index, carry):
            @pl.when(index < units)
            def _():
                for which, rank in ((1, 3), (0, 1)):

                    @pl.when((index >= 2) | (number > 0))
                    def _():
                        to_near(number, index, which).wait_send()

                    near_out[index % 2, which] = gradient(number, index, rank).astype(BF)
                    to_near(number, index, which).start()

            @pl.when(index > 0)
            def _():
                unit = index - 1
                for which, rank in ((1, 2), (0, 0)):
                    mine = gradient(number, unit, rank)
                    to_near(number, unit, which).wait_recv()
                    near_in[number, unit, which] = (
                        mine + near_in[number, unit, which].astype(F32)
                    ).astype(BF)
                    if which == 1 and number == 0:

                        @pl.when(unit < 2)
                        def _():
                            to_far(number, unit).start()

            return carry

        lax.fori_loop(0, units + 1, body, 0)

    def finish(index):
        number = index // units
        unit = index % units
        to_far(number, unit).wait_recv()
        near_in[number, unit, 0] = (
            near_in[number, unit, 0].astype(F32) + far_in[number, unit].astype(F32)
        ).astype(BF)
        if inner:
            block = owner(unit)

            @pl.when(((block > data) & (data > 0)) | ((block < data) & (data < depth - 1)))
            def _():
                rightward(number, block, unit).wait_recv()
                near_in[number, unit, 0] = (
                    near_in[number, unit, 0].astype(F32) + depth_in[number, block].astype(F32)
                ).astype(BF)

            @pl.when(block > data)
            def _():
                rightward(number, block, unit).start()

            @pl.when(block < data)
            def _():
                landing = block + (depth - block) * ((block + 1) // data)
                leftward(number, block, unit, landing).start()

        @pl.when(index + 2 < 3 * units)
        def _():
            to_far((index + 2) // units, (index + 2) % units).start()


    @pl.when(section == 0)
    def _():
        arrived(4)
        reduce_stage(0)

    @pl.when(section != 0)
    def _():
        later_y.start()

    arrived(1)
    block = 256
    blocks = wu.shape[2] // block

    def narrow(index, carry):
        rank = index // blocks
        columns = pl.ds(pl.multiple_of((index % blocks) * block, block), block)
        value = nt(low[...], wd[rank, columns, :]) * slope[rank, :, columns].astype(F32)
        value = value.astype(BF)
        slope[rank, :, columns] = value
        vec[0, pl.ds(rank, 1), columns] = jnp.sum(value.astype(F32), axis=0, keepdims=True)
        return carry

    lax.fori_loop(0, ranks * blocks, narrow, 0)

    @pl.when(section == 0)
    def _():
        finish(0)

    arrived(2)

    def first_transpose(step, carry):
        rows = pl.ds(pl.multiple_of(step * STEP, STEP), STEP)
        value = n1[rows, :].astype(F32) * first_gain_ref[...].astype(F32)
        value = value + first_shift_ref[...].astype(F32)
        first_t[:, rows] = jnp.transpose(value, (1, 0)).astype(BF)
        return carry

    def up_gradients():
        lax.fori_loop(0, steps, first_transpose, 0)
        reduce_stage(1)

    @pl.when(section == 0)
    def _():
        up_gradients()
        finish(1)

    def first_back(step, carry):
        rows = pl.ds(pl.multiple_of(step * STEP, STEP), STEP)
        arriving = dsum[rows, :]
        for rank in range(ranks):
            arriving = arriving + nt(slope[rank, rows, :], wu[rank])
        normal = n1[rows, :].astype(F32)
        add_row(10, arriving * normal)
        add_row(11, arriving)
        value = norm_back(arriving, normal, rs1[rows, 0:1], first_gain_ref[...].astype(F32))
        dsum[rows, :] = value
        value = value.astype(BF)
        low[rows, :] = value
        add_row(8, value.astype(F32))
        return carry

    lax.fori_loop(0, steps, first_back, 0)

    @pl.when(section == 0)
    def _():
        finish(2)

    @pl.when(section != 0)
    def _():
        later_y.wait()
        pl.semaphore_wait(barrier, len(partners))
        share_outputs(g)

    arrived(3)

    def context_back(rank, carry):
        dcontext[rank] = nt(wa[rank, 3 * part : 4 * part, :], low[...]).astype(BF)
        return carry

    lax.fori_loop(0, ranks, context_back, 0)
    here = length_ref[tensor // sequences, tensor % sequences]
    visible = lax.broadcasted_iota(jnp.int32, (length, length), 0) < here

    def attend_back(head, carry):
        rank = head // heads
        base = (head % heads) * HD
        at_query = pl.ds(pl.multiple_of(base, HD), HD)
        at_keys = pl.ds(pl.multiple_of(part + base, HD), HD)
        at_values = pl.ds(pl.multiple_of(2 * part + base, HD), HD)
        query = (p[rank, at_query, :].astype(F32) * HD ** (-0.5)).astype(BF)
        keys = p[rank, at_keys, :]
        values = p[rank, at_values, :]
        dout = dcontext[rank, at_query, :]
        weights = jnp.where(visible, jnp.exp(tn(keys, query) - lse[head]), 0.0)
        dweights = tn(values, dout)
        inner_sum = jnp.sum(weights * dweights, axis=0, keepdims=True)
        dscores = (weights * (dweights - inner_sum)).astype(BF)
        p[rank, at_query, :] = (nn(keys, dscores) * HD ** (-0.5)).astype(BF)
        p[rank, at_keys, :] = nt(query, dscores).astype(BF)
        p[rank, at_values, :] = nt(dout, weights.astype(BF)).astype(BF)

        @pl.when((section == 0) & (head % 5 == 4))
        def _():
            finish(3 + head // 5)

        return carry

    lax.fori_loop(0, ranks * heads, attend_back, 0)
    early = 3 + ranks * heads // 5 + 1

    @pl.when(section != 0)
    def _():
        arrived(4)


    def entering_back(step, carry):
        rows = pl.ds(pl.multiple_of(step * STEP, STEP), STEP)
        total = dsum[rows, :]
        for rank in range(ranks):
            total = total + tn(p[rank, 0 : 3 * part, rows], wa[rank, 0 : 3 * part, :])
        dx[rows, :] = total.astype(BF)

        @pl.when(section != 0)
        def _():
            relay(step).start()

        return carry

    lax.fori_loop(0, steps, entering_back, 0)
    for rank in range(ranks):
        vec[0, 4 + rank : 5 + rank, :] = nt(jnp.ones((8, length), BF), p[rank])[0:1, :]
    vec_near = remote(vec.at[0], vec_in.at[0], vec_send.at[0], vec_recv.at[0], near)
    vec_near.start()
    turn(dx, dx_t)
    for copy in dx_copies:
        copy.start()
    dx_in[tensor] = dx_t[tensor]
    vec_near.wait_recv()

    def join(level, swap):
        for row in range(vec.shape[1]):
            pair = row ^ swap if row < 8 else row
            vec[level + 1, row : row + 1, :] = (
                vec[level, row : row + 1, :] + vec_in[level, pair : pair + 1, :]
            )

    join(0, 1)
    vec_far = remote(vec.at[1], vec_in.at[1], vec_send.at[1], vec_recv.at[1], far)
    vec_far.start()

    @pl.when(section == 0)
    def _():
        finish(early - 1)

    @pl.when(section != 0)
    def _():
        reduce_stage(0)
        up_gradients()
        finish(0)

    def entering_transpose(step, carry):
        rows = pl.ds(pl.multiple_of(step * STEP, STEP), STEP)
        first_t[:, rows] = jnp.transpose(xb[rows, :].astype(F32), (1, 0)).astype(BF)
        low_t[:, rows] = jnp.transpose(low[rows, :].astype(F32), (1, 0)).astype(BF)
        return carry

    lax.fori_loop(0, steps, entering_transpose, 0)
    reduce_stage(2)

    vec_far.wait_recv()
    join(1, 2)
    vec_deep = [
        remote(vec.at[2], vec_in.at[2 + hop], vec_send.at[2 + hop], vec_recv.at[2 + hop], device)
        for hop, device in enumerate(deep)
    ]
    for copy in vec_deep:
        copy.start()

    @pl.when(section != 0)
    def _():
        lax.fori_loop(1, early, lambda index, carry: (finish(index), carry)[1], 0)

    lax.fori_loop(early, 2 * units - 1, lambda index, carry: (finish(index), carry)[1], 0)
    for copy in dx_copies:
        copy.wait_recv()
    dx_done = pltpu.make_async_copy(dx_in, dx_out, out_sem.at[1])
    dx_done.start()
    half = table.shape[0]
    table_x = remote(table_away, table, table_send.at[0], table_recv.at[0], other)
    table_deep = [
        remote(table, table_in.at[hop], table_send.at[1 + hop], table_recv.at[1 + hop], device)
        for hop, device in enumerate(deep)
    ]

    @pl.when(section == 0)
    def _():
        types_each = table_out.shape[0]
        table_sum[...] = jnp.zeros_like(table_sum)

        def count(number, carry):
            row = lax.broadcasted_iota(jnp.int32, (2 * half, length), 0)
            picks = jnp.zeros((2 * half, length), F32)
            micro, item = number // sequences, number % sequences
            offset = 0
            for ids_ref, number_of in (
                (segment_ref, 2),
                (column_ref, COLS),
                (row_ref, ROWS),
                (answer_ref, 2),
            ):
                ids = ids_ref[micro, pl.ds(item, 1), :] + offset
                ids = ids + jnp.where(ids >= types_each, half - types_each, 0)
                picks = picks + jnp.where(ids == row, 1.0, 0.0)
                offset += number_of
            table_sum[...] += nt(picks.astype(BF), dx_in[number])
            return carry

        lax.fori_loop(0, ranks, count, 0)
        table[...] = table_sum[:half].astype(BF)
        table_away[...] = table_sum[half:].astype(BF)
        table_x.start()
        for copy in table_deep:
            copy.start()

    lax.fori_loop(2 * units - 1, 3 * units - 1, lambda index, carry: (finish(index), carry)[1], 0)

    @pl.when(section != 0)
    def _():
        table_x.wait_recv()
        for copy in table_deep:
            copy.start()

    finish(3 * units - 1)
    copies = []
    if inner:
        for number in range(3):
            total = jnp.zeros(final.shape[1:], F32)
            for unit in range(units):
                keep = jnp.where(owner(unit) == data, 1.0, 0.0)
                total = total + near_in[number, unit, 0].astype(F32) * keep
            final[number] = total

            @pl.when(data > 0)
            def _():
                rightward(number, data, 0).wait_recv()
                final[number] = final[number] + depth_in[number, data].astype(F32)

            @pl.when(data < depth - 1)
            def _():
                leftward(number, data, 0, depth).wait_recv()
                final[number] = final[number] + depth_in[number, depth].astype(F32)

            copy = pltpu.make_async_copy(
                final.at[number], sums_out.at[number], out_sem.at[2 + number]
            )
            copy.start()
            copies.append(copy)
    else:
        copy = pltpu.make_async_copy(
            near_in.at[:, :, 0], sums_out, out_sem.at[2]
        )
        copy.start()
        copies.append(copy)
    total = vec[2]
    for hop, copy in enumerate(vec_deep):
        copy.wait_recv()
        total = total + vec_in[2 + hop]
    vec_out[...] = total
    total = table[...].astype(F32)
    for hop, copy in enumerate(table_deep):
        copy.wait_recv()
        total = total + table_in[hop].astype(F32)
    table_out[...] = total[: table_out.shape[0]]

    for copy in y_copies:
        copy.wait()
    y_own.wait()
    for copy in dx_copies:
        copy.wait_send()
    vec_near.wait_send()
    vec_far.wait_send()
    for copy in vec_deep + table_deep:
        copy.wait_send()
    for unit in range(2):
        for which in range(2):
            to_near(2, unit, which).wait_send()
    for number in range(3):
        for unit in range(units):
            to_far(number, unit).wait_send()
            if inner:

                @pl.when(owner(unit) != data)
                def _():
                    rightward(number, 0, unit).wait_send()

    @pl.when(section != 0)
    def _():
        for step in range(steps):
            relay(step).wait_send()

    @pl.when(section == 0)
    def _():
        table_x.wait_send()

    dx_done.wait()
    for copy in copies:
        copy.wait()


def backward(cotangent, saved, lengths, vectors, ids, type_half, inner):
    wa, wu, wd, p, lse, act, slope, n1, n2, rs1, rs2, x, y = saved
    ranks = wa.shape[0]
    length, width = x.shape
    steps = length // STEP
    depth = lax.axis_size("dp")
    units = depth if inner else 4
    hops = depth - 1 if inner else 0
    share = width // units
    anywhere = pl.BlockSpec(memory_space=pl.ANY)
    inside = pl.BlockSpec(memory_space=pltpu.VMEM)
    part = wa.shape[1] // 4
    each = width // ranks
    half = -(-type_half // 16) * 16

    def like(value):
        return pltpu.VMEM(value.shape, value.dtype)

    plane = (length, width)
    turned = (width, length)
    chunk = (share, width)
    spread = (ranks, each, length)
    semaphores = pltpu.SemaphoreType.DMA
    sums = ((3,) + chunk, F32) if inner else ((3, units) + chunk, BF)
    return pl.pallas_call(
        functools.partial(backward_kernel, inner),
        name="backward_layer",
        out_shape=(
            jax.ShapeDtypeStruct(*sums),
            jax.ShapeDtypeStruct(spread, BF),
            jax.ShapeDtypeStruct(spread, BF),
            jax.ShapeDtypeStruct((16, width), F32),
            jax.ShapeDtypeStruct((type_half, each), F32),
        ),
        in_specs=[anywhere] * 14
        + [pl.BlockSpec(memory_space=pltpu.SMEM)]
        + [inside] * (len(vectors) + len(ids)),
        out_specs=(anywhere, anywhere, anywhere, inside, inside),
        scratch_shapes=[like(value) for value in saved[:-1]]
        + [
            pltpu.VMEM(plane, BF),
            pltpu.VMEM(plane, F32),
            pltpu.VMEM(plane, BF),
            pltpu.VMEM(turned, BF),
            pltpu.VMEM(turned, BF),
            pltpu.VMEM((ranks, part, length), BF),
            pltpu.VMEM(plane, BF),
            pltpu.VMEM(spread, BF),
            pltpu.VMEM(spread, BF),
            pltpu.VMEM(spread, BF),
            pltpu.VMEM((2, 2) + chunk, BF),
            pltpu.VMEM((3, units, 2) + chunk, BF),
            pltpu.VMEM((3, units) + chunk, BF),
            pltpu.VMEM((3, units + 1) + (chunk if inner else (16, 128)), BF),
            pltpu.VMEM((3,) + (chunk if inner else (16, 128)), F32),
            pltpu.VMEM((3, 16, width), F32),
            pltpu.VMEM((2 + hops, 16, width), F32),
            pltpu.VMEM((half, each), BF),
            pltpu.VMEM((half, each), BF),
            pltpu.VMEM((max(hops, 1), half, each), BF),
            pltpu.VMEM((2 * half, each), F32),
            semaphores((15,)),
            semaphores((2, 2)),
            semaphores((3, units, 2)),
            semaphores((3, units)),
            semaphores((3, units)),
            semaphores((3, units)),
            semaphores((3, units + 1)),
            semaphores((steps,)),
            semaphores((steps,)),
            semaphores((3,)),
            semaphores((3,)),
            semaphores((3,)),
            semaphores((3,)),
            semaphores((2 + hops,)),
            semaphores((2 + hops,)),
            semaphores((1 + hops,)),
            semaphores((1 + hops,)),
            semaphores((5,)),
        ],
        compiler_params=pltpu.CompilerParams(
            collective_id=1, has_side_effects=True, vmem_limit_bytes=VMEM_LIMIT
        ),
        cost_estimate=pl.CostEstimate(
            flops=17_000_000_000, bytes_accessed=60_000_000, transcendentals=3_000_000
        ),
    )(cotangent, *saved, lengths, *vectors, *ids)


def on_device(
    inputs,
    cotangent,
    segment_ids,
    column_ids,
    row_ids,
    answer_ids,
    lengths,
    type_table,
    query_weight,
    query_bias,
    key_weight,
    value_weight,
    value_bias,
    output_weight,
    output_bias,
    first_gain,
    first_shift,
    up_weight,
    up_bias,
    down_weight,
    down_bias,
    second_gain,
    second_shift,
):
    tensor = lax.axis_index("tensor")
    ranks = lax.axis_size("tensor")
    micro_count, sequences, length, width = inputs.shape
    type_count = 4 + COLS + ROWS
    part = query_weight.shape[2]
    hidden = up_weight.shape[2]

    ids = (segment_ids, column_ids, row_ids, answer_ids)
    wa = jnp.concatenate(
        [query_weight[0].T, key_weight[0].T, value_weight[0].T, output_weight[0]], axis=0
    )
    vectors = (
        query_bias,
        value_bias,
        up_bias,
        output_bias,
        first_gain,
        first_shift,
        down_bias,
        second_gain,
        second_shift,
    )
    saved = forward(
        inputs, ids, type_table, lengths, wa, up_weight[0], down_weight[0], vectors, ranks
    )
    depth = lax.axis_size("dp")
    inner = depth == 4 and width % (16 * depth) == 0
    type_half = type_count // lax.axis_size("section")
    sums, dx, leaving, vecs, table_grad = backward(
        cotangent, saved, lengths, (first_gain, first_shift, second_gain), ids, type_half, inner
    )

    def in_columns(value):
        return jnp.swapaxes(value, 1, 2).reshape(
            1, micro_count, sequences, length, width // ranks
        )

    layer_outputs = in_columns(leaving)
    layer_input_grads = in_columns(dx).astype(F32)
    if inner:
        summed = sums
    else:
        summed = lax.psum_scatter(
            sums.reshape(3, width, width), "dp", scatter_dimension=1, tiled=True
        ).astype(F32)
        vecs = lax.psum(vecs, "dp")
        table_grad = lax.psum(table_grad.astype(BF), "dp").astype(F32)
    mine = lax.dynamic_slice_in_dim(
        vecs[8:14].reshape(6, ranks, width // ranks), tensor, 1, 1
    ).reshape(1, 6 * (width // ranks))
    mine = jnp.concatenate([vecs[0:1], vecs[4:5], mine], axis=1)

    def vector(start, count):
        return mine[:, start : start + count]

    share = width // ranks
    after = 2 * width
    return (
        layer_outputs,
        layer_input_grads,
        summed[2, :, 0:part][None],
        vector(width, part),
        summed[2, :, part : 2 * part][None],
        summed[2, :, 2 * part : 3 * part][None],
        vector(width + 2 * part, part),
        summed[2, :, 3 * part : 4 * part].T[None],
        vector(after, share),
        vector(after + 2 * share, share),
        vector(after + 3 * share, share),
        summed[1][None],
        vector(0, hidden),
        summed[0].T[None],
        vector(after + share, share),
        vector(after + 4 * share, share),
        vector(after + 5 * share, share),
        table_grad,
    )


def solution(mesh):
    return jax.shard_map(
        on_device,
        mesh=mesh,
        in_specs=(
            P(None, "dp", None, None),
            P(None, "dp", None, None),
            P(None, "dp", None),
            P(None, "dp", None),
            P(None, "dp", None),
            P(None, "dp", None),
            P(None, "dp"),
            P(),
            P("section", None, "tensor"),
            P("section", "tensor"),
            P("section", None, "tensor"),
            P("section", None, "tensor"),
            P("section", "tensor"),
            P("section", "tensor", None),
            P("section", None),
            P("section", None),
            P("section", None),
            P("section", None, "tensor"),
            P("section", "tensor"),
            P("section", "tensor", None),
            P("section", None),
            P("section", None),
            P("section", None),
        ),
        out_specs=(
            P("section", None, "dp", None, "tensor"),
            P("section", None, "dp", None, "tensor"),
            P("section", "dp", "tensor"),
            P("section", "tensor"),
            P("section", "dp", "tensor"),
            P("section", "dp", "tensor"),
            P("section", "tensor"),
            P("section", "tensor", "dp"),
            P("section", "tensor"),
            P("section", "tensor"),
            P("section", "tensor"),
            P("section", "dp", "tensor"),
            P("section", "tensor"),
            P("section", "tensor", "dp"),
            P("section", "tensor"),
            P("section", "tensor"),
            P("section", "tensor"),
            P("section", "tensor"),
        ),
        check_vma=False,
    )
```

```python
import functools

import jax
import jax.numpy as jnp
from jax import lax
from jax.experimental import pallas as pl
from jax.experimental.pallas import tpu as pltpu
from jax.sharding import PartitionSpec as P

HD = 64
COLS = 256
ROWS = 256
EPSILON = 1e-12
MASKED = -1e30
BF = jnp.bfloat16
F32 = jnp.float32
MESH = pl.DeviceIdType.MESH
VMEM_LIMIT = 60 * 1024 * 1024
STEP = 256
SHARES = (5, 5, 5)
OUTS = ("wa", "wu", "wd", "p", "lse", "act", "slope", "n1", "n2", "rs1", "rs2", "x", "y")


def nn(left, right):
    return lax.dot_general(left, right, (((1,), (0,)), ((), ())), preferred_element_type=F32)


def nt(left, right):
    return lax.dot_general(left, right, (((1,), (1,)), ((), ())), preferred_element_type=F32)


def tn(left, right):
    return lax.dot_general(left, right, (((0,), (0,)), ((), ())), preferred_element_type=F32)


def normalize(value):
    centered = value - jnp.mean(value, axis=-1, keepdims=True)
    variance = jnp.mean(centered * centered, axis=-1, keepdims=True)
    scale = lax.rsqrt(variance + EPSILON)
    return centered * scale, scale


def place():
    section = lax.axis_index("section")
    data = lax.axis_index("dp")
    tensor = lax.axis_index("tensor")
    beside = tensor + 1 - 2 * (tensor % 2)
    across = tensor + 2 - 4 * ((tensor // 2) % 2)
    return section, data, tensor, beside, across


def greet(partners):
    barrier = pltpu.get_barrier_semaphore()
    for partner in partners:
        pl.semaphore_signal(barrier, inc=1, device_id=partner, device_id_type=MESH)
    pl.semaphore_wait(barrier, len(partners))


def remote(src, dst, send, recv, device):
    return pltpu.make_async_remote_copy(
        src_ref=src, dst_ref=dst, send_sem=send, recv_sem=recv, device_id=device, device_id_type=MESH
    )


def forward_kernel(
    inputs_ref,
    segment_ref,
    column_ref,
    row_ref,
    answer_ref,
    table_ref,
    length_ref,
    wa_ref,
    wu_ref,
    wd_ref,
    query_bias_ref,
    value_bias_ref,
    up_bias_ref,
    output_bias_ref,
    first_gain_ref,
    first_shift_ref,
    down_bias_ref,
    second_gain_ref,
    second_shift_ref,
    wa_out,
    wu_out,
    wd_out,
    p_out,
    lse_out,
    act_out,
    slope_out,
    n1_out,
    n2_out,
    rs1_out,
    rs2_out,
    x_out,
    y_out,
    wa,
    wu,
    wd,
    bias,
    table,
    p,
    lse,
    act,
    slope,
    xf,
    xb,
    first,
    low,
    n1,
    n2,
    rs1,
    rs2,
    y,
    gather_send,
    gather_recv,
    chain_send,
    chain_recv,
    relay_send,
    relay_recv,
    local_sem,
    out_sem,
    turn_sem,
):
    section, data, tensor, beside, across = place()
    length, width = xf.shape
    ranks = wa.shape[0]
    heads = wa.shape[1] // (4 * HD)
    part = heads * HD
    steps = length // STEP
    sequences = inputs_ref.shape[1]
    near = (section, data, beside)
    far = (section, data, across)
    other = (1 - section, data, tensor)
    depth = lax.axis_size("dp")
    group = 4 if depth % 4 == 0 else 1
    spot = data % group
    before = (section, data - spot + (spot + group - 1) % group, tensor)
    after = (section, data - spot + (spot + 1) % group, tensor)
    greet([near, far, other] + ([before, after] if group > 1 else []))

    shards = ((wa_ref, wa), (wu_ref, wu), (wd_ref, wd))
    direct = [wa.shape[1] * count // 12 for count in SHARES]
    piece = [(wa.shape[1] - count) // group for count in direct]

    def rows_of(number, part_at):
        start = direct[number] + part_at * piece[number]
        return pl.ds(pl.multiple_of(start, 16), piece[number])

    to_far = []
    to_near = []
    onward = []
    own = []
    for number, (source, target) in enumerate(shards):
        to_far.append(
            [
                remote(
                    source.at[rows],
                    target.at[2, rows],
                    gather_send.at[number, which],
                    gather_recv.at[number, which],
                    far,
                )
                for which, rows in enumerate((rows_of(number, spot), pl.ds(0, direct[number])))
            ]
        )
        to_near.append(
            remote(source, target.at[1], gather_send.at[number, 2], gather_recv.at[number, 2], near)
        )
        rest = wa.shape[1] - direct[number]
        onward.append(
            [
                remote(
                    target.at[2, rows],
                    target.at[3, rows],
                    gather_send.at[number, 3 + which],
                    gather_recv.at[number, 3 + which],
                    near,
                )
                for which, rows in enumerate(
                    (pl.ds(0, direct[number]), pl.ds(direct[number], rest))
                )
            ]
        )
        own.append(pltpu.make_async_copy(source, target.at[0], local_sem.at[number]))
    to_far[0][0].start()
    for copy in to_near:
        copy.start()
    for copy in own:
        copy.start()
    bias[0] = jnp.zeros(bias.shape[1:], F32)
    bias[0, 0:1, :] = up_bias_ref[...].astype(F32)
    bias[0, 1:2, 0:part] = query_bias_ref[...].astype(F32)
    bias[0, 1:2, 2 * part : 3 * part] = value_bias_ref[...].astype(F32)
    bias_copies = [
        remote(bias.at[0], bias.at[1 + which], gather_send.at[3, which], gather_recv.at[3, which], to)
        for which, to in enumerate((near, far))
    ]
    bias_onward = remote(bias.at[2], bias.at[3], gather_send.at[3, 2], gather_recv.at[3, 2], near)
    for copy in bias_copies:
        copy.start()

    def chain(number, hop, up):
        rows = rows_of(number, spot - (hop - 1) if up else spot + (hop - 1))
        target = shards[number][1]
        at = 0 if up else 1
        return remote(
            target.at[2, rows],
            target.at[2, rows],
            chain_send.at[number, at, hop - 1],
            chain_recv.at[number, at, hop - 1],
            after if up else before,
        )

    def chained(number, hop, up):
        rows = rows_of(number, spot - hop if up else spot + hop)
        target = shards[number][1]
        at = 0 if up else 1
        return remote(
            target.at[2, rows],
            target.at[2, rows],
            chain_send.at[number, at, hop - 1],
            chain_recv.at[number, at, hop - 1],
            before if up else after,
        )

    def piece_in(number):
        to_far[number][0].wait_recv()

    def send_piece(number):
        to_far[number][0].start()

    def send_direct(number):
        to_far[number][1].start()

    def hand_on(number, hop):
        if group == 1 or hop == group:
            return
        if hop > 0:

            @pl.when(spot >= hop)
            def _():
                chained(number, hop, True).wait_recv()

            @pl.when(spot + hop < group)
            def _():
                chained(number, hop, False).wait_recv()

        if hop + 1 < group:

            @pl.when((spot >= hop) & (spot + 1 < group))
            def _():
                chain(number, hop + 1, True).start()

            @pl.when((spot + hop < group) & (spot >= 1))
            def _():
                chain(number, hop + 1, False).start()

    def direct_in(number):
        to_far[number][1].wait_recv()
        onward[number][0].start()

    def pass_on(number):
        onward[number][1].start()

    def ready(number):
        own[number].wait()
        to_near[number].wait_recv()
        for copy in onward[number]:
            copy.wait_recv()

    def at_first(actions):
        @pl.when(section == 0)
        def _():
            for action, *values in actions:
                action(*values)

    out_copies = []

    wu_copy = pltpu.make_async_copy(wu, wu_out, out_sem.at[len(OUTS)])
    wd_copy = pltpu.make_async_copy(wd, wd_out, out_sem.at[len(OUTS) + 1])

    def put_out(source, target):
        copy = pltpu.make_async_copy(source, target, out_sem.at[len(out_copies)])
        copy.start()
        out_copies.append(copy)

    relays = [
        remote(
            y.at[pl.ds(step * STEP, STEP)],
            xb.at[pl.ds(step * STEP, STEP)],
            relay_send.at[step],
            relay_recv.at[step],
            other,
        )
        for step in range(steps)
    ]

    load_input = pltpu.make_async_copy(
        inputs_ref.at[tensor // sequences, tensor % sequences], xb, local_sem.at[3]
    )

    @pl.when(section == 0)
    def _():
        load_input.start()

    piece_in(0)
    hand_on(0, 0)
    send_piece(1)
    send_direct(0)
    bias_copies[1].wait_recv()
    bias_onward.start()

    @pl.when(section == 0)
    def _():
        load_input.wait()
        types = table.shape[0]
        table[...] = jnp.zeros_like(table)
        table[0 : table_ref.shape[0], :] = table_ref[...]
        micro, item = tensor // sequences, tensor % sequences
        offset = 0
        row = lax.broadcasted_iota(jnp.int32, (types, length), 0)
        picks = jnp.zeros((types, length), F32)
        for ids_ref, count in (
            (segment_ref, 2),
            (column_ref, COLS),
            (row_ref, ROWS),
            (answer_ref, 2),
        ):
            ids = ids_ref[micro, pl.ds(item, 1), :] + offset
            picks = picks + jnp.where(ids == row, 1.0, 0.0)
            offset += count
        xf[...] = xb[...].astype(F32) + tn(picks.astype(BF), table[...])
        xb[...] = xf[...].astype(BF)

    hand_on(0, 1)
    hand_on(0, 2)
    piece_in(1)
    hand_on(1, 0)
    send_piece(2)
    direct_in(0)
    send_direct(1)
    hand_on(0, 3)
    pass_on(0)
    hand_on(1, 1)
    ready(0)
    put_out(wa, wa_out)

    @pl.when(section != 0)
    def _():
        piece_in(2)
        hand_on(2, 0)
        hand_on(1, 2)
        hand_on(2, 1)
        hand_on(1, 3)
        direct_in(1)
        pass_on(1)
        send_direct(2)
        hand_on(2, 2)
        hand_on(2, 3)
        direct_in(2)
        pass_on(2)
        ready(1)
        wu_copy.start()
        ready(2)
        wd_copy.start()
        for relay in relays:
            relay.wait_recv()
        xf[...] = xb[...].astype(F32)

    bias_copies[0].wait_recv()
    bias_onward.wait_recv()
    put_out(xb, x_out)

    def project(rank, carry):
        columns = jnp.transpose(bias[rank], (1, 0))
        p[rank, 0 : 3 * part, :] = (
            nt(wa[rank, 0 : 3 * part, :], xb[...]) + columns[0 : 3 * part, 1:2]
        ).astype(BF)
        return carry

    lax.fori_loop(0, ranks, project, 0)
    at_first([(piece_in, 2), (hand_on, 2, 0)])

    here = length_ref[tensor // sequences, tensor % sequences]
    visible = lax.broadcasted_iota(jnp.int32, (length, length), 0) < here

    def attend(head, carry):
        rank = head // heads
        base = (head % heads) * HD
        query = p[rank, pl.ds(pl.multiple_of(base, HD), HD), :]
        keys = p[rank, pl.ds(pl.multiple_of(part + base, HD), HD), :]
        values = p[rank, pl.ds(pl.multiple_of(2 * part + base, HD), HD), :]
        query = (query.astype(F32) * HD ** (-0.5)).astype(BF)
        scores = jnp.where(visible, tn(keys, query), MASKED)
        maximum = jnp.max(scores, axis=0, keepdims=True)
        raised = jnp.exp(scores - maximum)
        total = jnp.sum(raised, axis=0, keepdims=True)
        context = nn(values, raised.astype(BF)) / total
        p[rank, pl.ds(pl.multiple_of(3 * part + base, HD), HD), :] = context.astype(BF)
        lse[head] = maximum + jnp.log(total)
        for at, action in (
            (2, (hand_on, 1, 2)),
            (7, (hand_on, 2, 1)),
            (7, (direct_in, 1)),
            (7, (send_direct, 2)),
            (11, (hand_on, 1, 3)),
            (11, (pass_on, 1)),
        ):

            @pl.when((section == 0) & (head == at))
            def _():
                action[0](*action[1:])

        return carry

    lax.fori_loop(0, ranks * heads, attend, 0)
    put_out(p, p_out)
    put_out(lse, lse_out)

    def first_norm(step, carry):
        rows = pl.ds(pl.multiple_of(step * STEP, STEP), STEP)
        total = xf[rows, :] + output_bias_ref[...].astype(F32)
        for rank in range(ranks):
            total = total + tn(p[rank, 3 * part : 4 * part, rows], wa[rank, 3 * part : 4 * part, :])
        normal, scale = normalize(total)
        value = normal * first_gain_ref[...].astype(F32) + first_shift_ref[...].astype(F32)
        first[rows, :] = value
        low[rows, :] = value.astype(BF)
        n1[rows, :] = normal.astype(BF)
        rs1[rows, :] = jnp.broadcast_to(scale, (STEP, 128))
        return carry

    lax.fori_loop(0, steps, first_norm, 0)
    put_out(n1, n1_out)
    put_out(rs1, rs1_out)
    at_first([(hand_on, 2, 2), (ready, 1), (wu_copy.start,)])
    block = 256
    blocks = wu.shape[2] // block

    def widen(index, carry):
        rank = index // blocks
        columns = pl.ds(pl.multiple_of((index % blocks) * block, block), block)
        hidden = nn(low[...], wu[rank, :, columns]) + bias[rank, 0:1, columns]
        inner = 0.5 * (1.0 + lax.erf(hidden * (0.5**0.5)))
        act[rank, :, columns] = (hidden * inner).astype(BF)
        density = jnp.exp(hidden * hidden * (-0.5)) * 0.3989422804014327
        slope[rank, :, columns] = (inner + hidden * density).astype(BF)

        @pl.when((section == 0) & (index == ranks * blocks - 4))
        def _():
            direct_in(2)
            hand_on(2, 3)
            pass_on(2)

        return carry

    lax.fori_loop(0, ranks * blocks, widen, 0)
    put_out(act, act_out)
    put_out(slope, slope_out)
    at_first([(ready, 2), (wd_copy.start,)])

    for step in range(steps):
        rows = pl.ds(step * STEP, STEP)
        total = first[rows, :] + down_bias_ref[...].astype(F32)
        for rank in range(ranks):
            total = total + nn(act[rank, rows, :], wd[rank])
        normal, scale = normalize(total)
        y[rows, :] = (
            normal * second_gain_ref[...].astype(F32) + second_shift_ref[...].astype(F32)
        ).astype(BF)
        n2[rows, :] = normal.astype(BF)
        rs2[rows, :] = jnp.broadcast_to(scale, (STEP, 128))

        @pl.when((section == 0) & (tensor % 2 == 0))
        def _():
            relays[step].start()

    put_out(n2, n2_out)
    put_out(rs2, rs2_out)
    put_out(y, y_out)

    @pl.when((section == 0) & (tensor % 2 == 0))
    def _():
        for relay in relays:
            relay.wait_send()
        pl.semaphore_signal(turn_sem, inc=1, device_id=near, device_id_type=MESH)

    @pl.when((section == 0) & (tensor % 2 == 1))
    def _():
        pl.semaphore_wait(turn_sem, 1)
        for relay in relays:
            relay.start()
        for relay in relays:
            relay.wait_send()

    for copy in out_copies + [wu_copy, wd_copy]:
        copy.wait()
    for copies in to_far + onward + [to_near, bias_copies, [bias_onward]]:
        for copy in copies:
            copy.wait_send()
    for number in range(3):
        for hop in range(group - 1):

            @pl.when((spot >= hop) & (spot + 1 < group))
            def _():
                chain(number, hop + 1, True).wait_send()

            @pl.when((spot + hop < group) & (spot >= 1))
            def _():
                chain(number, hop + 1, False).wait_send()


def forward(inputs, ids, table, lengths, wa, wu, wd, vectors, ranks):
    length, width = inputs.shape[2], inputs.shape[3]
    rows_a = wa.shape[0]
    hidden = wu.shape[1]
    heads = ranks * (rows_a // (4 * HD))
    steps = length // STEP
    shapes = dict(
        wa=((ranks, rows_a, width), BF),
        wu=((ranks, width, hidden), BF),
        wd=((ranks, hidden, width), BF),
        p=((ranks, rows_a, length), BF),
        lse=((heads, 1, length), F32),
        act=((ranks, length, hidden), BF),
        slope=((ranks, length, hidden), BF),
        n1=((length, width), BF),
        n2=((length, width), BF),
        rs1=((length, 128), F32),
        rs2=((length, 128), F32),
        x=((length, width), BF),
        y=((length, width), BF),
    )

    def buffer(name):
        return pltpu.VMEM(*shapes[name])

    anywhere = pl.BlockSpec(memory_space=pl.ANY)
    inside = pl.BlockSpec(memory_space=pltpu.VMEM)
    return pl.pallas_call(
        forward_kernel,
        name="forward_layer",
        out_shape=tuple(jax.ShapeDtypeStruct(*shapes[name]) for name in OUTS),
        in_specs=[
            anywhere,
            inside,
            inside,
            inside,
            inside,
            inside,
            pl.BlockSpec(memory_space=pltpu.SMEM),
            anywhere,
            anywhere,
            anywhere,
        ]
        + [inside] * len(vectors),
        out_specs=tuple(anywhere for _ in OUTS),
        scratch_shapes=[
            buffer("wa"),
            buffer("wu"),
            buffer("wd"),
            pltpu.VMEM((ranks, 8, hidden), F32),
            pltpu.VMEM((-(-table.shape[0] // 16) * 16, width), BF),
            buffer("p"),
            buffer("lse"),
            buffer("act"),
            buffer("slope"),
            pltpu.VMEM((length, width), F32),
            buffer("x"),
            pltpu.VMEM((length, width), F32),
            pltpu.VMEM((length, width), BF),
            buffer("n1"),
            buffer("n2"),
            buffer("rs1"),
            buffer("rs2"),
            buffer("y"),
            pltpu.SemaphoreType.DMA((4, 5)),
            pltpu.SemaphoreType.DMA((4, 5)),
            pltpu.SemaphoreType.DMA((3, 2, 3)),
            pltpu.SemaphoreType.DMA((3, 2, 3)),
            pltpu.SemaphoreType.DMA((steps,)),
            pltpu.SemaphoreType.DMA((steps,)),
            pltpu.SemaphoreType.DMA((5,)),
            pltpu.SemaphoreType.DMA((len(OUTS) + 2,)),
            pltpu.SemaphoreType.REGULAR,
        ],
        compiler_params=pltpu.CompilerParams(
            collective_id=0, has_side_effects=True, vmem_limit_bytes=VMEM_LIMIT
        ),
        cost_estimate=pl.CostEstimate(
            flops=8_000_000_000, bytes_accessed=60_000_000, transcendentals=6_000_000
        ),
    )(inputs, *ids, table, lengths, wa, wu, wd, *vectors)


def backward_kernel(
    inner,
    cotangent_ref,
    wa_ref,
    wu_ref,
    wd_ref,
    p_ref,
    lse_ref,
    act_ref,
    slope_ref,
    n1_ref,
    n2_ref,
    rs1_ref,
    rs2_ref,
    x_ref,
    y_ref,
    length_ref,
    first_gain_ref,
    first_shift_ref,
    second_gain_ref,
    segment_ref,
    column_ref,
    row_ref,
    answer_ref,
    sums_out,
    dx_out,
    y_out,
    vec_out,
    table_out,
    wa,
    wu,
    wd,
    p,
    lse,
    act,
    slope,
    n1,
    n2,
    rs1,
    rs2,
    xb,
    g,
    dsum,
    low,
    low_t,
    first_t,
    dcontext,
    dx,
    dx_t,
    dx_in,
    y_t,
    near_out,
    near_in,
    far_in,
    depth_in,
    final,
    vec,
    vec_in,
    table,
    table_away,
    table_in,
    table_sum,
    load_sem,
    near_send,
    near_recv,
    far_send,
    far_recv,
    depth_send,
    depth_recv,
    relay_send,
    relay_recv,
    dx_send,
    dx_recv,
    y_send,
    y_recv,
    vec_send,
    vec_recv,
    table_send,
    table_recv,
    out_sem,
):
    section, data, tensor, beside, across = place()
    diagonal = beside + 2 - 4 * ((beside // 2) % 2)
    length, width = g.shape
    ranks = wa.shape[0]
    heads = wa.shape[1] // (4 * HD)
    part = heads * HD
    steps = length // STEP
    sequences = cotangent_ref.shape[1]
    units = near_in.shape[1]
    share = near_in.shape[3]
    columns_each = width // ranks
    depth = lax.axis_size("dp")
    near = (section, data, beside)
    far = (section, data, across)
    corner = (section, data, diagonal)
    other = (1 - section, data, tensor)
    deep = []
    left = right = None
    if inner:
        deep = [(section, (data + 1 + hop) % depth, tensor) for hop in range(depth - 1)]
        left = (section, (data + depth - 1) % depth, tensor)
        right = (section, (data + 1) % depth, tensor)
    partners = [near, far, corner, other] + deep
    barrier = pltpu.get_barrier_semaphore()
    for partner in partners:
        pl.semaphore_signal(barrier, inc=1, device_id=partner, device_id_type=MESH)

    @pl.when(section == 0)
    def _():
        pl.semaphore_wait(barrier, len(partners))

    loads = {}
    for name, source, target in (
        ("n2", n2_ref, n2),
        ("rs2", rs2_ref, rs2),
        ("wd", wd_ref, wd),
        ("slope", slope_ref, slope),
        ("wu", wu_ref, wu),
        ("act", act_ref, act),
        ("n1", n1_ref, n1),
        ("rs1", rs1_ref, rs1),
        ("wa", wa_ref, wa),
        ("p", p_ref, p),
        ("lse", lse_ref, lse),
        ("xb", x_ref, xb),
    ):
        loads[name] = pltpu.make_async_copy(source, target, load_sem.at[len(loads)])
    start_g = pltpu.make_async_copy(
        cotangent_ref.at[tensor // sequences, tensor % sequences], g, load_sem.at[len(loads)]
    )
    first_y = pltpu.make_async_copy(y_ref, dx, load_sem.at[len(loads) + 1])
    later_y = pltpu.make_async_copy(y_ref, g, load_sem.at[len(loads) + 1])
    waves = (("n2", "rs2"), ("wd", "slope"), ("wu", "n1", "rs1"), ("wa", "p", "lse"), ("act", "xb"))

    def begin(wave):
        for name in waves[wave]:
            loads[name].start()

    def arrived(wave):
        for name in waves[wave]:
            loads[name].wait()
        if wave + 1 < len(waves):

            @pl.when(section != 0)
            def _():
                begin(wave + 1)


    def relay(step):
        rows = pl.ds(pl.multiple_of(step * STEP, STEP), STEP)
        return remote(dx.at[rows], g.at[rows], relay_send.at[step], relay_recv.at[step], other)

    around = ((beside, near), (across, far), (diagonal, corner))
    y_copies = [
        remote(y_t.at[rank], y_out.at[tensor], y_send.at[number], y_recv.at[number], device)
        for number, (rank, device) in enumerate(around)
    ]
    y_own = pltpu.make_async_copy(y_t.at[tensor], y_out.at[tensor], out_sem.at[0])
    dx_copies = [
        remote(dx_t.at[rank], dx_in.at[tensor], dx_send.at[number], dx_recv.at[number], device)
        for number, (rank, device) in enumerate(around)
    ]

    def turn(source, target):
        def body(step, carry):
            rows = pl.ds(pl.multiple_of(step * STEP, STEP), STEP)
            value = jnp.transpose(source[rows, :].astype(F32), (1, 0)).astype(BF)
            for rank in range(ranks):
                target[rank, :, rows] = value[rank * columns_each : (rank + 1) * columns_each]
            return carry

        lax.fori_loop(0, steps, body, 0)

    def share_outputs(source):
        turn(source, y_t)
        for copy in y_copies:
            copy.start()
        y_own.start()

    begin(0)
    vec[0] = jnp.zeros(vec.shape[1:], F32)

    @pl.when(section == 0)
    def _():
        first_y.start()
        for wave in range(1, len(waves)):
            begin(wave)
        first_y.wait()
        share_outputs(dx)

    @pl.when(section != 0)
    def _():
        start_g.start()
        start_g.wait()

    arrived(0)

    def add_row(row, value):
        vec[0, row : row + 1, :] += jnp.sum(value, axis=0, keepdims=True)

    def norm_back(arriving, normal, scale, gain):
        scaled = arriving * gain
        return (
            scaled
            - jnp.mean(scaled, axis=-1, keepdims=True)
            - normal * jnp.mean(scaled * normal, axis=-1, keepdims=True)
        ) * scale

    def second_back(step, carry):
        rows = pl.ds(pl.multiple_of(step * STEP, STEP), STEP)

        @pl.when(section == 0)
        def _():
            relay(step).wait_recv()

        arriving = g[rows, :].astype(F32)
        normal = n2[rows, :].astype(F32)
        add_row(12, arriving * normal)
        add_row(13, arriving)
        value = norm_back(arriving, normal, rs2[rows, 0:1], second_gain_ref[...].astype(F32))
        dsum[rows, :] = value
        value = value.astype(BF)
        low[rows, :] = value
        value = value.astype(F32)
        add_row(9, value)
        low_t[:, rows] = jnp.transpose(value, (1, 0)).astype(BF)
        return carry

    lax.fori_loop(0, steps, second_back, 0)

    def to_near(number, unit, which):
        return remote(
            near_out.at[unit % 2, which],
            near_in.at[number, unit, which],
            near_send.at[unit % 2, which],
            near_recv.at[number, unit, which],
            near,
        )

    def to_far(number, unit):
        return remote(
            near_in.at[number, unit, 1],
            far_in.at[number, unit],
            far_send.at[number, unit],
            far_recv.at[number, unit],
            far,
        )

    factor = (depth - data) * (depth - data) * (depth - data) % (depth + 1)

    def owner(unit):
        return (factor * (unit + 1)) % (depth + 1) - 1

    def rightward(number, block, slot):
        return remote(
            near_in.at[number, slot, 0],
            depth_in.at[number, block],
            depth_send.at[number, slot],
            depth_recv.at[number, block],
            right,
        )

    def leftward(number, block, slot, landing):
        return remote(
            near_in.at[number, slot, 0],
            depth_in.at[number, landing],
            depth_send.at[number, slot],
            depth_recv.at[number, landing],
            left,
        )

    def gradient(number, unit, rank):
        at = owner(unit) if inner else unit
        rows = pl.ds(pl.multiple_of(at * share, share), share)
        if number == 0:
            return nn(low_t[rows, :], act[rank])
        if number == 1:
            return nn(first_t[rows, :], slope[rank])
        main = nt(first_t[rows, :], p[rank])
        edge = (3 * part // 256) * 256
        tail = nt(low_t[rows, :], p[rank, edge : 4 * part, :])
        lane = lax.broadcasted_iota(jnp.int32, tail.shape, 1)
        tail = jnp.where(lane < 3 * part - edge, main[:, edge:], tail)
        return jnp.concatenate([main[:, :edge], tail], axis=1)

    def reduce_stage(number):
        def body(index, carry):
            @pl.when(index < units)
            def _():
                for which, rank in ((1, 3), (0, 1)):

                    @pl.when((index >= 2) | (number > 0))
                    def _():
                        to_near(number, index, which).wait_send()

                    near_out[index % 2, which] = gradient(number, index, rank).astype(BF)
                    to_near(number, index, which).start()

            @pl.when(index > 0)
            def _():
                unit = index - 1
                for which, rank in ((1, 2), (0, 0)):
                    mine = gradient(number, unit, rank)
                    to_near(number, unit, which).wait_recv()
                    near_in[number, unit, which] = (
                        mine + near_in[number, unit, which].astype(F32)
                    ).astype(BF)
                    if which == 1 and number == 0:

                        @pl.when(unit < 2)
                        def _():
                            to_far(number, unit).start()

            return carry

        lax.fori_loop(0, units + 1, body, 0)

    def finish(index):
        number = index // units
        unit = index % units
        to_far(number, unit).wait_recv()
        near_in[number, unit, 0] = (
            near_in[number, unit, 0].astype(F32) + far_in[number, unit].astype(F32)
        ).astype(BF)
        if inner:
            block = owner(unit)

            @pl.when(((block > data) & (data > 0)) | ((block < data) & (data < depth - 1)))
            def _():
                rightward(number, block, unit).wait_recv()
                near_in[number, unit, 0] = (
                    near_in[number, unit, 0].astype(F32) + depth_in[number, block].astype(F32)
                ).astype(BF)

            @pl.when(block > data)
            def _():
                rightward(number, block, unit).start()

            @pl.when(block < data)
            def _():
                landing = block + (depth - block) * ((block + 1) // data)
                leftward(number, block, unit, landing).start()

        @pl.when(index + 2 < 3 * units)
        def _():
            to_far((index + 2) // units, (index + 2) % units).start()


    @pl.when(section == 0)
    def _():
        arrived(4)
        reduce_stage(0)

    @pl.when(section != 0)
    def _():
        later_y.start()

    arrived(1)
    block = 256
    blocks = wu.shape[2] // block

    def narrow(index, carry):
        rank = index // blocks
        columns = pl.ds(pl.multiple_of((index % blocks) * block, block), block)
        value = nt(low[...], wd[rank, columns, :]) * slope[rank, :, columns].astype(F32)
        value = value.astype(BF)
        slope[rank, :, columns] = value
        vec[0, pl.ds(rank, 1), columns] = jnp.sum(value.astype(F32), axis=0, keepdims=True)
        return carry

    lax.fori_loop(0, ranks * blocks, narrow, 0)

    @pl.when(section == 0)
    def _():
        finish(0)

    arrived(2)

    def first_transpose(step, carry):
        rows = pl.ds(pl.multiple_of(step * STEP, STEP), STEP)
        value = n1[rows, :].astype(F32) * first_gain_ref[...].astype(F32)
        value = value + first_shift_ref[...].astype(F32)
        first_t[:, rows] = jnp.transpose(value, (1, 0)).astype(BF)
        return carry

    def up_gradients():
        lax.fori_loop(0, steps, first_transpose, 0)
        reduce_stage(1)

    @pl.when(section == 0)
    def _():
        up_gradients()
        finish(1)

    def first_back(step, carry):
        rows = pl.ds(pl.multiple_of(step * STEP, STEP), STEP)
        arriving = dsum[rows, :]
        for rank in range(ranks):
            arriving = arriving + nt(slope[rank, rows, :], wu[rank])
        normal = n1[rows, :].astype(F32)
        add_row(10, arriving * normal)
        add_row(11, arriving)
        value = norm_back(arriving, normal, rs1[rows, 0:1], first_gain_ref[...].astype(F32))
        dsum[rows, :] = value
        value = value.astype(BF)
        low[rows, :] = value
        add_row(8, value.astype(F32))
        return carry

    lax.fori_loop(0, steps, first_back, 0)

    @pl.when(section != 0)
    def _():
        later_y.wait()
        pl.semaphore_wait(barrier, len(partners))
        share_outputs(g)

    arrived(3)

    def context_back(rank, carry):
        dcontext[rank] = nt(wa[rank, 3 * part : 4 * part, :], low[...]).astype(BF)
        return carry

    lax.fori_loop(0, ranks, context_back, 0)
    here = length_ref[tensor // sequences, tensor % sequences]
    visible = lax.broadcasted_iota(jnp.int32, (length, length), 0) < here

    def attend_back(head, carry):
        rank = head // heads
        base = (head % heads) * HD
        at_query = pl.ds(pl.multiple_of(base, HD), HD)
        at_keys = pl.ds(pl.multiple_of(part + base, HD), HD)
        at_values = pl.ds(pl.multiple_of(2 * part + base, HD), HD)
        query = (p[rank, at_query, :].astype(F32) * HD ** (-0.5)).astype(BF)
        keys = p[rank, at_keys, :]
        values = p[rank, at_values, :]
        dout = dcontext[rank, at_query, :]
        weights = jnp.where(visible, jnp.exp(tn(keys, query) - lse[head]), 0.0)
        dweights = tn(values, dout)
        inner_sum = jnp.sum(weights * dweights, axis=0, keepdims=True)
        dscores = (weights * (dweights - inner_sum)).astype(BF)
        p[rank, at_query, :] = (nn(keys, dscores) * HD ** (-0.5)).astype(BF)
        p[rank, at_keys, :] = nt(query, dscores).astype(BF)
        p[rank, at_values, :] = nt(dout, weights.astype(BF)).astype(BF)

        @pl.when((section == 0) & (head == 1))
        def _():
            finish(2)

        @pl.when((section == 0) & (head % 5 == 4))
        def _():
            finish(3 + head // 5)

        return carry

    lax.fori_loop(0, ranks * heads, attend_back, 0)
    early = 3 + ranks * heads // 5 + 1

    @pl.when(section != 0)
    def _():
        arrived(4)


    def entering_back(step, carry):
        rows = pl.ds(pl.multiple_of(step * STEP, STEP), STEP)
        total = dsum[rows, :]
        for rank in range(ranks):
            total = total + tn(p[rank, 0 : 3 * part, rows], wa[rank, 0 : 3 * part, :])
        dx[rows, :] = total.astype(BF)

        @pl.when(section != 0)
        def _():
            relay(step).start()

        return carry

    lax.fori_loop(0, steps, entering_back, 0)
    for rank in range(ranks):
        vec[0, 4 + rank : 5 + rank, :] = nt(jnp.ones((8, length), BF), p[rank])[0:1, :]
    vec_near = remote(vec.at[0], vec_in.at[0], vec_send.at[0], vec_recv.at[0], near)
    vec_near.start()
    turn(dx, dx_t)
    for copy in dx_copies:
        copy.start()
    dx_in[tensor] = dx_t[tensor]
    vec_near.wait_recv()

    def join(level, swap):
        for row in range(vec.shape[1]):
            pair = row ^ swap if row < 8 else row
            vec[level + 1, row : row + 1, :] = (
                vec[level, row : row + 1, :] + vec_in[level, pair : pair + 1, :]
            )

    join(0, 1)
    vec_far = remote(vec.at[1], vec_in.at[1], vec_send.at[1], vec_recv.at[1], far)
    vec_far.start()

    @pl.when(section == 0)
    def _():
        finish(early - 1)

    @pl.when(section != 0)
    def _():
        reduce_stage(0)
        up_gradients()
        finish(0)

    def entering_transpose(step, carry):
        rows = pl.ds(pl.multiple_of(step * STEP, STEP), STEP)
        first_t[:, rows] = jnp.transpose(xb[rows, :].astype(F32), (1, 0)).astype(BF)
        low_t[:, rows] = jnp.transpose(low[rows, :].astype(F32), (1, 0)).astype(BF)
        return carry

    lax.fori_loop(0, steps, entering_transpose, 0)
    reduce_stage(2)

    vec_far.wait_recv()
    join(1, 2)
    vec_deep = [
        remote(vec.at[2], vec_in.at[2 + hop], vec_send.at[2 + hop], vec_recv.at[2 + hop], device)
        for hop, device in enumerate(deep)
    ]
    for copy in vec_deep:
        copy.start()

    @pl.when(section != 0)
    def _():
        lax.fori_loop(1, early, lambda index, carry: (finish(index), carry)[1], 0)

    lax.fori_loop(early, 2 * units - 1, lambda index, carry: (finish(index), carry)[1], 0)
    for copy in dx_copies:
        copy.wait_recv()
    dx_done = pltpu.make_async_copy(dx_in, dx_out, out_sem.at[1])
    dx_done.start()
    half = table.shape[0]
    table_x = remote(table_away, table, table_send.at[0], table_recv.at[0], other)
    table_deep = [
        remote(table, table_in.at[hop], table_send.at[1 + hop], table_recv.at[1 + hop], device)
        for hop, device in enumerate(deep)
    ]

    @pl.when(section == 0)
    def _():
        types_each = table_out.shape[0]
        table_sum[...] = jnp.zeros_like(table_sum)

        def count(number, carry):
            row = lax.broadcasted_iota(jnp.int32, (2 * half, length), 0)
            picks = jnp.zeros((2 * half, length), F32)
            micro, item = number // sequences, number % sequences
            offset = 0
            for ids_ref, number_of in (
                (segment_ref, 2),
                (column_ref, COLS),
                (row_ref, ROWS),
                (answer_ref, 2),
            ):
                ids = ids_ref[micro, pl.ds(item, 1), :] + offset
                ids = ids + jnp.where(ids >= types_each, half - types_each, 0)
                picks = picks + jnp.where(ids == row, 1.0, 0.0)
                offset += number_of
            table_sum[...] += nt(picks.astype(BF), dx_in[number])
            return carry

        lax.fori_loop(0, ranks, count, 0)
        table[...] = table_sum[:half].astype(BF)
        table_away[...] = table_sum[half:].astype(BF)
        table_x.start()
        for copy in table_deep:
            copy.start()

    lax.fori_loop(2 * units - 1, 3 * units - 1, lambda index, carry: (finish(index), carry)[1], 0)

    @pl.when(section != 0)
    def _():
        table_x.wait_recv()
        for copy in table_deep:
            copy.start()

    finish(3 * units - 1)
    copies = []
    if inner:
        for number in range(3):
            total = jnp.zeros(final.shape[1:], F32)
            for unit in range(units):
                keep = jnp.where(owner(unit) == data, 1.0, 0.0)
                total = total + near_in[number, unit, 0].astype(F32) * keep
            final[number] = total

            @pl.when(data > 0)
            def _():
                rightward(number, data, 0).wait_recv()
                final[number] = final[number] + depth_in[number, data].astype(F32)

            @pl.when(data < depth - 1)
            def _():
                leftward(number, data, 0, depth).wait_recv()
                final[number] = final[number] + depth_in[number, depth].astype(F32)

            copy = pltpu.make_async_copy(
                final.at[number], sums_out.at[number], out_sem.at[2 + number]
            )
            copy.start()
            copies.append(copy)
    else:
        copy = pltpu.make_async_copy(
            near_in.at[:, :, 0], sums_out, out_sem.at[2]
        )
        copy.start()
        copies.append(copy)
    total = vec[2]
    for hop, copy in enumerate(vec_deep):
        copy.wait_recv()
        total = total + vec_in[2 + hop]
    vec_out[...] = total
    total = table[...].astype(F32)
    for hop, copy in enumerate(table_deep):
        copy.wait_recv()
        total = total + table_in[hop].astype(F32)
    table_out[...] = total[: table_out.shape[0]]

    for copy in y_copies:
        copy.wait()
    y_own.wait()
    for copy in dx_copies:
        copy.wait_send()
    vec_near.wait_send()
    vec_far.wait_send()
    for copy in vec_deep + table_deep:
        copy.wait_send()
    for unit in range(2):
        for which in range(2):
            to_near(2, unit, which).wait_send()
    for number in range(3):
        for unit in range(units):
            to_far(number, unit).wait_send()
            if inner:

                @pl.when(owner(unit) != data)
                def _():
                    rightward(number, 0, unit).wait_send()

    @pl.when(section != 0)
    def _():
        for step in range(steps):
            relay(step).wait_send()

    @pl.when(section == 0)
    def _():
        table_x.wait_send()

    dx_done.wait()
    for copy in copies:
        copy.wait()


def backward(cotangent, saved, lengths, vectors, ids, type_half, inner):
    wa, wu, wd, p, lse, act, slope, n1, n2, rs1, rs2, x, y = saved
    ranks = wa.shape[0]
    length, width = x.shape
    steps = length // STEP
    depth = lax.axis_size("dp")
    units = depth if inner else 4
    hops = depth - 1 if inner else 0
    share = width // units
    anywhere = pl.BlockSpec(memory_space=pl.ANY)
    inside = pl.BlockSpec(memory_space=pltpu.VMEM)
    part = wa.shape[1] // 4
    each = width // ranks
    half = -(-type_half // 16) * 16

    def like(value):
        return pltpu.VMEM(value.shape, value.dtype)

    plane = (length, width)
    turned = (width, length)
    chunk = (share, width)
    spread = (ranks, each, length)
    semaphores = pltpu.SemaphoreType.DMA
    sums = ((3,) + chunk, F32) if inner else ((3, units) + chunk, BF)
    return pl.pallas_call(
        functools.partial(backward_kernel, inner),
        name="backward_layer",
        out_shape=(
            jax.ShapeDtypeStruct(*sums),
            jax.ShapeDtypeStruct(spread, BF),
            jax.ShapeDtypeStruct(spread, BF),
            jax.ShapeDtypeStruct((16, width), F32),
            jax.ShapeDtypeStruct((type_half, each), F32),
        ),
        in_specs=[anywhere] * 14
        + [pl.BlockSpec(memory_space=pltpu.SMEM)]
        + [inside] * (len(vectors) + len(ids)),
        out_specs=(anywhere, anywhere, anywhere, inside, inside),
        scratch_shapes=[like(value) for value in saved[:-1]]
        + [
            pltpu.VMEM(plane, BF),
            pltpu.VMEM(plane, F32),
            pltpu.VMEM(plane, BF),
            pltpu.VMEM(turned, BF),
            pltpu.VMEM(turned, BF),
            pltpu.VMEM((ranks, part, length), BF),
            pltpu.VMEM(plane, BF),
            pltpu.VMEM(spread, BF),
            pltpu.VMEM(spread, BF),
            pltpu.VMEM(spread, BF),
            pltpu.VMEM((2, 2) + chunk, BF),
            pltpu.VMEM((3, units, 2) + chunk, BF),
            pltpu.VMEM((3, units) + chunk, BF),
            pltpu.VMEM((3, units + 1) + (chunk if inner else (16, 128)), BF),
            pltpu.VMEM((3,) + (chunk if inner else (16, 128)), F32),
            pltpu.VMEM((3, 16, width), F32),
            pltpu.VMEM((2 + hops, 16, width), F32),
            pltpu.VMEM((half, each), BF),
            pltpu.VMEM((half, each), BF),
            pltpu.VMEM((max(hops, 1), half, each), BF),
            pltpu.VMEM((2 * half, each), F32),
            semaphores((15,)),
            semaphores((2, 2)),
            semaphores((3, units, 2)),
            semaphores((3, units)),
            semaphores((3, units)),
            semaphores((3, units)),
            semaphores((3, units + 1)),
            semaphores((steps,)),
            semaphores((steps,)),
            semaphores((3,)),
            semaphores((3,)),
            semaphores((3,)),
            semaphores((3,)),
            semaphores((2 + hops,)),
            semaphores((2 + hops,)),
            semaphores((1 + hops,)),
            semaphores((1 + hops,)),
            semaphores((5,)),
        ],
        compiler_params=pltpu.CompilerParams(
            collective_id=1, has_side_effects=True, vmem_limit_bytes=VMEM_LIMIT
        ),
        cost_estimate=pl.CostEstimate(
            flops=17_000_000_000, bytes_accessed=60_000_000, transcendentals=3_000_000
        ),
    )(cotangent, *saved, lengths, *vectors, *ids)


def on_device(
    inputs,
    cotangent,
    segment_ids,
    column_ids,
    row_ids,
    answer_ids,
    lengths,
    type_table,
    query_weight,
    query_bias,
    key_weight,
    value_weight,
    value_bias,
    output_weight,
    output_bias,
    first_gain,
    first_shift,
    up_weight,
    up_bias,
    down_weight,
    down_bias,
    second_gain,
    second_shift,
):
    tensor = lax.axis_index("tensor")
    ranks = lax.axis_size("tensor")
    micro_count, sequences, length, width = inputs.shape
    type_count = 4 + COLS + ROWS
    part = query_weight.shape[2]
    hidden = up_weight.shape[2]

    ids = (segment_ids, column_ids, row_ids, answer_ids)
    wa = jnp.concatenate(
        [query_weight[0].T, key_weight[0].T, value_weight[0].T, output_weight[0]], axis=0
    )
    vectors = (
        query_bias,
        value_bias,
        up_bias,
        output_bias,
        first_gain,
        first_shift,
        down_bias,
        second_gain,
        second_shift,
    )
    saved = forward(
        inputs, ids, type_table, lengths, wa, up_weight[0], down_weight[0], vectors, ranks
    )
    depth = lax.axis_size("dp")
    inner = depth == 4 and width % (16 * depth) == 0
    type_half = type_count // lax.axis_size("section")
    sums, dx, leaving, vecs, table_grad = backward(
        cotangent, saved, lengths, (first_gain, first_shift, second_gain), ids, type_half, inner
    )

    def in_columns(value):
        return jnp.swapaxes(value, 1, 2).reshape(
            1, micro_count, sequences, length, width // ranks
        )

    layer_outputs = in_columns(leaving)
    layer_input_grads = in_columns(dx).astype(F32)
    if inner:
        summed = sums
    else:
        summed = lax.psum_scatter(
            sums.reshape(3, width, width), "dp", scatter_dimension=1, tiled=True
        ).astype(F32)
        vecs = lax.psum(vecs, "dp")
        table_grad = lax.psum(table_grad.astype(BF), "dp").astype(F32)
    mine = lax.dynamic_slice_in_dim(
        vecs[8:14].reshape(6, ranks, width // ranks), tensor, 1, 1
    ).reshape(1, 6 * (width // ranks))
    mine = jnp.concatenate([vecs[0:1], vecs[4:5], mine], axis=1)

    def vector(start, count):
        return mine[:, start : start + count]

    share = width // ranks
    after = 2 * width
    return (
        layer_outputs,
        layer_input_grads,
        summed[2, :, 0:part][None],
        vector(width, part),
        summed[2, :, part : 2 * part][None],
        summed[2, :, 2 * part : 3 * part][None],
        vector(width + 2 * part, part),
        summed[2, :, 3 * part : 4 * part].T[None],
        vector(after, share),
        vector(after + 2 * share, share),
        vector(after + 3 * share, share),
        summed[1][None],
        vector(0, hidden),
        summed[0].T[None],
        vector(after + share, share),
        vector(after + 4 * share, share),
        vector(after + 5 * share, share),
        table_grad,
    )


def solution(mesh):
    return jax.shard_map(
        on_device,
        mesh=mesh,
        in_specs=(
            P(None, "dp", None, None),
            P(None, "dp", None, None),
            P(None, "dp", None),
            P(None, "dp", None),
            P(None, "dp", None),
            P(None, "dp", None),
            P(None, "dp"),
            P(),
            P("section", None, "tensor"),
            P("section", "tensor"),
            P("section", None, "tensor"),
            P("section", None, "tensor"),
            P("section", "tensor"),
            P("section", "tensor", None),
            P("section", None),
            P("section", None),
            P("section", None),
            P("section", None, "tensor"),
            P("section", "tensor"),
            P("section", "tensor", None),
            P("section", None),
            P("section", None),
            P("section", None),
        ),
        out_specs=(
            P("section", None, "dp", None, "tensor"),
            P("section", None, "dp", None, "tensor"),
            P("section", "dp", "tensor"),
            P("section", "tensor"),
            P("section", "dp", "tensor"),
            P("section", "dp", "tensor"),
            P("section", "tensor"),
            P("section", "tensor", "dp"),
            P("section", "tensor"),
            P("section", "tensor"),
            P("section", "tensor"),
            P("section", "dp", "tensor"),
            P("section", "tensor"),
            P("section", "tensor", "dp"),
            P("section", "tensor"),
            P("section", "tensor"),
            P("section", "tensor"),
            P("section", "tensor"),
        ),
        check_vma=False,
    )
```
